32 devices in a mesh: rep: 4 (over y, core), fsdp: 8 (over z, x).
Axes of the slice: x: 2, y: 2, z: 4, core: 2. Of those that a mesh axis runs over, the one named last changes fastest.
Arguments:
- tokens: bfloat16 [1536, 64, 512], P(('rep', 'fsdp')), may hold values from -6 to 6
- counts: int32 [4, 8], P('rep', 'fsdp'), may hold values from 1 to 48, 240 in all within a row
- attn_gain: float32 [512], P('fsdp'), may hold values from 0.5 to 1.5
- w_query: float32 [512, 384], P('fsdp'), may hold values from -0.125 to 0.125
- w_key: float32 [512, 384], P('fsdp'), may hold values from -0.125 to 0.125
- w_value: float32 [512, 384], P('fsdp'), may hold values from -0.25 to 0.25
- attention_output_weight: float32 [384, 512], P('fsdp'), may hold values from -0.875 to 0.875
- rel_bias: float32 [192], P('fsdp'), may hold values from -4 to 4
- ffn_gain: float32 [512], P('fsdp'), may hold values from 0.5 to 1.5
- gate_weight: float32 [512, 1024], P('fsdp'), may hold values from -0.25 to 0.25
- up_weight: float32 [512, 1024], P('fsdp'), may hold values from -0.25 to 0.25
- down_weight: float32 [1024, 512], P('fsdp'), may hold values from -0.25 to 0.25
- cotangent: bfloat16 [1536, 64, 512], P(('rep', 'fsdp')), may hold values from -6 to 6
Outputs:
- layer_out: bfloat16 [1536, 64, 512], P(('rep', 'fsdp'))
- grad_tokens: bfloat16 [1536, 64, 512], P(('rep', 'fsdp'))
- grad_attn_gain: float32 [512], P('fsdp')
- grad_query: float32 [512, 384], P('fsdp')
- grad_key: float32 [512, 384], P('fsdp')
- grad_value: float32 [512, 384], P('fsdp')
- grad_out: float32 [384, 512], P('fsdp')
- grad_bias: float32 [192], P('fsdp')
- grad_ffn_gain: float32 [512], P('fsdp')
- grad_gate: float32 [512, 1024], P('fsdp')
- grad_up: float32 [512, 1024], P('fsdp')
- grad_down: float32 [1024, 512], P('fsdp')
The draws below stay inside these ranges and needn't reach their ends.
Inputs may be any that keep to these rules, and one draw needn't show every extreme that they name: Each row of counts (one index of rep) sums to 240, and each row holds an entry equal to 48.
All inputs are finite; a program needn't handle non-finite values. No bound on the sum of `counts` on one device may be relied on, other than what follows from the above.
Results may differ from the reference program's by a relative error of at most 0.02.
Values may be sent and summed in bfloat16 or wider, within the bound.
No kernel may reach another device: no remote copies, remote signals or barrier semaphores. Data moves between devices by JAX's collectives and lax.ppermute only.
A program may use at most 192 MiB of HBM per device.

```python
import math
import jax
import jax.numpy as jnp
import numpy as np
from jax import lax

D = 512
HEADS = 6
HDIM = 64
FF = 1024
BUCKETS = 32
L = 64
S_CAP = 48
INNER = 384
SERIES_MEAN = 30
SLOTS = 1536
N_REP = 4
N_FSDP = 8


def shard_levels(own_key, extent, shards, least, high):
    def one(position, blocks):
        draws = jax.random.uniform(jax.random.fold_in(jax.random.fold_in(own_key, 6), position), (blocks,), jnp.float32, least / len(shards), high / len(shards))
        return jnp.repeat(jnp.exp(draws), extent[position] // blocks).reshape((-1,) + (1,) * (len(extent) - position - 1))

    loudness = one(*shards[0])
    for cut in shards[1:]:
        loudness = loudness * one(*cut)
    return loudness


def split_up(amount, total, limit, lean):
    portions = [(1 << 20) // math.isqrt(standing ** lean) + 1 for standing in range(2, amount + 1)]
    spare, given = total - limit - (amount - 1), [1] * (amount - 1)
    while spare > 0:
        candidates = [i for i in range(amount - 1) if given[i] < limit]
        pool, budget = sum([portions[i] for i in candidates]), spare
        for i in candidates:
            more = min(limit - given[i], max(1, budget * portions[i] // pool), spare)
            given[i] = given[i] + more
            spare = spare - more
    return np.array([limit] + given)


def ragged(stream_key, amount, total, limit, skew):
    if amount == 2:
        one = jax.random.randint(stream_key, (), max(1, total - limit), min(limit, total - 1) + 1)
        return jnp.stack([one, total - one])
    tallies = jnp.asarray(split_up(amount, total, limit, skew), jnp.int32)
    twos = (amount - 1) // 2
    source_of, sink = tallies[1:1 + 2 * twos:2], tallies[2:2 + 2 * twos:2]
    margin = jnp.minimum(source_of - 1, limit - sink)
    shifted = jax.random.randint(jax.random.fold_in(stream_key, 1), (twos,), 0, 1 << 20) % (margin + 1)
    tallies = tallies.at[1:1 + 2 * twos:2].set(source_of - shifted).at[2:2 + 2 * twos:2].set(sink + shifted)
    return tallies[jax.random.permutation(jax.random.fold_in(stream_key, 2), amount)]


def centred(rng, dims, deviation, reach, cuts=(), kind=jnp.bfloat16):
    values = deviation * jax.random.normal(rng, dims, jnp.float32)
    if cuts:
        values = values * shard_levels(rng, dims, cuts, -0.22, 0.18)
    return jnp.clip(values, -reach, reach).astype(kind)


def setup_inputs(seed: int = 0) -> dict:
    streams_of = jax.random.split(jax.random.key(seed), 14)
    tokens = centred(streams_of[0], (SLOTS, L, D), 1.0, 6.0, ((0, 32),))
    counts = jax.vmap(lambda own: ragged(own, N_FSDP, SERIES_MEAN * N_FSDP, S_CAP, 2))(jax.random.split(streams_of[1], N_REP)).reshape((N_REP, N_FSDP)).astype(jnp.int32)
    attn_gain = jnp.clip(1.0 + 0.1 * jax.random.normal(streams_of[2], (D,), jnp.float32), 0.5, 1.5)
    w_query = centred(streams_of[3], (D, INNER), (4 * D) ** -0.5, 0.125, ((0, 8),), jnp.float32)
    w_key = centred(streams_of[4], (D, INNER), (4 * D) ** -0.5, 0.125, ((0, 8),), jnp.float32)
    w_value = centred(streams_of[5], (D, INNER), D ** -0.5, 0.25, ((0, 8),), jnp.float32)
    attention_output_weight = centred(streams_of[6], (INNER, D), (INNER // 8) ** -0.5, 0.875, ((0, 8),), jnp.float32)
    rel_bias = centred(streams_of[7], (BUCKETS * HEADS,), 1.0, 4.0, ((0, 8),), jnp.float32)
    ffn_gain = jnp.clip(1.0 + 0.1 * jax.random.normal(streams_of[8], (D,), jnp.float32), 0.5, 1.5)
    gate_weight = centred(streams_of[9], (D, FF), D ** -0.5, 0.25, ((0, 8),), jnp.float32)
    up_weight = centred(streams_of[10], (D, FF), D ** -0.5, 0.25, ((0, 8),), jnp.float32)
    down_weight = centred(streams_of[11], (FF, D), (FF // 2) ** -0.5, 0.25, ((0, 8),), jnp.float32)
    cotangent = centred(streams_of[12], (SLOTS, L, D), 1.0, 6.0, ((0, 32),))
    return {"tokens": tokens, "counts": counts, "attn_gain": attn_gain, "w_query": w_query, "w_key": w_key, "w_value": w_value, "attention_output_weight": attention_output_weight, "rel_bias": rel_bias, "ffn_gain": ffn_gain, "gate_weight": gate_weight, "up_weight": up_weight, "down_weight": down_weight, "cotangent": cotangent}


@jax.custom_vjp
def reduced_precision(v):
    return lax.optimization_barrier(v.astype(jnp.bfloat16)).astype(jnp.float32)

@jax.custom_vjp
def reduced_precision_back(v):
    return v

def low_keep(v):
    return (reduced_precision(v), None)

def low_pass(kept, grad):
    return (grad,)

def back_keep(v):
    return (v, None)

def back_low(kept, grad):
    return (reduced_precision(grad),)
reduced_precision.defvjp(low_keep, low_pass)
reduced_precision_back.defvjp(back_keep, back_low)
epsilon = 1e-06
PRECISION_TOP = lax.Precision.HIGHEST

def distance_bucket(distance, half_count, exact_count):
    if distance < exact_count:
        return distance
    reached = 0
    for higher in range(1, half_count - exact_count):
        if distance ** (half_count - exact_count) * exact_count ** higher >= 128 ** higher * exact_count ** (half_count - exact_count):
            reached = higher
    return exact_count + reached

def position_buckets(length, buckets):
    half_count = buckets // 2
    exact_count = half_count // 2
    return np.array([[(half_count if column > row_index else 0) + distance_bucket(abs(column - row_index), half_count, exact_count) for column in range(length)] for row_index in range(length)], dtype=np.int32)

def rms_scale(values):
    return lax.rsqrt(lax.optimization_barrier(jnp.mean(values * values, axis=-1, keepdims=True)) + epsilon)

def forward(layer_inputs, live_rows, attn_gain, w_query, w_key, w_value, attention_output_weight, rel_bias, ffn_gain, gate_weight, up_weight, down_weight):
    series_count = layer_inputs.shape[0]
    normed_first = reduced_precision(layer_inputs * rms_scale(layer_inputs) * reduced_precision(attn_gain))

    def project(weight_matrix):
        return reduced_precision(reduced_precision_back(jnp.einsum('rit,tu->riu', normed_first, reduced_precision(weight_matrix), precision=PRECISION_TOP)))
    queries = project(w_query).reshape(series_count, L, HEADS, HDIM)
    keys_all = project(w_key).reshape(series_count, L, HEADS, HDIM)
    values_all = project(w_value).reshape(series_count, L, HEADS, HDIM)
    bucket_ids = position_buckets(L, BUCKETS)
    head_bias = jnp.transpose(reduced_precision(rel_bias).reshape(BUCKETS, HEADS)[bucket_ids], (2, 0, 1))
    raw_scores = reduced_precision_back(jnp.einsum('sihe,sjhe->shij', queries, keys_all, precision=PRECISION_TOP))
    probs = jax.nn.softmax(raw_scores + head_bias[None], axis=-1)
    merged_head_rows = reduced_precision(reduced_precision_back(jnp.einsum('shij,sjhe->sihe', reduced_precision(probs), values_all, precision=PRECISION_TOP))).reshape(series_count, L, HEADS * HDIM)
    hidden_state = layer_inputs + reduced_precision_back(jnp.einsum('rit,tu->riu', merged_head_rows, reduced_precision(attention_output_weight), precision=PRECISION_TOP))
    normed_second = reduced_precision(hidden_state * rms_scale(hidden_state) * reduced_precision(ffn_gain))
    gate_before_activation = reduced_precision_back(jnp.einsum('kot,te->koe', normed_second, reduced_precision(gate_weight), precision=PRECISION_TOP))
    up_projected = reduced_precision_back(jnp.einsum('kot,te->koe', normed_second, reduced_precision(up_weight), precision=PRECISION_TOP))
    activated_rows = reduced_precision(jax.nn.gelu(gate_before_activation, approximate=True) * up_projected)
    branch_result = reduced_precision_back(jnp.einsum('vpm,mb->vpb', activated_rows, reduced_precision(down_weight), precision=PRECISION_TOP))
    return (hidden_state + branch_result) * live_rows

def reference(tokens, counts, attn_gain, w_query, w_key, w_value, attention_output_weight, rel_bias, ffn_gain, gate_weight, up_weight, down_weight, cotangent):
    masters = (attn_gain, w_query, w_key, w_value, attention_output_weight, rel_bias, ffn_gain, gate_weight, up_weight, down_weight)
    block_count = N_REP * N_FSDP
    layer_inputs = tokens.astype(jnp.float32).reshape(block_count, S_CAP, L, D)
    seeds = cotangent.astype(jnp.float32).reshape(block_count, S_CAP, L, D)
    slot_ids = jnp.arange(S_CAP, dtype=jnp.int32)
    live_slots = (slot_ids[None, :] < counts.reshape(block_count, 1)).astype(jnp.float32)

    def one_block(running, pieces):
        block_in, block_seed, block_live = pieces
        live_rows = block_live[:, None, None]

        def apply(block_now, *weights):
            return forward(block_now, live_rows, *weights)
        result, pullback = jax.vjp(apply, block_in, *masters)
        gradients = pullback(block_seed)
        running = tuple((before + extra for before, extra in zip(running, gradients[1:])))
        return (running, (result.astype(jnp.bfloat16), gradients[0].astype(jnp.bfloat16)))
    initial = tuple((jnp.zeros_like(weight_matrix) for weight_matrix in masters))
    grad_sums, (outputs, grad_in) = lax.scan(one_block, initial, (layer_inputs, seeds, live_slots))
    full_shape = (block_count * S_CAP, L, D)
    return (outputs.reshape(full_shape), grad_in.reshape(full_shape), grad_sums[0], grad_sums[1], grad_sums[2], grad_sums[3], grad_sums[4], grad_sums[5], grad_sums[6], grad_sums[7], grad_sums[8], grad_sums[9])
```

```python
import functools

import jax
import jax.numpy as jnp
import numpy as np
from jax import lax
from jax.experimental import pallas as pl
from jax.experimental.pallas import tpu as pltpu
from jax.sharding import PartitionSpec as P

HEADS, HDIM, BUCKETS = 6, 64, 32
INNER = HEADS * HDIM
PAIRS = HEADS // 2
PAIR = 2 * HDIM
CUT = 640
GROUP = 8
EPS = 1e-6
VMEM_LIMIT = 56 * 1024 * 1024
bf16, f32 = jnp.bfloat16, jnp.float32
sds = jax.ShapeDtypeStruct


def nn(a, b):
    return jnp.dot(a, b, preferred_element_type=f32)


def nt(a, b):
    return lax.dot_general(a, b, (((1,), (1,)), ((), ())), preferred_element_type=f32)


def tn(a, b):
    return lax.dot_general(a, b, (((0,), (0,)), ((), ())), preferred_element_type=f32)


def distance_bucket(distance, half_count, exact_count):
    if distance < exact_count:
        return distance
    reached = 0
    for higher in range(1, half_count - exact_count):
        if distance ** (
            half_count - exact_count
        ) * exact_count**higher >= 128**higher * exact_count ** (half_count - exact_count):
            reached = higher
    return exact_count + reached


def bucket_table(length):
    half = BUCKETS // 2
    ids = np.array(
        [
            [(half if j > i else 0) + distance_bucket(abs(j - i), half, half // 2) for i in range(length)]
            for j in range(length)
        ],
        dtype=np.int32,
    )
    return np.concatenate([ids, ids], axis=1)


def lane_low(shape):
    return lax.broadcasted_iota(jnp.int32, shape, 1) < HDIM


def split_heads(pair):
    low, zero = lane_low(pair.shape), jnp.zeros_like(pair)
    return jnp.concatenate([jnp.where(low, pair, zero), jnp.where(low, zero, pair)], axis=0)


def join_heads(both):
    rows = both.shape[0] // 2
    return jnp.where(lane_low((rows, PAIR)), both[:rows], both[rows:])


def row_sums(values):
    rows, width = values.shape
    return jnp.sum(values.reshape(rows // 8, 8, width), axis=0)


def inverse_rms(values):
    return lax.rsqrt(jnp.mean(values * values, axis=-1, keepdims=True) + EPS)


class Place:
    def __init__(self, ref, n_z):
        self.count, self.core, self.x, self.z = ref[0], ref[1], ref[2], ref[3]
        self.n_z = n_z

    def shards(self):
        for xx in range(2):
            for k in range(self.n_z):
                yield xx, k, jnp.bitwise_xor(self.z, k) * 2 + jnp.bitwise_xor(self.x, xx)


def at(shard, size):
    return pl.ds(pl.multiple_of(shard * size, size), size)


def interleaved(values, n_f, chunk):
    width = values.shape[1] // n_f // 2
    return jnp.concatenate(
        [values[:, (2 * f + chunk) * width : (2 * f + chunk + 1) * width] for f in range(n_f)], axis=1
    )


def prepare(n_f, place_ref, bias_ref, wq, wk, wv, wo, wg, wu, wd, ga, gf, a_ref, p0_ref, p1_ref):
    core = place_ref[1]
    ds, is_, fh = wq.shape[0], wo.shape[0], wd.shape[0] // 2
    half = wo.shape[1] // 2
    joined = jnp.concatenate([wq[...], wk[...], wv[...]], axis=1)
    row = lax.broadcasted_iota(jnp.int32, (ds, PAIR), 0)
    low = lane_low((1, PAIR))
    small = jnp.zeros((ds, PAIR), f32)
    n_b = BUCKETS // n_f
    for b in range(n_b):
        for p in range(PAIRS):
            value = jnp.where(low, bias_ref[b * HEADS + 2 * p], bias_ref[b * HEADS + 2 * p + 1])
            small = jnp.where(row == b * PAIRS + p, value, small)
    for i, gain in enumerate((ga, gf)):
        tiled = jnp.concatenate([gain[...]] * (PAIR // ds), axis=1)
        small = jnp.where(row == n_b * PAIRS + i, tiled, small)

    def write(c):
        if c == 0:
            a_ref[...] = joined[:, :CUT].astype(bf16)
        else:
            a_ref[:, : 3 * INNER - CUT] = joined[:, CUT:].astype(bf16)
            a_ref[:, 3 * INNER - CUT :] = small.astype(bf16)
        cols = slice(c * half, (c + 1) * half)
        for chunk, ref in enumerate((p0_ref, p1_ref)):
            g = interleaved((wg, wu)[c][...], n_f, chunk).astype(bf16)
            ref[:ds, :] = g[:, :half]
            ref[ds : 2 * ds, :] = g[:, half:]
            ref[2 * ds : 2 * ds + fh, :] = wd[chunk * fh : (chunk + 1) * fh, cols].astype(bf16)
        tail = wo[:, cols]
        pad = p0_ref.shape[0] - (2 * ds + fh + is_)
        if pad:
            tail = jnp.concatenate([tail, jnp.zeros((pad, half), f32)], axis=0)
        p0_ref[2 * ds + fh :, :] = tail.astype(bf16)

    for c in range(2):
        pl.when(core == c)(functools.partial(write, c))


def padded(rows):
    return -(-rows // 16) * 16


def call_prepare(place, n_f, attn_gain, wq, wk, wv, wo, rel_bias, ffn_gain, wg, wu, wd):
    ds, fh, half = wq.shape[0], wd.shape[0] // 2, wo.shape[1] // 2
    vm, sm = pl.BlockSpec(memory_space=pltpu.VMEM), pl.BlockSpec(memory_space=pltpu.SMEM)
    return pl.pallas_call(
        functools.partial(prepare, n_f),
        out_shape=(
            sds((ds, CUT), bf16),
            sds((2 * ds + fh + padded(wo.shape[0]), half), bf16),
            sds((2 * ds + fh, half), bf16),
        ),
        in_specs=[sm, sm] + [vm] * 9,
        out_specs=[vm] * 3,
        name="prepare",
    )(place, rel_bias, wq, wk, wv, wo, wg, wu, wd, attn_gain.reshape(1, -1), ffn_gain.reshape(1, -1))


def attention_forward(G, L, n_z, place_ref, idx_ref, tok_ref, z_ref, x_ref, zc_ref, xc_ref,
                      qkv_ref, probs_ref, mixed_ref, w_ref, gains_ref, table_ref, st_ref, small_ref):
    step = pl.program_id(0)
    place = Place(place_ref, n_z)
    D = tok_ref.shape[-1]
    n_f = 2 * n_z
    ds = D // n_f
    rest = 3 * INNER - CUT

    def assemble(c):
        for xx, k, f in place.shards():
            here, there = ((z_ref, zc_ref), (x_ref, xc_ref))[xx]
            one, two = (here, there) if c == 0 else (there, here)
            w_ref[at(f, ds), :CUT] = one[k]
            w_ref[at(f, ds), CUT:] = two[k, :, :rest]
            small_ref[at(f, ds), :] = two[k, :, rest:].astype(f32)

    @pl.when(step == 0)
    def _():
        for c in range(2):
            pl.when(place.core == c)(functools.partial(assemble, c))
        n_b = BUCKETS // n_f
        ids = idx_ref[...]
        for p in range(PAIRS):
            total = jnp.zeros(ids.shape, f32)
            for b in range(BUCKETS):
                row = b // n_b * ds + (b % n_b) * PAIRS + p
                total = jnp.where(ids == b, small_ref[row : row + 1, :], total)
            table_ref[p] = total
        per = PAIR // ds
        lane = lax.broadcasted_iota(jnp.int32, (1, PAIR), 1) // ds
        gains_ref[...] = jnp.zeros_like(gains_ref)
        for i in range(2):
            for v in range(D // PAIR):
                total = jnp.zeros((1, PAIR), f32)
                for f in range(per):
                    row = (v * per + f) * ds + n_b * PAIRS + i
                    total = jnp.where(lane == f, small_ref[row : row + 1, :], total)
                gains_ref[i : i + 1, v * PAIR : (v + 1) * PAIR] = total

    @pl.when(step * G < place.count)
    def _():
        x = tok_ref[...].reshape(G * L, D).astype(f32)
        normed = (x * inverse_rms(x) * gains_ref[0:1, :]).astype(bf16)
        qkv_ref[...] = nn(normed, w_ref[...]).astype(bf16)
        for s in range(G):
            rows = pl.ds(s * L, L)
            for p in range(PAIRS):
                q = qkv_ref[rows, pl.ds(p * PAIR, PAIR)]
                k = qkv_ref[rows, pl.ds(INNER + p * PAIR, PAIR)]
                st_ref[s, p] = nt(k, split_heads(q))
        for s in range(G):
            for p in range(PAIRS):
                st = st_ref[s, p] + table_ref[p]
                e = jnp.exp(st - jnp.max(st, axis=0, keepdims=True))
                probs_ref[s, p] = (e * (1.0 / jnp.sum(e, axis=0, keepdims=True))).astype(bf16)
        for s in range(G):
            rows = pl.ds(s * L, L)
            for p in range(PAIRS):
                v = qkv_ref[rows, pl.ds(2 * INNER + p * PAIR, PAIR)]
                mixed_ref[rows, pl.ds(p * PAIR, PAIR)] = join_heads(tn(probs_ref[s, p], v)).astype(bf16)


def params():
    return pltpu.CompilerParams(dimension_semantics=("arbitrary",), vmem_limit_bytes=VMEM_LIMIT)


def whole(shape):
    return pl.BlockSpec(shape, lambda i, *_: (0,) * len(shape), pipeline_mode=pl.Buffered(1))


def live_group(i, place, G):
    return jnp.minimum(i, jnp.maximum((place[0] + G - 1) // G - 1, 0))


def series_spec(G, shape, every=False):
    tail = (0,) * (len(shape) - 1)
    return pl.BlockSpec((G,) + shape[1:], lambda i, c: ((i if every else live_group(i, c, G)),) + tail)


def row_spec(G, L, width):
    return pl.BlockSpec((G * L, width), lambda i, c: (live_group(i, c, G), 0))


def cost(rows, per_row, nbytes, exps=0):
    return pl.CostEstimate(flops=2 * rows * per_row, bytes_accessed=nbytes, transcendentals=exps)


def call_attention_forward(place, tokens, pieces):
    S, L, D = tokens.shape
    G, n_z = GROUP, pieces[0].shape[0]
    return pl.pallas_call(
        functools.partial(attention_forward, G, L, n_z),
        out_shape=(
            sds((S * L, 3 * INNER), bf16),
            sds((S, PAIRS, L, PAIR), bf16),
            sds((S * L, INNER), bf16),
            sds((D, 3 * INNER), bf16),
            sds((8, D), f32),
        ),
        grid_spec=pltpu.PrefetchScalarGridSpec(
            num_scalar_prefetch=1,
            grid=(S // G,),
            in_specs=[whole((L, PAIR)), series_spec(G, tokens.shape)] + [whole(piece.shape) for piece in pieces],
            out_specs=[
                row_spec(G, L, 3 * INNER),
                series_spec(G, (S, PAIRS, L, PAIR)),
                row_spec(G, L, INNER),
                whole((D, 3 * INNER)),
                whole((8, D)),
            ],
            scratch_shapes=[
                pltpu.VMEM((PAIRS, L, PAIR), f32),
                pltpu.VMEM((G, PAIRS, L, PAIR), f32),
                pltpu.VMEM((D, PAIR), f32),
            ],
        ),
        compiler_params=params(),
        cost_estimate=cost(S * L, D * 3 * INNER * 4, S * L * 5000),
        name="attention_forward",
    )(place, jnp.asarray(bucket_table(L)), tokens, *pieces)


def gelu_parts(v):
    c = 0.7978845608028654
    v2 = v * v
    t = jnp.tanh(v * (c + (c * 0.044715) * v2))
    half = 0.5 + 0.5 * t
    return v * half, half + (0.5 * v) * (1.0 - t * t) * (c + (3 * c * 0.044715) * v2)


def put_weights(place, first, n_z, pieces, wg, wu, wd, wo):
    z_ref, x_ref, zc_ref, xc_ref = pieces
    n_f = 2 * n_z
    D, FW = wg.shape
    ds, fh, half = D // n_f, FW // n_f, FW // 2

    def assemble(c):
        for xx, k, f in place.shards():
            here, there = ((z_ref, zc_ref), (x_ref, xc_ref))[xx]
            for which, piece in enumerate((here, there) if c == 0 else (there, here)):
                gated = (wg, wu)[which]
                gated[at(f, ds), :half] = piece[k, :ds, :]
                gated[at(f, ds), half:] = piece[k, ds : 2 * ds, :]
                cols = slice(which * half, (which + 1) * half)
                wd[at(f, fh), cols] = piece[k, 2 * ds : 2 * ds + fh, :]
                if first:
                    is_ = INNER // n_f
                    if is_ % 16 == 0:
                        wo[at(f, is_), cols] = piece[k, 2 * ds + fh : 2 * ds + fh + is_, :]
                    else:
                        wo[f, :, cols] = piece[k, 2 * ds + fh :, :]

    for c in range(2):
        pl.when(place.core == c)(functools.partial(assemble, c))


def put_grads(place, n_z, keep, send, ag, au, ad, ao=None):
    n_f = 2 * n_z
    D, FW = ag.shape
    ds, fh, half = D // n_f, FW // n_f, FW // 2

    def write(c):
        for xx, k, f in place.shards():
            for which, ref in enumerate((keep, send) if c == 0 else (send, keep)):
                gated = (ag, au)[which]
                cols = slice(which * half, (which + 1) * half)
                ref[xx, k, :ds, :] = gated[at(f, ds), :half].astype(bf16)
                ref[xx, k, ds : 2 * ds, :] = gated[at(f, ds), half:].astype(bf16)
                ref[xx, k, 2 * ds : 2 * ds + fh, :] = ad[at(f, fh), cols].astype(bf16)
                if ao is not None:
                    is_ = INNER // n_f
                    if is_ % 16 == 0:
                        ref[xx, k, 2 * ds + fh :, :] = ao[at(f, is_), cols].astype(bf16)
                    else:
                        ref[xx, k, 2 * ds + fh :, :] = ao[f, :, cols].astype(bf16)

    for c in range(2):
        pl.when(place.core == c)(functools.partial(write, c))


def ffn_half(G, L, CH, n_z, first, place_ref, *refs):
    if first:
        (tok_ref, ct_ref, mixed_ref, z_ref, x_ref, zc_ref, xc_ref, gains_ref,
         hid_ref, part_ref, gpart_ref, wo_out, keep, send,
         ag, au, ad, wg, wu, wd, n2, gb, gate, up, ga, act, ggr, gur, acc, gn, spread) = refs
    else:
        (hid_ref, ct_ref, mixed_ref, part_ref, gpart_ref, z_ref, x_ref, zc_ref, xc_ref, gains_ref, wo_in,
         out_ref, gh_ref, gm_ref, keep, send, gf_ref,
         ag, au, ad, wg, wu, wd, n2, gb, gate, up, ga, act, ggr, gur, acc, gn, ao, spread) = refs
    step = pl.program_id(0)
    last = pl.num_programs(0) - 1
    R = G * L
    D = ct_ref.shape[-1]
    FW = wg.shape[1]
    n_f = 2 * n_z
    is_ = INNER // n_f
    place = Place(place_ref, n_z)
    count = place.count

    @pl.when(step == 0)
    def _():
        wo = (wo_out if is_ % 16 == 0 else spread) if first else None
        put_weights(place, first, n_z, (z_ref, x_ref, zc_ref, xc_ref), wg, wu, wd, wo)
        if first and is_ % 16:
            wo_out[...] = jnp.concatenate([spread[f, :is_, :].astype(f32) for f in range(n_f)], axis=0).astype(bf16)
        for ref in (ag, au, ad) if first else (ag, au, ad, ao, gf_ref):
            ref[...] = jnp.zeros_like(ref)

    if not first:

        @pl.when(step * G >= count)
        def _():
            out_ref[...] = jnp.zeros_like(out_ref)

    @pl.when(step * G < count)
    def _():
        if first:
            hid_ref[...] = tok_ref[...].reshape(R, D).astype(f32) + nn(mixed_ref[...], wo_out[...])
        h = hid_ref[...]
        n2[...] = (h * inverse_rms(h) * gains_ref[1:2, :]).astype(bf16)
        live = (step * G + lax.broadcasted_iota(jnp.int32, (R, 1), 0) // L) < count
        gb[...] = jnp.where(live, ct_ref[...].reshape(R, D), jnp.zeros((), bf16))
        for c in range(FW // CH):
            cols = pl.ds(c * CH, CH)
            gate[...] = nn(n2[...], wg[:, cols])
            up[...] = nn(n2[...], wu[:, cols])
            ga[...] = nt(gb[...], wd[cols, :])
            for r in range(0, R, L):
                rows = pl.ds(r, L)
                u = up[rows, :]
                a = ga[rows, :]
                g, dg = gelu_parts(gate[rows, :])
                act[rows, :] = (g * u).astype(bf16)
                ggr[rows, :] = (a * u * dg).astype(bf16)
                gur[rows, :] = (a * g).astype(bf16)
            if c == 0:
                acc[...] = nn(act[...], wd[cols, :])
                gn[...] = nt(ggr[...], wg[:, cols]) + nt(gur[...], wu[:, cols])
            else:
                acc[...] += nn(act[...], wd[cols, :])
                gn[...] += nt(ggr[...], wg[:, cols]) + nt(gur[...], wu[:, cols])
            ad[cols, :] += tn(act[...], gb[...])
            ag[:, cols] += tn(n2[...], ggr[...])
            au[:, cols] += tn(n2[...], gur[...])
        if first:
            part_ref[...] = acc[...].astype(bf16)
            gpart_ref[...] = gn[...].astype(bf16)
        else:
            h = hid_ref[...]
            out = h + part_ref[...].astype(f32) + acc[...]
            out_ref[...] = jnp.where(live, out, 0.0).astype(bf16).reshape(G, L, D)
            scale = inverse_rms(h)
            hs = h * scale
            g2 = gn[...] + gpart_ref[...].astype(f32)
            gf_ref[...] += row_sums(g2 * hs)
            g2 = g2 * gains_ref[1:2, :]
            dot = jnp.mean(g2 * hs, axis=-1, keepdims=True)
            gh = (gb[...].astype(f32) + scale * (g2 - hs * dot)).astype(bf16)
            gh_ref[...] = gh
            ao[...] += tn(mixed_ref[...], gh)
            gm_ref[...] = nt(gh, wo_in[...]).astype(bf16)

    @pl.when(step == last)
    def _():
        if first:
            put_grads(place, n_z, keep, send, ag, au, ad)
        elif is_ % 16 == 0:
            put_grads(place, n_z, keep, send, ag, au, ad, ao)
        else:
            for f in range(n_f):
                spread[f, :is_, :] = ao[f * is_ : (f + 1) * is_, :]
            put_grads(place, n_z, keep, send, ag, au, ad, spread)


def call_ffn_half(first, place, pieces, gains, arrays, S, L, D, CH=256):
    G, n_z = GROUP, pieces[0].shape[0]
    R, n_f = G * L, 2 * n_z
    FW = D
    ds, fh, half, is_ = D // n_f, FW // n_f, FW // 2, INNER // n_f
    series = series_spec(G, (S, L, D))
    piece_specs = [whole(piece.shape) for piece in pieces] + [whole(gains.shape)]
    rows = functools.partial(row_spec, G, L)
    extra = 0 if first else padded(is_)
    pack = (2, n_z, 2 * ds + fh + extra, half)
    if first:
        in_specs = [series, series, rows(INNER)] + piece_specs
        out_shape = [sds((S * L, D), f32), sds((S * L, D), bf16), sds((S * L, D), bf16), sds((INNER, D), bf16),
                     sds(pack, bf16), sds(pack, bf16)]
        out_specs = [rows(D), rows(D), rows(D), whole((INNER, D)), whole(pack), whole(pack)]
        operands = arrays + tuple(pieces) + (gains,)
    else:
        *arrays, wo = arrays
        in_specs = [rows(D), series, rows(INNER), rows(D), rows(D)] + piece_specs + [whole(wo.shape)]
        out_shape = [sds((S, L, D), bf16), sds((S * L, D), bf16), sds((S * L, INNER), bf16),
                     sds(pack, bf16), sds(pack, bf16), sds((8, D), f32)]
        out_specs = [series_spec(G, (S, L, D), True), rows(D), rows(INNER), whole(pack), whole(pack), whole((8, D))]
        operands = tuple(arrays) + tuple(pieces) + (gains, wo)
    vm = pltpu.VMEM
    scratch = (
        [vm((D, FW), f32)] * 2 + [vm((FW, D), f32)]
        + [vm((D, FW), bf16)] * 2 + [vm((FW, D), bf16)]
        + [vm((R, D), bf16)] * 2 + [vm((R, CH), f32)] * 3 + [vm((R, CH), bf16)] * 3 + [vm((R, D), f32)] * 2
        + ([] if first else [vm((INNER, D), f32)])
        + [vm((n_f, padded(is_), D) if is_ % 16 else (1, 16, 128), bf16 if first else f32)]
    )
    return pl.pallas_call(
        functools.partial(ffn_half, G, L, CH, n_z, first),
        out_shape=tuple(out_shape),
        grid_spec=pltpu.PrefetchScalarGridSpec(
            num_scalar_prefetch=1, grid=(S // G,), in_specs=in_specs, out_specs=out_specs, scratch_shapes=scratch
        ),
        compiler_params=params(),
        cost_estimate=cost(S * L, 12 * D * FW, S * L * 9000),
        name="ffn_first" if first else "ffn_second",
    )(place, *operands)


def attention_backward(G, L, n_z, place_ref, idx_ref, tok_ref, qkv_ref, probs_ref, gm_ref, gh_ref, w_ref, gains_ref, gf_ref,
                       gt_ref, keep, send, aw, aq, ab, dqkv, dp_ref, ds_ref, small):
    step = pl.program_id(0)
    last = pl.num_programs(0) - 1
    R = G * L
    D = tok_ref.shape[-1]
    place = Place(place_ref, n_z)
    count = place.count

    @pl.when(step == 0)
    def _():
        for ref in (aw, aq, ab):
            ref[...] = jnp.zeros_like(ref)

    @pl.when(step * G >= count)
    def _():
        gt_ref[...] = jnp.zeros_like(gt_ref)

    @pl.when(step * G < count)
    def _():
        cols = [[pl.ds(b * INNER + p * PAIR, PAIR) for b in range(3)] for p in range(PAIRS)]
        for p in range(PAIRS):
            for s in range(G):
                rows = pl.ds(s * L, L)
                dm = split_heads(gm_ref[rows, pl.ds(p * PAIR, PAIR)])
                dp_ref[s, p] = nt(qkv_ref[rows, cols[p][2]], dm)
                dqkv[rows, cols[p][2]] = nn(probs_ref[s, p], dm).astype(bf16)
        for p in range(PAIRS):
            total = ab[p]
            for s in range(G):
                prf = probs_ref[s, p].astype(f32)
                dp = dp_ref[s, p]
                ds = prf * (dp - jnp.sum(prf * dp, axis=0, keepdims=True))
                total = total + ds
                ds_ref[s, p] = ds.astype(bf16)
            ab[p] = total
        for p in range(PAIRS):
            for s in range(G):
                rows = pl.ds(s * L, L)
                low = ds_ref[s, p]
                dqkv[rows, cols[p][1]] = nn(low, split_heads(qkv_ref[rows, cols[p][0]])).astype(bf16)
                dqkv[rows, cols[p][0]] = join_heads(tn(low, qkv_ref[rows, cols[p][1]])).astype(bf16)
        x = tok_ref[...].reshape(R, D).astype(f32)
        scale = inverse_rms(x)
        xs = x * scale
        aw[...] += tn((xs * gains_ref[0:1, :]).astype(bf16), dqkv[...])
        g = nt(dqkv[...], w_ref[...])
        aq[...] += row_sums(g * xs)
        g = g * gains_ref[0:1, :]
        dot = jnp.mean(g * xs, axis=-1, keepdims=True)
        gt_ref[...] = (gh_ref[...].astype(f32) + scale * (g - xs * dot)).astype(bf16).reshape(G, L, D)

    @pl.when(step == last)
    def _():
        n_f = 2 * n_z
        ds, n_b, rest = D // n_f, BUCKETS // n_f, 3 * INNER - CUT
        ids = idx_ref[...]
        low = lane_low((1, PAIR))
        small[...] = jnp.zeros_like(small)
        for p in range(PAIRS):
            t = ab[p]
            for b in range(BUCKETS):
                by_lane = jnp.sum(jnp.where(ids == b, t, 0.0), axis=0, keepdims=True)
                one = jnp.sum(jnp.where(low, by_lane, 0.0), axis=1, keepdims=True)
                two = jnp.sum(jnp.where(low, 0.0, by_lane), axis=1, keepdims=True)
                row = b // n_b * ds + (b % n_b) * PAIRS + p
                small[row : row + 1, :] = jnp.where(low, one, two)
        for i, ref in enumerate((aq, gf_ref)):
            total = jnp.sum(ref[...], axis=0, keepdims=True)
            for f in range(n_f):
                row = f * ds + n_b * PAIRS + i
                start = f * ds // PAIR * PAIR
                small[row : row + 1, :] = total[:, start : start + PAIR]

        def write(c):
            for xx, k, f in place.shards():
                one, two = (keep, send) if c == 0 else (send, keep)
                one[xx, k] = aw[at(f, ds), :CUT].astype(bf16)
                two[xx, k, :, :rest] = aw[at(f, ds), CUT:].astype(bf16)
                two[xx, k, :, rest:] = small[at(f, ds), :].astype(bf16)

        for c in range(2):
            pl.when(place.core == c)(functools.partial(write, c))


def call_attention_backward(place, n_z, tokens, qkv, probs, gm, gh, w, gains, gf):
    S, L, D = tokens.shape
    G = GROUP
    R = G * L
    rows = functools.partial(row_spec, G, L)
    pack = (2, n_z, D // (2 * n_z), CUT)
    vm = pltpu.VMEM
    return pl.pallas_call(
        functools.partial(attention_backward, G, L, n_z),
        out_shape=(sds((S, L, D), bf16), sds(pack, bf16), sds(pack, bf16)),
        grid_spec=pltpu.PrefetchScalarGridSpec(
            num_scalar_prefetch=1,
            grid=(S // G,),
            in_specs=[whole((L, PAIR)), series_spec(G, tokens.shape), rows(3 * INNER), series_spec(G, probs.shape),
                      rows(INNER), rows(D), whole(w.shape), whole(gains.shape), whole(gf.shape)],
            out_specs=[series_spec(G, tokens.shape, True), whole(pack), whole(pack)],
            scratch_shapes=[
                vm(w.shape, f32), vm((8, D), f32), vm((PAIRS, L, PAIR), f32), vm((R, 3 * INNER), bf16),
                vm((G, PAIRS, L, PAIR), f32), vm((G, PAIRS, L, PAIR), bf16), vm((D, PAIR), f32),
            ],
        ),
        compiler_params=params(),
        cost_estimate=cost(S * L, D * 3 * INNER * 6, S * L * 6000),
        name="attention_backward",
    )(place, jnp.asarray(bucket_table(L)), tokens, qkv, probs, gm, gh, w, gains, gf)


def tree(values):
    while len(values) > 1:
        values = [a + b for a, b in zip(values[0::2], values[1::2])]
    return values[0]


def finish(n_f, n_r, place_ref, *refs):
    packs = [refs[i * n_r : (i + 1) * n_r] for i in range(3)]
    gq, gk, gv, go, gg, gu, gd, gs = refs[3 * n_r :]
    core = place_ref[1]
    ds, is_, fh = gq.shape[0], go.shape[0], gd.shape[0] // 2
    half = go.shape[1] // 2

    def halves(pack):
        here = tree([ref[...].astype(f32) for ref in pack[0::2]])
        there = tree([ref[...].astype(f32) for ref in pack[1::2]])
        return jnp.where(core == 0, here, there), jnp.where(core == 0, there, here)

    one, two = halves(packs[2])
    gq[...] = one[:, :INNER]
    gk[...] = jnp.concatenate([one[:, INNER:CUT], two[:, : 2 * INNER - CUT]], axis=1)
    gv[...] = two[:, 2 * INNER - CUT : 3 * INNER - CUT]
    gs[...] = two[:, 3 * INNER - CUT :]
    chunks = [halves(packs[0]), halves(packs[1])]
    for which, ref in enumerate((gg, gu)):
        wide = [jnp.concatenate([c[which][:ds], c[which][ds : 2 * ds]], axis=1) for c in chunks]
        width = wide[0].shape[1] // n_f
        ref[...] = jnp.concatenate(
            [w[:, f * width : (f + 1) * width] for f in range(n_f) for w in wide], axis=1
        )
    for chunk, pair in enumerate(chunks):
        for which in range(2):
            gd[chunk * fh : (chunk + 1) * fh, which * half : (which + 1) * half] = pair[which][2 * ds : 2 * ds + fh]
    for which in range(2):
        go[:, which * half : (which + 1) * half] = chunks[1][which][2 * ds + fh : 2 * ds + fh + is_]


def call_finish(place, n_f, n_r, packs, shapes):
    vm, sm = pl.BlockSpec(memory_space=pltpu.VMEM), pl.BlockSpec(memory_space=pltpu.SMEM)
    flat = [piece for pack in packs for piece in pack]
    return pl.pallas_call(
        functools.partial(finish, n_f, n_r),
        out_shape=tuple(sds(shape, f32) for shape in shapes),
        in_specs=[sm] + [vm] * len(flat),
        out_specs=[vm] * len(shapes),
        name="finish",
    )(place, *flat)


def solution(mesh):
    n_r, n_f = mesh.shape["rep"], mesh.shape["fsdp"]
    n_z = n_f // 2

    def over_fsdp(value, distance):
        return lax.ppermute(value, "fsdp", [(i, i ^ distance) for i in range(n_f)])

    def over_rep(value, distance):
        return lax.ppermute(value, "rep", [(i, i ^ distance) for i in range(n_r)])

    def gather(pack):
        near = jnp.stack([pack] + [over_fsdp(pack, 2 * k) for k in range(1, n_z)])
        far = over_fsdp(near, 1)
        return near, far, over_rep(near, 1), over_rep(far, 1)

    def scatter(keep, send):
        got = over_rep(send, 1)
        away = (keep[1].astype(f32) + got[1].astype(f32)).astype(bf16)
        here = keep[0].astype(f32) + got[0].astype(f32) + over_fsdp(away, 1).astype(f32)
        own = here[0]
        for k in range(1, n_z):
            own = own + over_fsdp(here[k].astype(bf16), 2 * k).astype(f32)
        own = own.astype(bf16)
        return [own] + [over_rep(own, m) for m in range(1, n_r)]

    def body(tokens, counts, attn_gain, wq, wk, wv, wo, rel_bias, ffn_gain, wg, wu, wd, cotangent):
        S, L, D = tokens.shape
        r, f = lax.axis_index("rep"), lax.axis_index("fsdp")
        place = jnp.stack([counts[0, 0], r % 2, f % 2, f // 2]).astype(jnp.int32)
        pack_a, pack_0, pack_1 = call_prepare(place, n_f, attn_gain, wq, wk, wv, wo, rel_bias, ffn_gain, wg, wu, wd)
        qkv, probs, mixed, w_all, gains = call_attention_forward(place, tokens, gather(pack_a))
        hidden, part, gpart, wo_all, keep_0, send_0 = call_ffn_half(
            True, place, gather(pack_0), gains, (tokens, cotangent, mixed), S, L, D
        )
        sums_0 = scatter(keep_0, send_0)
        layer_out, gh, gm, keep_1, send_1, gf = call_ffn_half(
            False, place, gather(pack_1), gains, (hidden, cotangent, mixed, part, gpart, wo_all), S, L, D
        )
        sums_1 = scatter(keep_1, send_1)
        grad_tokens, keep_2, send_2 = call_attention_backward(
            place, n_z, tokens, qkv, probs, gm, gh, w_all, gains, gf
        )
        sums_2 = scatter(keep_2, send_2)
        ds, n_b = wq.shape[0], BUCKETS // n_f
        gq, gk, gv, go, gg, gu, gd, small = call_finish(
            place, n_f, n_r, (sums_0, sums_1, sums_2),
            (wq.shape, wk.shape, wv.shape, wo.shape, wg.shape, wu.shape, wd.shape, (ds, PAIR)),
        )
        grad_bias = small[: n_b * PAIRS, ::HDIM].reshape(-1)
        gain_rows = small[n_b * PAIRS : n_b * PAIRS + 2].reshape(2, PAIR // ds, ds)
        gain_rows = lax.dynamic_index_in_dim(gain_rows, f % (PAIR // ds), axis=1, keepdims=False)
        return (layer_out, grad_tokens, gain_rows[0], gq, gk, gv, go, grad_bias, gain_rows[1], gg, gu, gd)

    rows, cols, flat = P(("rep", "fsdp"), None, None), P("fsdp", None), P("fsdp")
    return jax.shard_map(
        body,
        mesh=mesh,
        in_specs=(rows, P("rep", "fsdp"), flat, cols, cols, cols, cols, flat, flat, cols, cols, cols, rows),
        out_specs=(rows, rows, flat, cols, cols, cols, cols, flat, flat, cols, cols, cols),
        check_vma=False,
    )
```

```python
import functools

import jax
import jax.numpy as jnp
import numpy as np
from jax import lax
from jax.experimental import pallas as pl
from jax.experimental.pallas import tpu as pltpu
from jax.sharding import PartitionSpec as P

HEADS, HDIM, BUCKETS = 6, 64, 32
INNER = HEADS * HDIM
PAIRS = HEADS // 2
PAIR = 2 * HDIM
CUT = 640
GROUP = 8
EPS = 1e-6
VMEM_LIMIT = 56 * 1024 * 1024
bf16, f32 = jnp.bfloat16, jnp.float32
sds = jax.ShapeDtypeStruct


def nn(a, b):
    return jnp.dot(a, b, preferred_element_type=f32)


def nt(a, b):
    return lax.dot_general(a, b, (((1,), (1,)), ((), ())), preferred_element_type=f32)


def tn(a, b):
    return lax.dot_general(a, b, (((0,), (0,)), ((), ())), preferred_element_type=f32)


def distance_bucket(distance, half_count, exact_count):
    if distance < exact_count:
        return distance
    reached = 0
    for higher in range(1, half_count - exact_count):
        if distance ** (
            half_count - exact_count
        ) * exact_count**higher >= 128**higher * exact_count ** (half_count - exact_count):
            reached = higher
    return exact_count + reached


def bucket_table(length):
    half = BUCKETS // 2
    ids = np.array(
        [
            [(half if j > i else 0) + distance_bucket(abs(j - i), half, half // 2) for i in range(length)]
            for j in range(length)
        ],
        dtype=np.int32,
    )
    return np.concatenate([ids, ids], axis=1)


def lane_low(shape):
    return lax.broadcasted_iota(jnp.int32, shape, 1) < HDIM


def split_heads(pair):
    low, zero = lane_low(pair.shape), jnp.zeros_like(pair)
    return jnp.concatenate([jnp.where(low, pair, zero), jnp.where(low, zero, pair)], axis=0)


def join_heads(both):
    rows = both.shape[0] // 2
    return jnp.where(lane_low((rows, PAIR)), both[:rows], both[rows:])


def row_sums(values):
    rows, width = values.shape
    return jnp.sum(values.reshape(rows // 8, 8, width), axis=0)


def inverse_rms(values):
    return lax.rsqrt(jnp.mean(values * values, axis=-1, keepdims=True) + EPS)


class Place:
    def __init__(self, ref, n_z):
        self.count, self.core, self.x, self.z = ref[0], ref[1], ref[2], ref[3]
        self.n_z = n_z

    def shards(self):
        for xx in range(2):
            for k in range(self.n_z):
                yield xx, k, jnp.bitwise_xor(self.z, k) * 2 + jnp.bitwise_xor(self.x, xx)


def at(shard, size):
    return pl.ds(pl.multiple_of(shard * size, size), size)


def interleaved(values, n_f, chunk):
    width = values.shape[1] // n_f // 2
    return jnp.concatenate(
        [values[:, (2 * f + chunk) * width : (2 * f + chunk + 1) * width] for f in range(n_f)], axis=1
    )


def prepare(n_f, place_ref, bias_ref, wq, wk, wv, wo, wg, wu, wd, ga, gf, a_ref, p0_ref, p1_ref):
    core = place_ref[1]
    ds, is_, fh = wq.shape[0], wo.shape[0], wd.shape[0] // 2
    half = wo.shape[1] // 2
    joined = jnp.concatenate([wq[...], wk[...], wv[...]], axis=1)
    row = lax.broadcasted_iota(jnp.int32, (ds, PAIR), 0)
    low = lane_low((1, PAIR))
    small = jnp.zeros((ds, PAIR), f32)
    n_b = BUCKETS // n_f
    for b in range(n_b):
        for p in range(PAIRS):
            value = jnp.where(low, bias_ref[b * HEADS + 2 * p], bias_ref[b * HEADS + 2 * p + 1])
            small = jnp.where(row == b * PAIRS + p, value, small)
    for i, gain in enumerate((ga, gf)):
        tiled = jnp.concatenate([gain[...]] * (PAIR // ds), axis=1)
        small = jnp.where(row == n_b * PAIRS + i, tiled, small)

    def write(c):
        if c == 0:
            a_ref[...] = joined[:, :CUT].astype(bf16)
        else:
            a_ref[:, : 3 * INNER - CUT] = joined[:, CUT:].astype(bf16)
            a_ref[:, 3 * INNER - CUT :] = small.astype(bf16)
        cols = slice(c * half, (c + 1) * half)
        for chunk, ref in enumerate((p0_ref, p1_ref)):
            g = interleaved((wg, wu)[c][...], n_f, chunk).astype(bf16)
            ref[:ds, :] = g[:, :half]
            ref[ds : 2 * ds, :] = g[:, half:]
            ref[2 * ds : 2 * ds + fh, :] = wd[chunk * fh : (chunk + 1) * fh, cols].astype(bf16)
        tail = wo[:, cols]
        pad = p0_ref.shape[0] - (2 * ds + fh + is_)
        if pad:
            tail = jnp.concatenate([tail, jnp.zeros((pad, half), f32)], axis=0)
        p0_ref[2 * ds + fh :, :] = tail.astype(bf16)

    for c in range(2):
        pl.when(core == c)(functools.partial(write, c))


def padded(rows):
    return -(-rows // 16) * 16


def call_prepare(place, n_f, attn_gain, wq, wk, wv, wo, rel_bias, ffn_gain, wg, wu, wd):
    ds, fh, half = wq.shape[0], wd.shape[0] // 2, wo.shape[1] // 2
    vm, sm = pl.BlockSpec(memory_space=pltpu.VMEM), pl.BlockSpec(memory_space=pltpu.SMEM)
    return pl.pallas_call(
        functools.partial(prepare, n_f),
        out_shape=(
            sds((ds, CUT), bf16),
            sds((2 * ds + fh + padded(wo.shape[0]), half), bf16),
            sds((2 * ds + fh, half), bf16),
        ),
        in_specs=[sm, sm] + [vm] * 9,
        out_specs=[vm] * 3,
        name="prepare",
    )(place, rel_bias, wq, wk, wv, wo, wg, wu, wd, attn_gain.reshape(1, -1), ffn_gain.reshape(1, -1))


def attention_forward(G, L, n_z, place_ref, idx_ref, tok_ref, z_ref, x_ref, zc_ref, xc_ref,
                      qkv_ref, probs_ref, mixed_ref, w_ref, gains_ref, table_ref, st_ref, small_ref):
    step = pl.program_id(0)
    place = Place(place_ref, n_z)
    D = tok_ref.shape[-1]
    n_f = 2 * n_z
    ds = D // n_f
    rest = 3 * INNER - CUT

    def assemble(c):
        for xx, k, f in place.shards():
            here, there = ((z_ref, zc_ref), (x_ref, xc_ref))[xx]
            one, two = (here, there) if c == 0 else (there, here)
            w_ref[at(f, ds), :CUT] = one[k]
            w_ref[at(f, ds), CUT:] = two[k, :, :rest]
            small_ref[at(f, ds), :] = two[k, :, rest:].astype(f32)

    @pl.when(step == 0)
    def _():
        for c in range(2):
            pl.when(place.core == c)(functools.partial(assemble, c))
        n_b = BUCKETS // n_f
        ids = idx_ref[...]
        for p in range(PAIRS):
            total = jnp.zeros(ids.shape, f32)
            for b in range(BUCKETS):
                row = b // n_b * ds + (b % n_b) * PAIRS + p
                total = jnp.where(ids == b, small_ref[row : row + 1, :], total)
            table_ref[p] = total
        per = PAIR // ds
        lane = lax.broadcasted_iota(jnp.int32, (1, PAIR), 1) // ds
        gains_ref[...] = jnp.zeros_like(gains_ref)
        for i in range(2):
            for v in range(D // PAIR):
                total = jnp.zeros((1, PAIR), f32)
                for f in range(per):
                    row = (v * per + f) * ds + n_b * PAIRS + i
                    total = jnp.where(lane == f, small_ref[row : row + 1, :], total)
                gains_ref[i : i + 1, v * PAIR : (v + 1) * PAIR] = total

    @pl.when(step * G < place.count)
    def _():
        x = tok_ref[...].reshape(G * L, D).astype(f32)
        normed = (x * inverse_rms(x) * gains_ref[0:1, :]).astype(bf16)
        qkv_ref[...] = nn(normed, w_ref[...]).astype(bf16)
        for s in range(G):
            rows = pl.ds(s * L, L)
            for p in range(PAIRS):
                q = qkv_ref[rows, pl.ds(p * PAIR, PAIR)]
                k = qkv_ref[rows, pl.ds(INNER + p * PAIR, PAIR)]
                st_ref[s, p] = nt(k, split_heads(q))
        for s in range(G):
            for p in range(PAIRS):
                st = st_ref[s, p] + table_ref[p]
                e = jnp.exp(st - jnp.max(st, axis=0, keepdims=True))
                probs_ref[s, p] = (e * (1.0 / jnp.sum(e, axis=0, keepdims=True))).astype(bf16)
        for s in range(G):
            rows = pl.ds(s * L, L)
            for p in range(PAIRS):
                v = qkv_ref[rows, pl.ds(2 * INNER + p * PAIR, PAIR)]
                mixed_ref[rows, pl.ds(p * PAIR, PAIR)] = join_heads(tn(probs_ref[s, p], v)).astype(bf16)


def params():
    return pltpu.CompilerParams(dimension_semantics=("arbitrary",), vmem_limit_bytes=VMEM_LIMIT)


def whole(shape):
    return pl.BlockSpec(shape, lambda i, *_: (0,) * len(shape), pipeline_mode=pl.Buffered(1))


def live_group(i, place, G):
    return jnp.minimum(i, jnp.maximum((place[0] + G - 1) // G - 1, 0))


def series_spec(G, shape, every=False):
    tail = (0,) * (len(shape) - 1)
    return pl.BlockSpec((G,) + shape[1:], lambda i, c: ((i if every else live_group(i, c, G)),) + tail)


def row_spec(G, L, width):
    return pl.BlockSpec((G * L, width), lambda i, c: (live_group(i, c, G), 0))


def cost(rows, per_row, nbytes, exps=0):
    return pl.CostEstimate(flops=2 * rows * per_row, bytes_accessed=nbytes, transcendentals=exps)


def call_attention_forward(place, tokens, pieces):
    S, L, D = tokens.shape
    G, n_z = GROUP, pieces[0].shape[0]
    return pl.pallas_call(
        functools.partial(attention_forward, G, L, n_z),
        out_shape=(
            sds((S * L, 3 * INNER), bf16),
            sds((S, PAIRS, L, PAIR), bf16),
            sds((S * L, INNER), bf16),
            sds((D, 3 * INNER), bf16),
            sds((8, D), f32),
        ),
        grid_spec=pltpu.PrefetchScalarGridSpec(
            num_scalar_prefetch=1,
            grid=(S // G,),
            in_specs=[whole((L, PAIR)), series_spec(G, tokens.shape)] + [whole(piece.shape) for piece in pieces],
            out_specs=[
                row_spec(G, L, 3 * INNER),
                series_spec(G, (S, PAIRS, L, PAIR)),
                row_spec(G, L, INNER),
                whole((D, 3 * INNER)),
                whole((8, D)),
            ],
            scratch_shapes=[
                pltpu.VMEM((PAIRS, L, PAIR), f32),
                pltpu.VMEM((G, PAIRS, L, PAIR), f32),
                pltpu.VMEM((D, PAIR), f32),
            ],
        ),
        compiler_params=params(),
        cost_estimate=cost(S * L, D * 3 * INNER * 4, S * L * 5000),
        name="attention_forward",
    )(place, jnp.asarray(bucket_table(L)), tokens, *pieces)


def gelu_parts(v):
    c = 0.7978845608028654
    v2 = v * v
    t = jnp.tanh(v * (c + (c * 0.044715) * v2))
    half = 0.5 + 0.5 * t
    return v * half, half + (0.5 * v) * (1.0 - t * t) * (c + (3 * c * 0.044715) * v2)


def put_weights(place, first, n_z, pieces, wg, wu, wd, wo):
    z_ref, x_ref, zc_ref, xc_ref = pieces
    n_f = 2 * n_z
    D, FW = wg.shape
    ds, fh, half = D // n_f, FW // n_f, FW // 2

    def assemble(c):
        for xx, k, f in place.shards():
            here, there = ((z_ref, zc_ref), (x_ref, xc_ref))[xx]
            for which, piece in enumerate((here, there) if c == 0 else (there, here)):
                gated = (wg, wu)[which]
                gated[at(f, ds), :half] = piece[k, :ds, :]
                gated[at(f, ds), half:] = piece[k, ds : 2 * ds, :]
                cols = slice(which * half, (which + 1) * half)
                wd[at(f, fh), cols] = piece[k, 2 * ds : 2 * ds + fh, :]
                if first:
                    is_ = INNER // n_f
                    if is_ % 16 == 0:
                        wo[at(f, is_), cols] = piece[k, 2 * ds + fh : 2 * ds + fh + is_, :]
                    else:
                        wo[f, :, cols] = piece[k, 2 * ds + fh :, :]

    for c in range(2):
        pl.when(place.core == c)(functools.partial(assemble, c))


def put_grads(place, n_z, keep, send, ag, au, ad, ao=None):
    n_f = 2 * n_z
    D, FW = ag.shape
    ds, fh, half = D // n_f, FW // n_f, FW // 2

    def write(c):
        for xx, k, f in place.shards():
            for which, ref in enumerate((keep, send) if c == 0 else (send, keep)):
                gated = (ag, au)[which]
                cols = slice(which * half, (which + 1) * half)
                ref[xx, k, :ds, :] = gated[at(f, ds), :half].astype(bf16)
                ref[xx, k, ds : 2 * ds, :] = gated[at(f, ds), half:].astype(bf16)
                ref[xx, k, 2 * ds : 2 * ds + fh, :] = ad[at(f, fh), cols].astype(bf16)
                if ao is not None:
                    is_ = INNER // n_f
                    if is_ % 16 == 0:
                        ref[xx, k, 2 * ds + fh :, :] = ao[at(f, is_), cols].astype(bf16)
                    else:
                        ref[xx, k, 2 * ds + fh :, :] = ao[f, :, cols].astype(bf16)

    for c in range(2):
        pl.when(place.core == c)(functools.partial(write, c))


def ffn_half(G, L, CH, n_z, first, place_ref, *refs):
    if first:
        (tok_ref, ct_ref, mixed_ref, z_ref, x_ref, zc_ref, xc_ref, gains_ref,
         hid_ref, part_ref, gpart_ref, wo_out, keep, send,
         ag, au, ad, wg, wu, wd, n2, gb, gate, up, ga, act, ggr, gur, acc, gn, spread) = refs
    else:
        (hid_ref, ct_ref, mixed_ref, part_ref, gpart_ref, z_ref, x_ref, zc_ref, xc_ref, gains_ref, wo_in,
         out_ref, gh_ref, gm_ref, keep, send, gf_ref,
         ag, au, ad, wg, wu, wd, n2, gb, gate, up, ga, act, ggr, gur, acc, gn, ao, spread) = refs
    step = pl.program_id(0)
    last = pl.num_programs(0) - 1
    R = G * L
    D = ct_ref.shape[-1]
    FW = wg.shape[1]
    n_f = 2 * n_z
    is_ = INNER // n_f
    place = Place(place_ref, n_z)
    count = place.count

    @pl.when(step == 0)
    def _():
        wo = (wo_out if is_ % 16 == 0 else spread) if first else None
        put_weights(place, first, n_z, (z_ref, x_ref, zc_ref, xc_ref), wg, wu, wd, wo)
        if first and is_ % 16:
            wo_out[...] = jnp.concatenate([spread[f, :is_, :].astype(f32) for f in range(n_f)], axis=0).astype(bf16)
        for ref in (ag, au, ad) if first else (ag, au, ad, ao, gf_ref):
            ref[...] = jnp.zeros_like(ref)

    if not first:

        @pl.when(step * G >= count)
        def _():
            out_ref[...] = jnp.zeros_like(out_ref)

    @pl.when(step * G < count)
    def _():
        if first:
            hid_ref[...] = tok_ref[...].reshape(R, D).astype(f32) + nn(mixed_ref[...], wo_out[...])
        h = hid_ref[...]
        n2[...] = (h * inverse_rms(h) * gains_ref[1:2, :]).astype(bf16)
        live = (step * G + lax.broadcasted_iota(jnp.int32, (R, 1), 0) // L) < count
        gb[...] = jnp.where(live, ct_ref[...].reshape(R, D), jnp.zeros((), bf16))
        for c in range(FW // CH):
            cols = pl.ds(c * CH, CH)
            gate[...] = nn(n2[...], wg[:, cols])
            up[...] = nn(n2[...], wu[:, cols])
            ga[...] = nt(gb[...], wd[cols, :])
            for r in range(0, R, L):
                rows = pl.ds(r, L)
                u = up[rows, :]
                a = ga[rows, :]
                g, dg = gelu_parts(gate[rows, :])
                act[rows, :] = (g * u).astype(bf16)
                ggr[rows, :] = (a * u * dg).astype(bf16)
                gur[rows, :] = (a * g).astype(bf16)
            if c == 0:
                acc[...] = nn(act[...], wd[cols, :])
                gn[...] = nt(ggr[...], wg[:, cols]) + nt(gur[...], wu[:, cols])
            else:
                acc[...] += nn(act[...], wd[cols, :])
                gn[...] += nt(ggr[...], wg[:, cols]) + nt(gur[...], wu[:, cols])
            ad[cols, :] += tn(act[...], gb[...])
            ag[:, cols] += tn(n2[...], ggr[...])
            au[:, cols] += tn(n2[...], gur[...])
        if first:
            part_ref[...] = acc[...].astype(bf16)
            gpart_ref[...] = gn[...].astype(bf16)
        else:
            h = hid_ref[...]
            out = h + part_ref[...].astype(f32) + acc[...]
            out_ref[...] = jnp.where(live, out, 0.0).astype(bf16).reshape(G, L, D)
            scale = inverse_rms(h)
            hs = h * scale
            g2 = gn[...] + gpart_ref[...].astype(f32)
            gf_ref[...] += row_sums(g2 * hs)
            g2 = g2 * gains_ref[1:2, :]
            dot = jnp.mean(g2 * hs, axis=-1, keepdims=True)
            gh = (gb[...].astype(f32) + scale * (g2 - hs * dot)).astype(bf16)
            gh_ref[...] = gh
            ao[...] += tn(mixed_ref[...], gh)
            gm_ref[...] = nt(gh, wo_in[...]).astype(bf16)

    @pl.when(step == last)
    def _():
        if first:
            put_grads(place, n_z, keep, send, ag, au, ad)
        elif is_ % 16 == 0:
            put_grads(place, n_z, keep, send, ag, au, ad, ao)
        else:
            for f in range(n_f):
                spread[f, :is_, :] = ao[f * is_ : (f + 1) * is_, :]
            put_grads(place, n_z, keep, send, ag, au, ad, spread)


def call_ffn_half(first, place, pieces, gains, arrays, S, L, D, CH=256):
    G, n_z = GROUP, pieces[0].shape[0]
    R, n_f = G * L, 2 * n_z
    FW = D
    ds, fh, half, is_ = D // n_f, FW // n_f, FW // 2, INNER // n_f
    series = series_spec(G, (S, L, D))
    piece_specs = [whole(piece.shape) for piece in pieces] + [whole(gains.shape)]
    rows = functools.partial(row_spec, G, L)
    extra = 0 if first else padded(is_)
    pack = (2, n_z, 2 * ds + fh + extra, half)
    if first:
        in_specs = [series, series, rows(INNER)] + piece_specs
        out_shape = [sds((S * L, D), f32), sds((S * L, D), bf16), sds((S * L, D), bf16), sds((INNER, D), bf16),
                     sds(pack, bf16), sds(pack, bf16)]
        out_specs = [rows(D), rows(D), rows(D), whole((INNER, D)), whole(pack), whole(pack)]
        operands = arrays + tuple(pieces) + (gains,)
    else:
        *arrays, wo = arrays
        in_specs = [rows(D), series, rows(INNER), rows(D), rows(D)] + piece_specs + [whole(wo.shape)]
        out_shape = [sds((S, L, D), bf16), sds((S * L, D), bf16), sds((S * L, INNER), bf16),
                     sds(pack, bf16), sds(pack, bf16), sds((8, D), f32)]
        out_specs = [series_spec(G, (S, L, D), True), rows(D), rows(INNER), whole(pack), whole(pack), whole((8, D))]
        operands = tuple(arrays) + tuple(pieces) + (gains, wo)
    vm = pltpu.VMEM
    scratch = (
        [vm((D, FW), f32)] * 2 + [vm((FW, D), f32)]
        + [vm((D, FW), bf16)] * 2 + [vm((FW, D), bf16)]
        + [vm((R, D), bf16)] * 2 + [vm((R, CH), f32)] * 3 + [vm((R, CH), bf16)] * 3 + [vm((R, D), f32)] * 2
        + ([] if first else [vm((INNER, D), f32)])
        + [vm((n_f, padded(is_), D) if is_ % 16 else (1, 16, 128), bf16 if first else f32)]
    )
    return pl.pallas_call(
        functools.partial(ffn_half, G, L, CH, n_z, first),
        out_shape=tuple(out_shape),
        grid_spec=pltpu.PrefetchScalarGridSpec(
            num_scalar_prefetch=1, grid=(S // G,), in_specs=in_specs, out_specs=out_specs, scratch_shapes=scratch
        ),
        compiler_params=params(),
        cost_estimate=cost(S * L, 12 * D * FW, S * L * 9000),
        name="ffn_first" if first else "ffn_second",
    )(place, *operands)


def attention_backward(G, L, n_z, place_ref, idx_ref, tok_ref, qkv_ref, probs_ref, gm_ref, w_ref, gains_ref, gf_ref,
                       dqkv, keep, send, aw, ab, dp_ref, ds_ref, small):
    step = pl.program_id(0)
    last = pl.num_programs(0) - 1
    R = G * L
    D = tok_ref.shape[-1]
    place = Place(place_ref, n_z)
    count = place.count

    @pl.when(step == 0)
    def _():
        for ref in (aw, ab):
            ref[...] = jnp.zeros_like(ref)

    @pl.when(step * G < count)
    def _():
        cols = [[pl.ds(b * INNER + p * PAIR, PAIR) for b in range(3)] for p in range(PAIRS)]
        for p in range(PAIRS):
            for s in range(G):
                rows = pl.ds(s * L, L)
                dm = split_heads(gm_ref[rows, pl.ds(p * PAIR, PAIR)])
                dp_ref[s, p] = nt(qkv_ref[rows, cols[p][2]], dm)
                dqkv[rows, cols[p][2]] = nn(probs_ref[s, p], dm).astype(bf16)
        for p in range(PAIRS):
            total = ab[p]
            for s in range(G):
                prf = probs_ref[s, p].astype(f32)
                dp = dp_ref[s, p]
                ds = prf * (dp - jnp.sum(prf * dp, axis=0, keepdims=True))
                total = total + ds
                ds_ref[s, p] = ds.astype(bf16)
            ab[p] = total
        for p in range(PAIRS):
            for s in range(G):
                rows = pl.ds(s * L, L)
                low = ds_ref[s, p]
                dqkv[rows, cols[p][1]] = nn(low, split_heads(qkv_ref[rows, cols[p][0]])).astype(bf16)
                dqkv[rows, cols[p][0]] = join_heads(tn(low, qkv_ref[rows, cols[p][1]])).astype(bf16)
        x = tok_ref[...].reshape(R, D).astype(f32)
        aw[...] += tn((x * inverse_rms(x) * gains_ref[0:1, :]).astype(bf16), dqkv[...])

    @pl.when(step == last)
    def _():
        n_f = 2 * n_z
        ds, n_b, rest = D // n_f, BUCKETS // n_f, 3 * INNER - CUT
        ids = idx_ref[...]
        low = lane_low((1, PAIR))
        lane = lax.broadcasted_iota(jnp.int32, (1, PAIR), 1)
        small[...] = jnp.zeros_like(small)
        for p in range(PAIRS):
            t = ab[p]
            for b in range(BUCKETS):
                by_lane = jnp.sum(jnp.where(ids == b, t, 0.0), axis=0, keepdims=True)
                one = jnp.sum(jnp.where(low, by_lane, 0.0), axis=1, keepdims=True)
                two = jnp.sum(jnp.where(low, 0.0, by_lane), axis=1, keepdims=True)
                row = b // n_b * ds + (b % n_b) * PAIRS + p
                small[row : row + 1, :] = jnp.where(lane == 2, one, two)
        gain = jnp.transpose(gains_ref[...])[:, 0:1]
        one = jnp.sum(aw[...] * w_ref[...].astype(f32), axis=1, keepdims=True) / gain
        two = jnp.sum(jnp.transpose(gf_ref[...]), axis=1, keepdims=True)
        lane = lax.broadcasted_iota(jnp.int32, (D, PAIR), 1)
        small[...] = jnp.where(lane == 0, one, jnp.where(lane == 1, two, small[...]))

        def write(c):
            for xx, k, f in place.shards():
                one, two = (keep, send) if c == 0 else (send, keep)
                one[xx, k] = aw[at(f, ds), :CUT].astype(bf16)
                two[xx, k, :, :rest] = aw[at(f, ds), CUT:].astype(bf16)
                two[xx, k, :, rest:] = small[at(f, ds), :].astype(bf16)

        for c in range(2):
            pl.when(place.core == c)(functools.partial(write, c))


def call_attention_backward(place, n_z, tokens, qkv, probs, gm, w, gains, gf):
    S, L, D = tokens.shape
    G = GROUP
    rows = functools.partial(row_spec, G, L)
    pack = (2, n_z, D // (2 * n_z), CUT)
    vm = pltpu.VMEM
    return pl.pallas_call(
        functools.partial(attention_backward, G, L, n_z),
        out_shape=(sds((S * L, 3 * INNER), bf16), sds(pack, bf16), sds(pack, bf16)),
        grid_spec=pltpu.PrefetchScalarGridSpec(
            num_scalar_prefetch=1,
            grid=(S // G,),
            in_specs=[whole((L, PAIR)), series_spec(G, tokens.shape), rows(3 * INNER), series_spec(G, probs.shape),
                      rows(INNER), whole(w.shape), whole(gains.shape), whole(gf.shape)],
            out_specs=[rows(3 * INNER), whole(pack), whole(pack)],
            scratch_shapes=[
                vm(w.shape, f32), vm((PAIRS, L, PAIR), f32),
                vm((G, PAIRS, L, PAIR), f32), vm((G, PAIRS, L, PAIR), bf16), vm((D, PAIR), f32),
            ],
        ),
        compiler_params=params(),
        cost_estimate=cost(S * L, D * 3 * INNER * 4, S * L * 6000),
        name="attention_backward",
    )(place, jnp.asarray(bucket_table(L)), tokens, qkv, probs, gm, w, gains, gf)


def token_gradient(G, L, place_ref, tok_ref, dqkv_ref, gh_ref, w_ref, gains_ref, gt_ref):
    step = pl.program_id(0)
    D = tok_ref.shape[-1]

    @pl.when(step * G >= place_ref[0])
    def _():
        gt_ref[...] = jnp.zeros_like(gt_ref)

    @pl.when(step * G < place_ref[0])
    def _():
        x = tok_ref[...].reshape(G * L, D).astype(f32)
        scale = inverse_rms(x)
        xs = x * scale
        g = nt(dqkv_ref[...], w_ref[...]) * gains_ref[0:1, :]
        dot = jnp.mean(g * xs, axis=-1, keepdims=True)
        gt_ref[...] = (gh_ref[...].astype(f32) + scale * (g - xs * dot)).astype(bf16).reshape(G, L, D)


def call_token_gradient(place, tokens, dqkv, gh, w, gains):
    S, L, D = tokens.shape
    G = GROUP
    rows = functools.partial(row_spec, G, L)
    return pl.pallas_call(
        functools.partial(token_gradient, G, L),
        out_shape=sds((S, L, D), bf16),
        grid_spec=pltpu.PrefetchScalarGridSpec(
            num_scalar_prefetch=1,
            grid=(S // G,),
            in_specs=[series_spec(G, tokens.shape), rows(3 * INNER), rows(D), whole(w.shape), whole(gains.shape)],
            out_specs=series_spec(G, tokens.shape, True),
        ),
        compiler_params=params(),
        cost_estimate=cost(S * L, D * 3 * INNER * 2, S * L * 5000),
        name="token_gradient",
    )(place, tokens, dqkv, gh, w, gains)


def tree(values):
    while len(values) > 1:
        values = [a + b for a, b in zip(values[0::2], values[1::2])]
    return values[0]


def finish(n_f, n_r, place_ref, *refs):
    packs = [refs[i * n_r : (i + 1) * n_r] for i in range(3)]
    gq, gk, gv, go, gg, gu, gd, ga, gf, gb = refs[3 * n_r :]
    core = place_ref[1]
    ds, is_, fh = gq.shape[0], go.shape[0], gd.shape[0] // 2
    half = go.shape[1] // 2

    def halves(pack):
        here = tree([ref[...].astype(f32) for ref in pack[0::2]])
        there = tree([ref[...].astype(f32) for ref in pack[1::2]])
        return jnp.where(core == 0, here, there), jnp.where(core == 0, there, here)

    one, two = halves(packs[2])
    gq[...] = one[:, :INNER]
    gk[...] = jnp.concatenate([one[:, INNER:CUT], two[:, : 2 * INNER - CUT]], axis=1)
    gv[...] = two[:, 2 * INNER - CUT : 3 * INNER - CUT]
    small = jnp.transpose(two[:, 3 * INNER - CUT :])
    ga[...] = small[0]
    gf[...] = small[1]
    n_b = BUCKETS // n_f
    heads = jnp.concatenate([small[2:3], small[3:4]], axis=0)
    gb[...] = heads[:, : n_b * PAIRS]
    chunks = [halves(packs[0]), halves(packs[1])]
    for which, ref in enumerate((gg, gu)):
        wide = [jnp.concatenate([c[which][:ds], c[which][ds : 2 * ds]], axis=1) for c in chunks]
        width = wide[0].shape[1] // n_f
        ref[...] = jnp.concatenate(
            [w[:, f * width : (f + 1) * width] for f in range(n_f) for w in wide], axis=1
        )
    for chunk, pair in enumerate(chunks):
        for which in range(2):
            gd[chunk * fh : (chunk + 1) * fh, which * half : (which + 1) * half] = pair[which][2 * ds : 2 * ds + fh]
    for which in range(2):
        go[:, which * half : (which + 1) * half] = chunks[1][which][2 * ds + fh : 2 * ds + fh + is_]


def call_finish(place, n_f, n_r, packs, shapes):
    vm, sm = pl.BlockSpec(memory_space=pltpu.VMEM), pl.BlockSpec(memory_space=pltpu.SMEM)
    flat = [piece for pack in packs for piece in pack]
    return pl.pallas_call(
        functools.partial(finish, n_f, n_r),
        out_shape=tuple(sds(shape, f32) for shape in shapes),
        in_specs=[sm] + [vm] * len(flat),
        out_specs=[vm] * len(shapes),
        name="finish",
    )(place, *flat)


def solution(mesh):
    n_r, n_f = mesh.shape["rep"], mesh.shape["fsdp"]
    n_z = n_f // 2

    def over_fsdp(value, distance):
        return lax.ppermute(value, "fsdp", [(i, i ^ distance) for i in range(n_f)])

    def over_rep(value, distance):
        return lax.ppermute(value, "rep", [(i, i ^ distance) for i in range(n_r)])

    def along_z(pack):
        return [pack] + [over_fsdp(pack, 2 * k) for k in range(1, n_z)]

    def halved(keep, got):
        away = (keep[1].astype(f32) + got[1].astype(f32)).astype(bf16)
        return keep[0].astype(f32) + got[0].astype(f32), away

    def joined(here, got):
        here = here + got.astype(f32)
        return here[0], [here[k].astype(bf16) for k in range(1, n_z)]

    def to_z(pieces):
        return [over_fsdp(piece, 2 * (k + 1)) for k, piece in enumerate(pieces)]

    def summed(own, got):
        for value in got:
            own = own + value.astype(f32)
        return own.astype(bf16)

    def replicas(own):
        return [own] + [over_rep(own, m) for m in range(1, n_r)]

    together = lax.optimization_barrier

    def body(tokens, counts, attn_gain, wq, wk, wv, wo, rel_bias, ffn_gain, wg, wu, wd, cotangent):
        S, L, D = tokens.shape
        r, f = lax.axis_index("rep"), lax.axis_index("fsdp")
        place = jnp.stack([counts[0, 0], r % 2, f % 2, f // 2]).astype(jnp.int32)
        pack_a, pack_0, pack_1 = call_prepare(place, n_f, attn_gain, wq, wk, wv, wo, rel_bias, ffn_gain, wg, wu, wd)
        near_a = jnp.stack(along_z(pack_a))
        near_a, pack_0 = together((near_a, pack_0))
        far_a, near_ac, z_0 = over_fsdp(near_a, 1), over_rep(near_a, 1), along_z(pack_0)
        far_a, near_ac, z_0, pack_1 = together((far_a, near_ac, z_0, pack_1))
        far_ac, near_0 = over_rep(far_a, 1), jnp.stack(z_0)
        far_ac, near_0 = together((far_ac, near_0))

        far_0, near_0c, z_1 = over_fsdp(near_0, 1), over_rep(near_0, 1), along_z(pack_1)
        qkv, probs, mixed, w_all, gains = call_attention_forward(place, tokens, (near_a, far_a, near_ac, far_ac))
        qkv, probs, mixed, w_all, gains, far_0, near_0c, z_1 = together(
            (qkv, probs, mixed, w_all, gains, far_0, near_0c, z_1)
        )
        far_0c, near_1 = over_rep(far_0, 1), jnp.stack(z_1)
        far_0c, near_1 = together((far_0c, near_1))

        far_1, near_1c = over_fsdp(near_1, 1), over_rep(near_1, 1)
        hidden, part, gpart, wo_all, keep_0, send_0 = call_ffn_half(
            True, place, (near_0, far_0, near_0c, far_0c), gains, (tokens, cotangent, mixed), S, L, D
        )
        hidden, part, gpart, wo_all, keep_0, send_0, far_1, near_1c = together(
            (hidden, part, gpart, wo_all, keep_0, send_0, far_1, near_1c)
        )
        far_1c = over_rep(far_1, 1)

        got_0 = over_rep(send_0, 1)
        layer_out, gh, gm, keep_1, send_1, gf = call_ffn_half(
            False, place, (near_1, far_1, near_1c, far_1c), gains, (hidden, cotangent, mixed, part, gpart, wo_all), S, L, D
        )
        layer_out, gh, gm, keep_1, send_1, gf, got_0 = together((layer_out, gh, gm, keep_1, send_1, gf, got_0))
        here_0, away_0 = halved(keep_0, got_0)
        away_0, gm = together((away_0, gm))

        got_0, got_1 = over_fsdp(away_0, 1), over_rep(send_1, 1)
        dqkv, keep_2, send_2 = call_attention_backward(place, n_z, tokens, qkv, probs, gm, w_all, gains, gf)
        dqkv, keep_2, send_2, got_0, got_1 = together((dqkv, keep_2, send_2, got_0, got_1))
        own_0, z_0 = joined(here_0, got_0)
        here_1, away_1 = halved(keep_1, got_1)
        dqkv, z_0, away_1 = together((dqkv, z_0, away_1))

        z_0, got_1, got_2 = to_z(z_0), over_fsdp(away_1, 1), over_rep(send_2, 1)
        grad_tokens = call_token_gradient(place, tokens, dqkv, gh, w_all, gains)
        grad_tokens, z_0, got_1, got_2 = together((grad_tokens, z_0, got_1, got_2))
        here_2, away_2 = halved(keep_2, got_2)
        own_1, z_1 = joined(here_1, got_1)
        sum_0 = summed(own_0, z_0)

        own_2, z_2 = joined(here_2, over_fsdp(away_2, 1))
        sum_1 = summed(own_1, to_z(z_1))
        sum_2 = summed(own_2, to_z(z_2))
        n_b = BUCKETS // n_f
        gq, gk, gv, go, gg, gu, gd, grad_attn_gain, grad_ffn_gain, grad_bias = call_finish(
            place, n_f, n_r, [replicas(value) for value in (sum_0, sum_1, sum_2)],
            (wq.shape, wk.shape, wv.shape, wo.shape, wg.shape, wu.shape, wd.shape,
             attn_gain.shape, ffn_gain.shape, (2, n_b * PAIRS)),
        )
        grad_bias = grad_bias.T.reshape(-1)
        return (layer_out, grad_tokens, grad_attn_gain, gq, gk, gv, go, grad_bias, grad_ffn_gain, gg, gu, gd)

    rows, cols, flat = P(("rep", "fsdp"), None, None), P("fsdp", None), P("fsdp")
    return jax.shard_map(
        body,
        mesh=mesh,
        in_specs=(rows, P("rep", "fsdp"), flat, cols, cols, cols, cols, flat, flat, cols, cols, cols, rows),
        out_specs=(rows, rows, flat, cols, cols, cols, cols, flat, flat, cols, cols, cols),
        check_vma=False,
    )
```

```python
import functools

import jax
import jax.numpy as jnp
from jax import lax
from jax.experimental import pallas as pl
from jax.experimental.pallas import tpu as pltpu
from jax.sharding import PartitionSpec as P

HEADS, HDIM, BUCKETS = 6, 64, 32
INNER = HEADS * HDIM
PAIRS = HEADS // 2
PAIR = 2 * HDIM
CUT = 640
GROUP = 8
EPS = 1e-6
VMEM_LIMIT = 18 * 1024 * 1024
bf16, f32 = jnp.bfloat16, jnp.float32
sds = jax.ShapeDtypeStruct


def in_hbm(value):
    return pltpu.with_memory_space_constraint(value, pltpu.HBM)


def nn(a, b):
    return jnp.dot(a, b, preferred_element_type=f32)


def nt(a, b):
    return lax.dot_general(a, b, (((1,), (1,)), ((), ())), preferred_element_type=f32)


def tn(a, b):
    return lax.dot_general(a, b, (((0,), (0,)), ((), ())), preferred_element_type=f32)


def bucket_edges():
    half = BUCKETS // 2
    exact = half // 2
    power = half - exact
    return [
        min(m for m in range(exact, 129) if m**power * exact**k >= 128**k * exact**power) for k in range(1, power)
    ]


def bucket_table(length):
    half = BUCKETS // 2
    exact = half // 2
    shape = (length, PAIR)
    apart = lax.broadcasted_iota(jnp.int32, shape, 0) - lax.broadcasted_iota(jnp.int32, shape, 1) % HDIM
    distance = jnp.abs(apart)
    bucket = jnp.minimum(distance, exact)
    for edge in bucket_edges():
        bucket = bucket + (distance >= edge).astype(jnp.int32)
    return bucket + jnp.where(apart > 0, half, 0)


def lane_low(shape):
    return lax.broadcasted_iota(jnp.int32, shape, 1) < HDIM


def split_heads(pair):
    low, zero = lane_low(pair.shape), jnp.zeros_like(pair)
    return jnp.concatenate([jnp.where(low, pair, zero), jnp.where(low, zero, pair)], axis=0)


def join_heads(both):
    rows = both.shape[0] // 2
    return jnp.where(lane_low((rows, PAIR)), both[:rows], both[rows:])


def row_sums(values):
    rows, width = values.shape
    return jnp.sum(values.reshape(rows // 8, 8, width), axis=0)


def inverse_rms(values):
    return lax.rsqrt(jnp.mean(values * values, axis=-1, keepdims=True) + EPS)


class Place:
    def __init__(self, ref, n_z):
        self.count, self.core, self.x, self.z = ref[0], ref[1], ref[2], ref[3]
        self.n_z = n_z

    def shards(self):
        for xx in range(2):
            for k in range(self.n_z):
                yield xx, k, jnp.bitwise_xor(self.z, k) * 2 + jnp.bitwise_xor(self.x, xx)


def at(shard, size):
    return pl.ds(pl.multiple_of(shard * size, size), size)


def interleaved(values, n_f, chunk):
    width = values.shape[1] // n_f // 2
    return jnp.concatenate(
        [values[:, (2 * f + chunk) * width : (2 * f + chunk + 1) * width] for f in range(n_f)], axis=1
    )


def prepare_attention(n_f, place_ref, bias_ref, wq, wk, wv, ga, gf, a_ref):
    core = place_ref[1]
    ds = wq.shape[0]
    joined = jnp.concatenate([wq[...], wk[...], wv[...]], axis=1)
    row = lax.broadcasted_iota(jnp.int32, (ds, PAIR), 0)
    low = lane_low((1, PAIR))
    small = jnp.zeros((ds, PAIR), f32)
    n_b = BUCKETS // n_f
    for b in range(n_b):
        for p in range(PAIRS):
            value = jnp.where(low, bias_ref[b * HEADS + 2 * p], bias_ref[b * HEADS + 2 * p + 1])
            small = jnp.where(row == b * PAIRS + p, value, small)
    for i, gain in enumerate((ga, gf)):
        tiled = jnp.concatenate([gain[...]] * (PAIR // ds), axis=1)
        small = jnp.where(row == n_b * PAIRS + i, tiled, small)

    def write(c):
        if c == 0:
            a_ref[...] = joined[:, :CUT].astype(bf16)
        else:
            a_ref[:, : 3 * INNER - CUT] = joined[:, CUT:].astype(bf16)
            a_ref[:, 3 * INNER - CUT :] = small.astype(bf16)

    for c in range(2):
        pl.when(core == c)(functools.partial(write, c))


def prepare_ffn(n_f, place_ref, wo, wg, wu, wd, p0_ref, p1_ref):
    core = place_ref[1]
    ds, is_, fh = wg.shape[0], wo.shape[0], wd.shape[0] // 2
    half = wo.shape[1] // 2

    def write(c):
        cols = slice(c * half, (c + 1) * half)
        for chunk, ref in enumerate((p0_ref, p1_ref)):
            g = interleaved((wg, wu)[c][...], n_f, chunk).astype(bf16)
            ref[:ds, :] = g[:, :half]
            ref[ds : 2 * ds, :] = g[:, half:]
            ref[2 * ds : 2 * ds + fh, :] = wd[chunk * fh : (chunk + 1) * fh, cols].astype(bf16)
        tail = wo[:, cols]
        pad = p0_ref.shape[0] - (2 * ds + fh + is_)
        if pad:
            tail = jnp.concatenate([tail, jnp.zeros((pad, half), f32)], axis=0)
        p0_ref[2 * ds + fh :, :] = tail.astype(bf16)

    for c in range(2):
        pl.when(core == c)(functools.partial(write, c))


def padded(rows):
    return -(-rows // 16) * 16


def call_prepare_attention(place, n_f, attn_gain, wq, wk, wv, rel_bias, ffn_gain):
    vm, sm = pl.BlockSpec(memory_space=pltpu.VMEM), pl.BlockSpec(memory_space=pltpu.SMEM)
    return pl.pallas_call(
        functools.partial(prepare_attention, n_f),
        out_shape=sds((wq.shape[0], CUT), bf16),
        in_specs=[sm, sm] + [vm] * 5,
        out_specs=vm,
        name="prepare_attention",
    )(place, rel_bias, wq, wk, wv, attn_gain.reshape(1, -1), ffn_gain.reshape(1, -1))


def call_prepare_ffn(place, n_f, wo, wg, wu, wd):
    ds, fh, half = wg.shape[0], wd.shape[0] // 2, wo.shape[1] // 2
    vm, sm = pl.BlockSpec(memory_space=pltpu.VMEM), pl.BlockSpec(memory_space=pltpu.SMEM)
    return pl.pallas_call(
        functools.partial(prepare_ffn, n_f),
        out_shape=(sds((2 * ds + fh + padded(wo.shape[0]), half), bf16), sds((2 * ds + fh, half), bf16)),
        in_specs=[sm] + [vm] * 4,
        out_specs=[vm] * 2,
        name="prepare_ffn",
    )(place, wo, wg, wu, wd)


def attention_forward(G, L, n_z, place_ref, tok_ref, *refs):
    pieces, refs = refs[:4], refs[4:]
    all_qkv, all_probs, mixed_ref, w_ref, gains_ref, table_ref, st_ref, small_ref = refs
    step = pl.program_id(0)
    place = Place(place_ref, n_z)
    D = tok_ref.shape[-1]
    n_f = 2 * n_z
    ds = D // n_f
    rest = 3 * INNER - CUT

    def assemble(c):
        for xx, k, f in place.shards():
            one, two = pieces[xx].at[k], pieces[2 + xx].at[k]
            one, two = (one, two) if c == 0 else (two, one)
            w_ref[at(f, ds), :CUT] = one[...]
            w_ref[at(f, ds), CUT:] = two[:, :rest]
            small_ref[at(f, ds), :] = two[:, rest:].astype(f32)

    @pl.when(step == 0)
    def _():
        for c in range(2):
            pl.when(place.core == c)(functools.partial(assemble, c))
        n_b = BUCKETS // n_f
        ids = bucket_table(L)
        for p in range(PAIRS):
            total = jnp.zeros(ids.shape, f32)
            for b in range(BUCKETS):
                row = b // n_b * ds + (b % n_b) * PAIRS + p
                total = jnp.where(ids == b, small_ref[row : row + 1, :], total)
            table_ref[p] = total
        per = PAIR // ds
        lane = lax.broadcasted_iota(jnp.int32, (1, PAIR), 1) // ds
        gains_ref[...] = jnp.zeros_like(gains_ref)
        for i in range(2):
            for v in range(D // PAIR):
                total = jnp.zeros((1, PAIR), f32)
                for f in range(per):
                    row = (v * per + f) * ds + n_b * PAIRS + i
                    total = jnp.where(lane == f, small_ref[row : row + 1, :], total)
                gains_ref[i : i + 1, v * PAIR : (v + 1) * PAIR] = total

    @pl.when(step * G < place.count)
    def _():
        mixed, qkv_ref = group_rows(mixed_ref, step, G * L), group_rows(all_qkv, step, G * L)
        probs_ref = all_probs.at[pl.ds(step * G, G)]
        x = tok_ref[...].reshape(G * L, D).astype(f32)
        normed = (x * inverse_rms(x) * gains_ref[0:1, :]).astype(bf16)
        qkv_ref[...] = nn(normed, w_ref[...]).astype(bf16)
        for s in range(G):
            rows = pl.ds(s * L, L)
            for p in range(PAIRS):
                q = qkv_ref[rows, pl.ds(p * PAIR, PAIR)]
                k = qkv_ref[rows, pl.ds(INNER + p * PAIR, PAIR)]
                st_ref[s, p] = nt(k, split_heads(q))
        for s in range(G):
            for p in range(PAIRS):
                st = st_ref[s, p] + table_ref[p]
                e = jnp.exp(st - jnp.max(st, axis=0, keepdims=True))
                probs_ref[s, p] = (e * (1.0 / jnp.sum(e, axis=0, keepdims=True))).astype(bf16)
        for s in range(G):
            rows = pl.ds(s * L, L)
            for p in range(PAIRS):
                v = qkv_ref[rows, pl.ds(2 * INNER + p * PAIR, PAIR)]
                mixed[rows, pl.ds(p * PAIR, PAIR)] = join_heads(tn(probs_ref[s, p], v)).astype(bf16)


def params():
    return pltpu.CompilerParams(dimension_semantics=("arbitrary",), vmem_limit_bytes=VMEM_LIMIT)


def whole(shape):
    return pl.BlockSpec(memory_space=pltpu.VMEM)


def live_group(i, place, G):
    return jnp.minimum(i, jnp.maximum((place[0] + G - 1) // G - 1, 0))


def series_spec(G, shape, every=False):
    tail = (0,) * (len(shape) - 1)
    return pl.BlockSpec((G,) + shape[1:], lambda i, c: ((i if every else live_group(i, c, G)),) + tail)


def row_spec(G, L, width):
    return pl.BlockSpec((G * L, width), lambda i, c: (live_group(i, c, G), 0))


def group_rows(ref, step, rows):
    return ref.at[pl.ds(pl.multiple_of(step * rows, rows), rows), :]


def cost(rows, per_row, nbytes, exps=0):
    return pl.CostEstimate(flops=2 * rows * per_row, bytes_accessed=nbytes, transcendentals=exps)


def call_attention_forward(place, tokens, pieces):
    S, L, D = tokens.shape
    G, n_z = GROUP, pieces[0].shape[0]
    return pl.pallas_call(
        functools.partial(attention_forward, G, L, n_z),
        out_shape=(
            sds((S * L, 3 * INNER), bf16),
            sds((S, PAIRS, L, PAIR), bf16),
            sds((S * L, INNER), bf16),
            sds((D, 3 * INNER), bf16),
            sds((8, D), f32),
        ),
        grid_spec=pltpu.PrefetchScalarGridSpec(
            num_scalar_prefetch=1,
            grid=(S // G,),
            in_specs=[series_spec(G, tokens.shape)] + [whole(piece.shape) for piece in pieces],
            out_specs=[
                whole((S * L, 3 * INNER)),
                whole((S, PAIRS, L, PAIR)),
                whole((S * L, INNER)),
                whole((D, 3 * INNER)),
                whole((8, D)),
            ],
            scratch_shapes=[
                pltpu.VMEM((PAIRS, L, PAIR), f32),
                pltpu.VMEM((G, PAIRS, L, PAIR), f32),
                pltpu.VMEM((D, PAIR), f32),
            ],
        ),
        compiler_params=params(),
        cost_estimate=cost(S * L, D * 3 * INNER * 4, S * L * 5000),
        name="attention_forward",
    )(place, in_hbm(tokens), *pieces)


def gelu_parts(v):
    c = 0.7978845608028654
    v2 = v * v
    t = jnp.tanh(v * (c + (c * 0.044715) * v2))
    half = 0.5 + 0.5 * t
    return v * half, half + (0.5 * v) * (1.0 - t * t) * (c + (3 * c * 0.044715) * v2)


def put_weights(place, first, n_z, pieces, wg, wu, wd, wo):
    n_f = 2 * n_z
    D, FW = wg.shape
    ds, fh, half = D // n_f, FW // n_f, FW // 2

    def assemble(c):
        for xx, k, f in place.shards():
            here, there = pieces[xx].at[k], pieces[2 + xx].at[k]
            for which, piece in enumerate((here, there) if c == 0 else (there, here)):
                gated = (wg, wu)[which]
                gated[at(f, ds), :half] = piece[:ds, :]
                gated[at(f, ds), half:] = piece[ds : 2 * ds, :]
                cols = slice(which * half, (which + 1) * half)
                wd[at(f, fh), cols] = piece[2 * ds : 2 * ds + fh, :]
                if first:
                    is_ = INNER // n_f
                    if is_ % 16 == 0:
                        wo[at(f, is_), cols] = piece[2 * ds + fh : 2 * ds + fh + is_, :]
                    else:
                        wo[f, :, cols] = piece[2 * ds + fh :, :]

    for c in range(2):
        pl.when(place.core == c)(functools.partial(assemble, c))


def put_grads(place, n_z, keep, send, ag, au, ad, ao=None):
    n_f = 2 * n_z
    D, FW = ag.shape
    ds, fh, half = D // n_f, FW // n_f, FW // 2

    def write(c):
        for xx, k, f in place.shards():
            for which, ref in enumerate((keep, send) if c == 0 else (send, keep)):
                gated = (ag, au)[which]
                cols = slice(which * half, (which + 1) * half)
                ref[xx, k, :ds, :] = gated[at(f, ds), :half].astype(bf16)
                ref[xx, k, ds : 2 * ds, :] = gated[at(f, ds), half:].astype(bf16)
                ref[xx, k, 2 * ds : 2 * ds + fh, :] = ad[at(f, fh), cols].astype(bf16)
                if ao is not None:
                    is_ = INNER // n_f
                    if is_ % 16 == 0:
                        ref[xx, k, 2 * ds + fh :, :] = ao[at(f, is_), cols].astype(bf16)
                    else:
                        ref[xx, k, 2 * ds + fh :, :] = ao[f, :, cols].astype(bf16)

    for c in range(2):
        pl.when(place.core == c)(functools.partial(write, c))


def ffn_half(G, L, CH, n_z, first, place_ref, *refs):
    pieces, refs = refs[:4], refs[4:]
    if first:
        (tok_ref, ct_ref, mixed_ref, gains_ref,
         hid_ref, part_ref, gpart_ref, wo_out, keep, send,
         ag, au, ad, wg, wu, wd, n2, gb, gate, up, ga, act, ggr, gur, acc, gn, spread) = refs
    else:
        (hid_ref, ct_ref, mixed_ref, part_ref, gpart_ref, gains_ref, wo_in,
         out_ref, gh_ref, gm_ref, keep, send, gf_ref,
         ag, au, ad, wg, wu, wd, n2, gb, gate, up, ga, act, ggr, gur, acc, gn, ao, spread) = refs
    step = pl.program_id(0)
    last = pl.num_programs(0) - 1
    R = G * L
    D = ct_ref.shape[-1]
    FW = wg.shape[1]
    n_f = 2 * n_z
    is_ = INNER // n_f
    place = Place(place_ref, n_z)
    count = place.count
    group = jnp.minimum(step, (count + G - 1) // G - 1)
    hid_ref, mixed_ref, part_ref, gpart_ref = (
        group_rows(ref, group, R) for ref in (hid_ref, mixed_ref, part_ref, gpart_ref)
    )
    if not first:
        gm_ref, gh_ref = group_rows(gm_ref, group, R), group_rows(gh_ref, group, R)

    @pl.when(step == 0)
    def _():
        wo = (wo_out if is_ % 16 == 0 else spread) if first else None
        put_weights(place, first, n_z, pieces, wg, wu, wd, wo)
        if first and is_ % 16:
            wo_out[...] = jnp.concatenate([spread[f, :is_, :].astype(f32) for f in range(n_f)], axis=0).astype(bf16)
        for ref in (ag, au, ad) if first else (ag, au, ad, ao, gf_ref):
            ref[...] = jnp.zeros_like(ref)

    if not first:

        @pl.when(step * G >= count)
        def _():
            out_ref[...] = jnp.zeros_like(out_ref)

    @pl.when(step * G < count)
    def _():
        if first:
            hid_ref[...] = tok_ref[...].reshape(R, D).astype(f32) + nn(mixed_ref[...], wo_out[...])
        h = hid_ref[...]
        n2[...] = (h * inverse_rms(h) * gains_ref[1:2, :]).astype(bf16)
        live = (step * G + lax.broadcasted_iota(jnp.int32, (R, 1), 0) // L) < count
        gb[...] = jnp.where(live, ct_ref[...].reshape(R, D), jnp.zeros((), bf16))
        for c in range(FW // CH):
            cols = pl.ds(c * CH, CH)
            gate[...] = nn(n2[...], wg[:, cols])
            up[...] = nn(n2[...], wu[:, cols])
            ga[...] = nt(gb[...], wd[cols, :])
            for r in range(0, R, L):
                rows = pl.ds(r, L)
                u = up[rows, :]
                a = ga[rows, :]
                g, dg = gelu_parts(gate[rows, :])
                act[rows, :] = (g * u).astype(bf16)
                ggr[rows, :] = (a * u * dg).astype(bf16)
                gur[rows, :] = (a * g).astype(bf16)
            if c == 0:
                acc[...] = nn(act[...], wd[cols, :])
                gn[...] = nt(ggr[...], wg[:, cols]) + nt(gur[...], wu[:, cols])
            else:
                acc[...] += nn(act[...], wd[cols, :])
                gn[...] += nt(ggr[...], wg[:, cols]) + nt(gur[...], wu[:, cols])
            ad[cols, :] += tn(act[...], gb[...])
            ag[:, cols] += tn(n2[...], ggr[...])
            au[:, cols] += tn(n2[...], gur[...])
        if first:
            part_ref[...] = acc[...].astype(bf16)
            gpart_ref[...] = gn[...].astype(bf16)
        else:
            h = hid_ref[...]
            out = h + part_ref[...].astype(f32) + acc[...]
            out_ref[...] = jnp.where(live, out, 0.0).astype(bf16).reshape(G, L, D)
            scale = inverse_rms(h)
            hs = h * scale
            g2 = gn[...] + gpart_ref[...].astype(f32)
            gf_ref[...] += row_sums(g2 * hs)
            g2 = g2 * gains_ref[1:2, :]
            dot = jnp.mean(g2 * hs, axis=-1, keepdims=True)
            gh = (gb[...].astype(f32) + scale * (g2 - hs * dot)).astype(bf16)
            gh_ref[...] = gh
            ao[...] += tn(mixed_ref[...], gh)
            gm_ref[...] = nt(gh, wo_in[...]).astype(bf16)

    @pl.when(step == last)
    def _():
        if first:
            put_grads(place, n_z, keep, send, ag, au, ad)
        elif is_ % 16 == 0:
            put_grads(place, n_z, keep, send, ag, au, ad, ao)
        else:
            for f in range(n_f):
                spread[f, :is_, :] = ao[f * is_ : (f + 1) * is_, :]
            put_grads(place, n_z, keep, send, ag, au, ad, spread)


def call_ffn_half(first, place, pieces, gains, arrays, S, L, D, CH=256):
    G, n_z = GROUP, pieces[0].shape[0]
    R, n_f = G * L, 2 * n_z
    FW = D
    ds, fh, half, is_ = D // n_f, FW // n_f, FW // 2, INNER // n_f
    series = series_spec(G, (S, L, D))
    piece_specs = [whole(piece.shape) for piece in pieces]
    rows = functools.partial(row_spec, G, L)
    extra = 0 if first else padded(is_)
    pack = (2, n_z, 2 * ds + fh + extra, half)
    if first:
        tokens, ct, mixed = arrays
        in_specs = piece_specs + [series, series, whole(mixed.shape), whole(gains.shape)]
        out_shape = [sds((S * L, D), f32), sds((S * L, D), bf16), sds((S * L, D), bf16), sds((INNER, D), bf16),
                     sds(pack, bf16), sds(pack, bf16)]
        out_specs = [whole(shape.shape) for shape in out_shape]
        operands = tuple(pieces) + (in_hbm(tokens), in_hbm(ct), mixed, gains)
    else:
        hidden, ct, *arrays, wo = arrays
        in_specs = piece_specs + [whole(hidden.shape), series] + [whole(a.shape) for a in (*arrays, gains, wo)]
        out_shape = [pltpu.HBM((S, L, D), bf16), sds((S * L, D), bf16), sds((S * L, INNER), bf16),
                     sds(pack, bf16), sds(pack, bf16), sds((8, D), f32)]
        out_specs = [series_spec(G, (S, L, D), True)] + [whole(pack)] * 5
        operands = tuple(pieces) + (hidden, in_hbm(ct), *arrays, gains, wo)
    vm = pltpu.VMEM
    scratch = (
        [vm((D, FW), f32)] * 2 + [vm((FW, D), f32)]
        + [vm((D, FW), bf16)] * 2 + [vm((FW, D), bf16)]
        + [vm((R, D), bf16)] * 2 + [vm((R, CH), f32)] * 3 + [vm((R, CH), bf16)] * 3 + [vm((R, D), f32)] * 2
        + ([] if first else [vm((INNER, D), f32)])
        + [vm((n_f, padded(is_), D) if is_ % 16 else (1, 16, 128), bf16 if first else f32)]
    )
    return pl.pallas_call(
        functools.partial(ffn_half, G, L, CH, n_z, first),
        out_shape=tuple(out_shape),
        grid_spec=pltpu.PrefetchScalarGridSpec(
            num_scalar_prefetch=1, grid=(S // G,), in_specs=in_specs, out_specs=out_specs, scratch_shapes=scratch
        ),
        compiler_params=params(),
        cost_estimate=cost(S * L, 12 * D * FW, S * L * 9000),
        name="ffn_first" if first else "ffn_second",
    )(place, *operands)


def attention_backward(G, L, n_z, place_ref, tok_ref, qkv_ref, probs_ref, gm_ref, w_ref, gains_ref, gf_ref,
                       dqkv, keep, send, aw, ab, dp_ref, ds_ref, small):
    step = pl.program_id(0)
    last = pl.num_programs(0) - 1
    R = G * L
    D = tok_ref.shape[-1]
    place = Place(place_ref, n_z)
    count = place.count
    group = jnp.minimum(step, (count + G - 1) // G - 1)
    gm_ref, dqkv, qkv_ref = (group_rows(ref, group, R) for ref in (gm_ref, dqkv, qkv_ref))
    probs_ref = probs_ref.at[pl.ds(group * G, G)]

    @pl.when(step == 0)
    def _():
        for ref in (aw, ab):
            ref[...] = jnp.zeros_like(ref)

    @pl.when(step * G < count)
    def _():
        cols = [[pl.ds(b * INNER + p * PAIR, PAIR) for b in range(3)] for p in range(PAIRS)]
        for p in range(PAIRS):
            for s in range(G):
                rows = pl.ds(s * L, L)
                dm = split_heads(gm_ref[rows, pl.ds(p * PAIR, PAIR)])
                dp_ref[s, p] = nt(qkv_ref[rows, cols[p][2]], dm)
                dqkv[rows, cols[p][2]] = nn(probs_ref[s, p], dm).astype(bf16)
        for p in range(PAIRS):
            total = ab[p]
            for s in range(G):
                prf = probs_ref[s, p].astype(f32)
                dp = dp_ref[s, p]
                ds = prf * (dp - jnp.sum(prf * dp, axis=0, keepdims=True))
                total = total + ds
                ds_ref[s, p] = ds.astype(bf16)
            ab[p] = total
        for p in range(PAIRS):
            for s in range(G):
                rows = pl.ds(s * L, L)
                low = ds_ref[s, p]
                dqkv[rows, cols[p][1]] = nn(low, split_heads(qkv_ref[rows, cols[p][0]])).astype(bf16)
                dqkv[rows, cols[p][0]] = join_heads(tn(low, qkv_ref[rows, cols[p][1]])).astype(bf16)
        x = tok_ref[...].reshape(R, D).astype(f32)
        aw[...] += tn((x * inverse_rms(x) * gains_ref[0:1, :]).astype(bf16), dqkv[...])

    @pl.when(step == last)
    def _():
        n_f = 2 * n_z
        ds, n_b, rest = D // n_f, BUCKETS // n_f, 3 * INNER - CUT
        ids = bucket_table(L)
        low = lane_low((1, PAIR))
        small[...] = jnp.zeros_like(small)
        for p in range(PAIRS):
            t = ab[p]
            for b in range(BUCKETS):
                by_lane = jnp.sum(jnp.where(ids == b, t, 0.0), axis=0, keepdims=True)
                one = jnp.sum(jnp.where(low, by_lane, 0.0), axis=1, keepdims=True)
                two = jnp.sum(jnp.where(low, 0.0, by_lane), axis=1, keepdims=True)
                row = b // n_b * ds + (b % n_b) * HEADS + 2 * p
                small[row : row + 1, :] = jnp.broadcast_to(one, (1, PAIR))
                small[row + 1 : row + 2, :] = jnp.broadcast_to(two, (1, PAIR))
        gain = jnp.transpose(gains_ref[...])[:, 0:1]
        one = jnp.sum(aw[...] * w_ref[...].astype(f32), axis=1, keepdims=True) / gain
        two = jnp.sum(jnp.transpose(gf_ref[...]), axis=1, keepdims=True)
        lane = lax.broadcasted_iota(jnp.int32, (D, PAIR), 1)
        small[...] = jnp.where(lane == 0, one, jnp.where(lane == 1, two, small[...]))

        def write(c):
            for xx, k, f in place.shards():
                one, two = keep.at[xx, k], send.at[xx, k]
                one, two = (one, two) if c == 0 else (two, one)
                one[...] = aw[at(f, ds), :CUT].astype(bf16)
                two[:, :rest] = aw[at(f, ds), CUT:].astype(bf16)
                two[:, rest:] = small[at(f, ds), :].astype(bf16)

        for c in range(2):
            pl.when(place.core == c)(functools.partial(write, c))


def call_attention_backward(place, n_z, tokens, qkv, probs, gm, w, gains, gf):
    S, L, D = tokens.shape
    G = GROUP
    pack = (2, n_z, D // (2 * n_z), CUT)
    vm = pltpu.VMEM
    return pl.pallas_call(
        functools.partial(attention_backward, G, L, n_z),
        out_shape=(sds((S * L, 3 * INNER), bf16), sds(pack, bf16), sds(pack, bf16)),
        grid_spec=pltpu.PrefetchScalarGridSpec(
            num_scalar_prefetch=1,
            grid=(S // G,),
            in_specs=[series_spec(G, tokens.shape), whole(qkv.shape), whole(probs.shape),
                      whole(gm.shape), whole(w.shape), whole(gains.shape), whole(gf.shape)],
            out_specs=[whole(pack)] * 3,
            scratch_shapes=[
                vm(w.shape, f32), vm((PAIRS, L, PAIR), f32),
                vm((G, PAIRS, L, PAIR), f32), vm((G, PAIRS, L, PAIR), bf16), vm((D, PAIR), f32),
            ],
        ),
        compiler_params=params(),
        cost_estimate=cost(S * L, D * 3 * INNER * 4, S * L * 6000),
        name="attention_backward",
    )(place, in_hbm(tokens), qkv, probs, gm, w, gains, gf)


def token_gradient(G, L, first_step, place_ref, tok_ref, dqkv_ref, gh_ref, w_ref, gains_ref, *refs):
    gt_ref, done_ref = refs[-2:]
    done_ref[...] = gains_ref[...]
    step = pl.program_id(0) + first_step
    D = tok_ref.shape[-1]
    group = jnp.minimum(step, (place_ref[0] + G - 1) // G - 1)
    dqkv_ref, gh_ref = group_rows(dqkv_ref, group, G * L), group_rows(gh_ref, group, G * L)

    @pl.when(step * G >= place_ref[0])
    def _():
        gt_ref[...] = jnp.zeros_like(gt_ref)

    @pl.when(step * G < place_ref[0])
    def _():
        x = tok_ref[...].reshape(G * L, D).astype(f32)
        scale = inverse_rms(x)
        xs = x * scale
        g = nt(dqkv_ref[...], w_ref[...]) * gains_ref[0:1, :]
        dot = jnp.mean(g * xs, axis=-1, keepdims=True)
        gt_ref[...] = (gh_ref[...].astype(f32) + scale * (g - xs * dot)).astype(bf16).reshape(G, L, D)


def call_token_gradient(place, tokens, dqkv, gh, w, gains, part, earlier=None):
    S, L, D = tokens.shape
    G = GROUP
    steps = S // G // 2 if part == 0 else S // G - S // G // 2
    shift = part * (S // G // 2)

    def rows(width):
        return pl.BlockSpec((G * L, width), lambda i, c: (live_group(i + shift, c, G), 0))

    def series(every):
        return pl.BlockSpec((G, L, D), lambda i, c: (i + shift if every else live_group(i + shift, c, G), 0, 0))

    more = [] if earlier is None else [earlier]
    return pl.pallas_call(
        functools.partial(token_gradient, G, L, shift),
        out_shape=(pltpu.HBM((S, L, D), bf16), sds(gains.shape, f32)),
        grid_spec=pltpu.PrefetchScalarGridSpec(
            num_scalar_prefetch=1,
            grid=(steps,),
            in_specs=[series(False), whole(dqkv.shape), whole(gh.shape), whole(w.shape), whole(gains.shape)]
            + [pl.BlockSpec(memory_space=pl.ANY)] * len(more),
            out_specs=(series(True), whole(gains.shape)),
        ),
        input_output_aliases={6: 0} if more else {},
        compiler_params=params(),
        cost_estimate=cost(S * L // 2, D * 3 * INNER * 2, S * L * 2500),
        name="token_gradient",
    )(place, in_hbm(tokens), dqkv, gh, w, gains, *more)


def finish(n_f, place_ref, *refs):
    packs = [refs[2 * i : 2 * i + 2] for i in range(3)]
    gq, gk, gv, go, gg, gu, gd, ga, gf, gb = refs[7:]
    core = place_ref[1]
    ds, is_, fh = gq.shape[0], go.shape[0], gd.shape[0] // 2
    half = go.shape[1] // 2

    def halves(pack):
        here, there = pack[0][...].astype(f32), pack[1][...].astype(f32)
        return jnp.where(core == 0, here, there), jnp.where(core == 0, there, here)

    one, two = halves(packs[2])
    gq[...] = one[:, :INNER]
    gk[...] = jnp.concatenate([one[:, INNER:CUT], two[:, : 2 * INNER - CUT]], axis=1)
    gv[...] = two[:, 2 * INNER - CUT : 3 * INNER - CUT]
    small = jnp.transpose(two[:, 3 * INNER - CUT :])
    ga[...] = small[0]
    gf[...] = small[1]
    gb[...] = small[2, : BUCKETS // n_f * HEADS]
    chunks = [halves(packs[0]), halves(packs[1])]
    for which, ref in enumerate((gg, gu)):
        wide = [jnp.concatenate([c[which][:ds], c[which][ds : 2 * ds]], axis=1) for c in chunks]
        width = wide[0].shape[1] // n_f
        ref[...] = jnp.concatenate(
            [w[:, f * width : (f + 1) * width] for f in range(n_f) for w in wide], axis=1
        )
    for chunk, pair in enumerate(chunks):
        for which in range(2):
            gd[chunk * fh : (chunk + 1) * fh, which * half : (which + 1) * half] = pair[which][2 * ds : 2 * ds + fh]
    for which in range(2):
        go[:, which * half : (which + 1) * half] = chunks[1][which][2 * ds + fh : 2 * ds + fh + is_]


def call_finish(place, n_f, packs, shapes, after):
    vm, sm = pl.BlockSpec(memory_space=pltpu.VMEM), pl.BlockSpec(memory_space=pltpu.SMEM)
    flat = [piece for pack in packs for piece in pack]
    return pl.pallas_call(
        functools.partial(finish, n_f),
        out_shape=tuple(sds(shape, f32) for shape in shapes),
        in_specs=[sm] + [vm] * len(flat) + [pl.BlockSpec(memory_space=pl.ANY)],
        out_specs=[vm] * len(shapes),
        name="finish",
    )(place, *flat, after)


def solution(mesh):
    n_r, n_f = mesh.shape["rep"], mesh.shape["fsdp"]
    n_z = n_f // 2

    def over_fsdp(value, distance):
        return lax.ppermute(value, "fsdp", [(i, i ^ distance) for i in range(n_f)])

    def over_rep(value, distance):
        return lax.ppermute(value, "rep", [(i, i ^ distance) for i in range(n_r)])

    def along_z(pack):
        return [pack] + [over_fsdp(pack, 2 * k) for k in range(1, n_z)]

    def halved(keep, got):
        away = (keep[1].astype(f32) + got[1].astype(f32)).astype(bf16)
        return keep[0].astype(f32) + got[0].astype(f32), away

    def joined(here, got):
        here = here + got.astype(f32)
        return here[0], [here[k].astype(bf16) for k in range(1, n_z)]

    def to_z(pieces):
        return [over_fsdp(piece, 2 * (k + 1)) for k, piece in enumerate(pieces)]

    def summed(own, got):
        for value in got:
            own = own + value.astype(f32)
        return own.astype(bf16)

    def replicas(own):
        distance = 2
        while distance < n_r:
            own = (own.astype(f32) + over_rep(own, distance).astype(f32)).astype(bf16)
            distance *= 2
        return own, over_rep(own, 1)

    together = lax.optimization_barrier

    def body(tokens, counts, attn_gain, wq, wk, wv, wo, rel_bias, ffn_gain, wg, wu, wd, cotangent):
        S, L, D = tokens.shape
        r, f = lax.axis_index("rep"), lax.axis_index("fsdp")
        place = in_hbm(jnp.stack([counts[0, 0], r % 2, f % 2, f // 2]).astype(jnp.int32))
        pack_a = call_prepare_attention(place, n_f, attn_gain, wq, wk, wv, rel_bias, ffn_gain)
        pack_0, pack_1 = call_prepare_ffn(place, n_f, wo, wg, wu, wd)

        z_a, pack_0, pack_1 = together((along_z(pack_a), pack_0, pack_1))
        near_a = jnp.stack(z_a)
        z_0 = along_z(pack_0)
        far_a, near_ac = over_fsdp(near_a, 1), over_rep(near_a, 1)
        far_a, near_ac, z_0, pack_1 = together((far_a, near_ac, z_0, pack_1))
        far_ac, near_0 = over_rep(far_a, 1), jnp.stack(z_0)
        far_ac, near_0 = together((far_ac, near_0))

        far_0, near_0c, z_1 = over_fsdp(near_0, 1), over_rep(near_0, 1), along_z(pack_1)
        qkv, probs, mixed, w_all, gains = call_attention_forward(place, tokens, (near_a, far_a, near_ac, far_ac))
        gains, far_0, near_0c, z_1 = together((gains, far_0, near_0c, z_1))
        far_0c, near_1 = over_rep(far_0, 1), jnp.stack(z_1)
        far_0c, near_1 = together((far_0c, near_1))

        far_1, near_1c = over_fsdp(near_1, 1), over_rep(near_1, 1)
        hidden, part, gpart, wo_all, keep_0, send_0 = call_ffn_half(
            True, place, (near_0, far_0, near_0c, far_0c), gains, (tokens, cotangent, mixed), S, L, D
        )
        wo_all, keep_0, send_0, far_1, near_1c = together((wo_all, keep_0, send_0, far_1, near_1c))

        far_1c = over_rep(far_1, 1)
        got_0 = over_rep(send_0, 1)
        layer_out, gh, gm, keep_1, send_1, gf = call_ffn_half(
            False, place, (near_1, far_1, near_1c, far_1c), gains, (hidden, cotangent, mixed, part, gpart, wo_all), S, L, D
        )
        keep_1, send_1, gf, got_0 = together((keep_1, send_1, gf, got_0))
        here_0, away_0 = halved(keep_0, got_0)
        away_0, gf = together((away_0, gf))

        got_0, got_1 = over_fsdp(away_0, 1), over_rep(send_1, 1)
        dqkv, keep_2, send_2 = call_attention_backward(place, n_z, tokens, qkv, probs, gm, w_all, gains, gf)
        keep_2, send_2, got_0, got_1 = together((keep_2, send_2, got_0, got_1))
        own_0, z_0 = joined(here_0, got_0)
        here_1, away_1 = halved(keep_1, got_1)
        gains, z_0, away_1 = together((gains, z_0, away_1))

        z_0, got_1, got_2 = to_z(z_0), over_fsdp(away_1, 1), over_rep(send_2, 1)
        half_tokens, done = call_token_gradient(place, tokens, dqkv, gh, w_all, gains, 0)
        done, z_0, got_1, got_2 = together((done, z_0, got_1, got_2))
        sum_0 = summed(own_0, z_0)
        here_2, away_2 = halved(keep_2, got_2)
        own_1, z_1 = joined(here_1, got_1)
        done, away_2, z_1, sum_0 = together((done, away_2, z_1, sum_0))
        got_2, z_1 = over_fsdp(away_2, 1), to_z(z_1)
        grad_tokens, done = call_token_gradient(place, tokens, dqkv, gh, w_all, done, 1, half_tokens)
        done, got_2, z_1 = together((done, got_2, z_1))
        own_2, z_2 = joined(here_2, got_2)
        sum_1 = summed(own_1, z_1)
        sum_2 = summed(own_2, to_z(z_2))
        gq, gk, gv, go, gg, gu, gd, grad_attn_gain, grad_ffn_gain, grad_bias = call_finish(
            place, n_f, [replicas(value) for value in (sum_0, sum_1, sum_2)],
            (wq.shape, wk.shape, wv.shape, wo.shape, wg.shape, wu.shape, wd.shape,
             attn_gain.shape, ffn_gain.shape, rel_bias.shape), done,
        )
        return (layer_out, grad_tokens, grad_attn_gain, gq, gk, gv, go, grad_bias, grad_ffn_gain, gg, gu, gd)

    rows, cols, flat = P(("rep", "fsdp"), None, None), P("fsdp", None), P("fsdp")
    return jax.shard_map(
        body,
        mesh=mesh,
        in_specs=(rows, P("rep", "fsdp"), flat, cols, cols, cols, cols, flat, flat, cols, cols, cols, rows),
        out_specs=(rows, rows, flat, cols, cols, cols, cols, flat, flat, cols, cols, cols),
        check_vma=False,
    )
```

```python
import functools

import jax
import jax.numpy as jnp
from jax import lax
from jax.experimental import pallas as pl
from jax.experimental.pallas import tpu as pltpu
from jax.sharding import PartitionSpec as P

HEADS, HDIM, BUCKETS = 6, 64, 32
INNER = HEADS * HDIM
PAIRS = HEADS // 2
PAIR = 2 * HDIM
CUT = 640
GROUP = 8
EPS = 1e-6
bf16, f32 = jnp.bfloat16, jnp.float32
sds = jax.ShapeDtypeStruct


def in_hbm(value):
    return pltpu.with_memory_space_constraint(value, pltpu.HBM)


def nn(a, b):
    return jnp.dot(a, b, preferred_element_type=f32)


def nt(a, b):
    return lax.dot_general(a, b, (((1,), (1,)), ((), ())), preferred_element_type=f32)


def tn(a, b):
    return lax.dot_general(a, b, (((0,), (0,)), ((), ())), preferred_element_type=f32)


def bucket_edges():
    half = BUCKETS // 2
    exact = half // 2
    power = half - exact
    return [
        min(m for m in range(exact, 129) if m**power * exact**k >= 128**k * exact**power) for k in range(1, power)
    ]


def bucket_table(length):
    half = BUCKETS // 2
    exact = half // 2
    shape = (length, PAIR)
    apart = lax.broadcasted_iota(jnp.int32, shape, 0) - lax.broadcasted_iota(jnp.int32, shape, 1) % HDIM
    distance = jnp.abs(apart)
    bucket = jnp.minimum(distance, exact)
    for edge in bucket_edges():
        bucket = bucket + (distance >= edge).astype(jnp.int32)
    return bucket + jnp.where(apart > 0, half, 0)


def lane_low(shape):
    return lax.broadcasted_iota(jnp.int32, shape, 1) < HDIM


def split_heads(pair):
    low, zero = lane_low(pair.shape), jnp.zeros_like(pair)
    return jnp.concatenate([jnp.where(low, pair, zero), jnp.where(low, zero, pair)], axis=0)


def join_heads(both):
    rows = both.shape[0] // 2
    return jnp.where(lane_low((rows, PAIR)), both[:rows], both[rows:])


def row_sums(values):
    rows, width = values.shape
    return jnp.sum(values.reshape(rows // 8, 8, width), axis=0)


def inverse_rms(values):
    return lax.rsqrt(jnp.mean(values * values, axis=-1, keepdims=True) + EPS)


class Place:
    def __init__(self, ref, n_z):
        self.count, self.core, self.x, self.z = ref[0], ref[1], ref[2], ref[3]
        self.n_z = n_z

    def shards(self):
        for xx in range(2):
            for k in range(self.n_z):
                yield xx, k, jnp.bitwise_xor(self.z, k) * 2 + jnp.bitwise_xor(self.x, xx)


def at(shard, size):
    return pl.ds(pl.multiple_of(shard * size, size), size)


def interleaved(values, n_f, chunk):
    width = values.shape[1] // n_f // 2
    return jnp.concatenate(
        [values[:, (2 * f + chunk) * width : (2 * f + chunk + 1) * width] for f in range(n_f)], axis=1
    )


def prepare_attention(n_f, place_ref, bias_ref, wq, wk, wv, ga, gf, a_ref):
    core = place_ref[1]
    ds = wq.shape[0]
    joined = jnp.concatenate([wq[...], wk[...], wv[...]], axis=1)
    row = lax.broadcasted_iota(jnp.int32, (ds, PAIR), 0)
    low = lane_low((1, PAIR))
    small = jnp.zeros((ds, PAIR), f32)
    n_b = BUCKETS // n_f
    for b in range(n_b):
        for p in range(PAIRS):
            value = jnp.where(low, bias_ref[b * HEADS + 2 * p], bias_ref[b * HEADS + 2 * p + 1])
            small = jnp.where(row == b * PAIRS + p, value, small)
    for i, gain in enumerate((ga, gf)):
        tiled = jnp.concatenate([gain[...]] * (PAIR // ds), axis=1)
        small = jnp.where(row == n_b * PAIRS + i, tiled, small)

    def write(c):
        if c == 0:
            a_ref[...] = joined[:, :CUT].astype(bf16)
        else:
            a_ref[:, : 3 * INNER - CUT] = joined[:, CUT:].astype(bf16)
            a_ref[:, 3 * INNER - CUT :] = small.astype(bf16)

    for c in range(2):
        pl.when(core == c)(functools.partial(write, c))


def prepare_ffn(n_f, place_ref, wo, wg, wu, wd, p0_ref, p1_ref):
    core = place_ref[1]
    ds, is_, fh = wg.shape[0], wo.shape[0], wd.shape[0] // 2
    half = wo.shape[1] // 2

    def write(c):
        cols = slice(c * half, (c + 1) * half)
        for chunk, ref in enumerate((p0_ref, p1_ref)):
            g = interleaved((wg, wu)[c][...], n_f, chunk).astype(bf16)
            ref[:ds, :] = g[:, :half]
            ref[ds : 2 * ds, :] = g[:, half:]
            ref[2 * ds : 2 * ds + fh, :] = wd[chunk * fh : (chunk + 1) * fh, cols].astype(bf16)
        tail = wo[:, cols]
        pad = p0_ref.shape[0] - (2 * ds + fh + is_)
        if pad:
            tail = jnp.concatenate([tail, jnp.zeros((pad, half), f32)], axis=0)
        p0_ref[2 * ds + fh :, :] = tail.astype(bf16)

    for c in range(2):
        pl.when(core == c)(functools.partial(write, c))


def small_params():
    return pltpu.CompilerParams(vmem_limit_bytes=12 * 1024 * 1024)


def padded(rows):
    return -(-rows // 16) * 16


def call_prepare_attention(place, n_f, attn_gain, wq, wk, wv, rel_bias, ffn_gain):
    vm, sm = pl.BlockSpec(memory_space=pltpu.VMEM), pl.BlockSpec(memory_space=pltpu.SMEM)
    return pl.pallas_call(
        functools.partial(prepare_attention, n_f),
        out_shape=sds((wq.shape[0], CUT), bf16),
        in_specs=[sm, sm] + [vm] * 5,
        out_specs=vm,
        name="prepare_attention",
    )(place, rel_bias, wq, wk, wv, attn_gain.reshape(1, -1), ffn_gain.reshape(1, -1))


def call_prepare_ffn(place, n_f, wo, wg, wu, wd):
    ds, fh, half = wg.shape[0], wd.shape[0] // 2, wo.shape[1] // 2
    vm, sm = pl.BlockSpec(memory_space=pltpu.VMEM), pl.BlockSpec(memory_space=pltpu.SMEM)
    return pl.pallas_call(
        functools.partial(prepare_ffn, n_f),
        out_shape=(sds((2 * ds + fh + padded(wo.shape[0]), half), bf16), sds((2 * ds + fh, half), bf16)),
        in_specs=[sm] + [vm] * 4,
        out_specs=[vm] * 2,
        name="prepare_ffn",
    )(place, wo, wg, wu, wd)


def attention_forward(G, L, n_z, place_ref, tok_ref, *refs):
    pieces, refs = refs[:4], refs[4:]
    all_qkv, probs_ref, mixed_ref, w_ref, gains_ref, table_ref, st_ref, small_ref = refs
    step = pl.program_id(0)
    place = Place(place_ref, n_z)
    D = tok_ref.shape[-1]
    n_f = 2 * n_z
    ds = D // n_f
    rest = 3 * INNER - CUT

    def assemble(c):
        for xx, k, f in place.shards():
            one, two = pieces[xx].at[k], pieces[2 + xx].at[k]
            one, two = (one, two) if c == 0 else (two, one)
            w_ref[at(f, ds), :CUT] = one[...]
            w_ref[at(f, ds), CUT:] = two[:, :rest]
            small_ref[at(f, ds), :] = two[:, rest:].astype(f32)

    @pl.when(step == 0)
    def _():
        for c in range(2):
            pl.when(place.core == c)(functools.partial(assemble, c))
        n_b = BUCKETS // n_f
        ids = bucket_table(L)
        for p in range(PAIRS):
            total = jnp.zeros(ids.shape, f32)
            for b in range(BUCKETS):
                row = b // n_b * ds + (b % n_b) * PAIRS + p
                total = jnp.where(ids == b, small_ref[row : row + 1, :], total)
            table_ref[p] = total
        per = PAIR // ds
        lane = lax.broadcasted_iota(jnp.int32, (1, PAIR), 1) // ds
        gains_ref[...] = jnp.zeros_like(gains_ref)
        for i in range(2):
            for v in range(D // PAIR):
                total = jnp.zeros((1, PAIR), f32)
                for f in range(per):
                    row = (v * per + f) * ds + n_b * PAIRS + i
                    total = jnp.where(lane == f, small_ref[row : row + 1, :], total)
                gains_ref[i : i + 1, v * PAIR : (v + 1) * PAIR] = total

    @pl.when(step * G < place.count)
    def _():
        mixed, qkv_ref = group_rows(mixed_ref, step, G * L), group_rows(all_qkv, step, G * L)
        x = tok_ref[...].reshape(G * L, D).astype(f32)
        normed = (x * inverse_rms(x) * gains_ref[0:1, :]).astype(bf16)
        qkv_ref[...] = nn(normed, w_ref[...]).astype(bf16)
        for s in range(G):
            rows = pl.ds(s * L, L)
            for p in range(PAIRS):
                q = qkv_ref[rows, pl.ds(p * PAIR, PAIR)]
                k = qkv_ref[rows, pl.ds(INNER + p * PAIR, PAIR)]
                st_ref[s, p] = nt(k, split_heads(q))
        for s in range(G):
            for p in range(PAIRS):
                st = st_ref[s, p] + table_ref[p]
                e = jnp.exp(st - jnp.max(st, axis=0, keepdims=True))
                probs_ref[s, p] = (e * (1.0 / jnp.sum(e, axis=0, keepdims=True))).astype(bf16)
        for s in range(G):
            rows = pl.ds(s * L, L)
            for p in range(PAIRS):
                v = qkv_ref[rows, pl.ds(2 * INNER + p * PAIR, PAIR)]
                mixed[rows, pl.ds(p * PAIR, PAIR)] = join_heads(tn(probs_ref[s, p], v)).astype(bf16)


MIB_FORWARD, MIB_FFN, MIB_BACKWARD, MIB_TOKENS, MIB_RESULT = 12, 18, 14, 10, 10


def params(mib):
    return pltpu.CompilerParams(dimension_semantics=("arbitrary",), vmem_limit_bytes=mib * 1024 * 1024)


def whole(shape):
    return pl.BlockSpec(memory_space=pltpu.VMEM)


def live_group(i, place, G):
    return jnp.minimum(i, jnp.maximum((place[0] + G - 1) // G - 1, 0))


def series_spec(G, shape, every=False):
    tail = (0,) * (len(shape) - 1)
    return pl.BlockSpec((G,) + shape[1:], lambda i, c: ((i if every else live_group(i, c, G)),) + tail)


def row_spec(G, L, width):
    return pl.BlockSpec((G * L, width), lambda i, c: (live_group(i, c, G), 0))


def group_rows(ref, step, rows):
    return ref.at[pl.ds(pl.multiple_of(step * rows, rows), rows), :]


def cost(rows, per_row, nbytes, exps=0):
    return pl.CostEstimate(flops=2 * rows * per_row, bytes_accessed=nbytes, transcendentals=exps)


def call_attention_forward(place, tokens, pieces):
    S, L, D = tokens.shape
    G, n_z = GROUP, pieces[0].shape[0]
    return pl.pallas_call(
        functools.partial(attention_forward, G, L, n_z),
        out_shape=(
            sds((S * L, 3 * INNER), bf16),
            pltpu.HBM((S, PAIRS, L, PAIR), bf16),
            sds((S * L, INNER), bf16),
            sds((D, 3 * INNER), bf16),
            sds((8, D), f32),
        ),
        grid_spec=pltpu.PrefetchScalarGridSpec(
            num_scalar_prefetch=1,
            grid=(S // G,),
            in_specs=[series_spec(G, tokens.shape)] + [whole(piece.shape) for piece in pieces],
            out_specs=[
                whole((S * L, 3 * INNER)),
                series_spec(G, (S, PAIRS, L, PAIR)),
                whole((S * L, INNER)),
                whole((D, 3 * INNER)),
                whole((8, D)),
            ],
            scratch_shapes=[
                pltpu.VMEM((PAIRS, L, PAIR), f32),
                pltpu.VMEM((G, PAIRS, L, PAIR), f32),
                pltpu.VMEM((D, PAIR), f32),
            ],
        ),
        compiler_params=params(MIB_FORWARD),
        cost_estimate=cost(S * L, D * 3 * INNER * 4, S * L * 5000),
        name="attention_forward",
    )(place, in_hbm(tokens), *pieces)


def gelu_parts(v):
    c = 0.7978845608028654
    v2 = v * v
    t = jnp.tanh(v * (c + (c * 0.044715) * v2))
    half = 0.5 + 0.5 * t
    return v * half, half + (0.5 * v) * (1.0 - t * t) * (c + (3 * c * 0.044715) * v2)


def put_weights(place, pieces, wgu, wd, wo=None):
    FW, D = wd.shape

    def assemble(c):
        for f, here, there in pieces:
            for which, piece in enumerate((here, there) if c == 0 else (there, here)):
                n_f = len(pieces)
                ds, fh, half, is_ = D // n_f, FW // n_f, FW // 2, INNER // n_f
                for part in range(2):
                    start = (2 * part + which) * half
                    wgu[at(f, ds), start : start + half] = piece[part * ds : (part + 1) * ds, :]
                cols = slice(which * half, (which + 1) * half)
                wd[at(f, fh), cols] = piece[2 * ds : 2 * ds + fh, :]
                if wo is None:
                    continue
                if is_ % 16 == 0:
                    wo[at(f, is_), cols] = piece[2 * ds + fh : 2 * ds + fh + is_, :]
                else:
                    wo[f, :, cols] = piece[2 * ds + fh :, :]

    for c in range(2):
        pl.when(place.core == c)(functools.partial(assemble, c))


def put_grads(place, n_z, keep, send, agu, ad, ao=None):
    n_f = 2 * n_z
    FW, D = ad.shape
    ds, fh, half = D // n_f, FW // n_f, FW // 2

    def write(c):
        for xx, k, f in place.shards():
            for which, ref in enumerate((keep, send) if c == 0 else (send, keep)):
                for part in range(2):
                    start = (2 * part + which) * half
                    ref[xx, k, part * ds : (part + 1) * ds, :] = agu[at(f, ds), start : start + half].astype(bf16)
                cols = slice(which * half, (which + 1) * half)
                ref[xx, k, 2 * ds : 2 * ds + fh, :] = ad[at(f, fh), cols].astype(bf16)
                if ao is not None:
                    is_ = INNER // n_f
                    if is_ % 16 == 0:
                        ref[xx, k, 2 * ds + fh :, :] = ao[at(f, is_), cols].astype(bf16)
                    else:
                        ref[xx, k, 2 * ds + fh :, :] = ao[f, :, cols].astype(bf16)

    for c in range(2):
        pl.when(place.core == c)(functools.partial(write, c))


def ffn_half(G, L, n_z, first, place_ref, *refs):
    n_f = 2 * n_z
    place = Place(place_ref, n_z)
    pieces, refs = refs[:4], refs[4:]
    pieces = [(f, pieces[xx].at[k], pieces[2 + xx].at[k]) for xx, k, f in place.shards()]
    if first:
        (tok_ref, ct_ref, mixed_ref, gains_ref,
         hid_ref, act, gpart_ref, wd, wo_out, keep, send,
         agu, ad, wgu, n2, gb, gu, ga, low, gn, spread) = refs
    else:
        (hid_ref, ct_ref, mixed_ref, gpart_ref, gains_ref, wo_in,
         gh_ref, gm_ref, act, wd, keep, send, gf_ref,
         agu, ad, wgu, n2, gb, gu, ga, low, gn, ao, spread) = refs
    step = pl.program_id(0)
    last = pl.num_programs(0) - 1
    R = G * L
    FW, D = wd.shape
    CH = FW // 2
    is_ = INNER // n_f
    count = place.count
    group = jnp.minimum(step, (count + G - 1) // G - 1)
    hid_ref, mixed_ref, act, gpart_ref = (group_rows(ref, group, R) for ref in (hid_ref, mixed_ref, act, gpart_ref))
    if not first:
        gm_ref, gh_ref = group_rows(gm_ref, group, R), group_rows(gh_ref, group, R)

    @pl.when(step == 0)
    def _():
        wo = (wo_out if is_ % 16 == 0 else spread) if first else None
        put_weights(place, pieces, wgu, wd, wo)
        if first and is_ % 16:
            wo_out[...] = jnp.concatenate([spread[f, :is_, :].astype(f32) for f in range(n_f)], axis=0).astype(bf16)
        for ref in (agu, ad) if first else (agu, ad, ao, gf_ref):
            ref[...] = jnp.zeros_like(ref)

    @pl.when(step * G < count)
    def _():
        if first:
            hid_ref[...] = tok_ref[...].reshape(R, D).astype(f32) + nn(mixed_ref[...], wo_out[...])
        h = hid_ref[...]
        n2[...] = (h * inverse_rms(h) * gains_ref[1:2, :]).astype(bf16)
        live = (step * G + lax.broadcasted_iota(jnp.int32, (R, 1), 0) // L) < count
        gb[...] = jnp.where(live, ct_ref[...].reshape(R, D), jnp.zeros((), bf16))
        for c in range(2):
            cols, both = pl.ds(c * CH, CH), pl.ds(2 * c * CH, 2 * CH)
            gu[c] = nn(n2[...], wgu[:, both])
            ga[c] = nt(gb[...], wd[cols, :])
        for c in range(2):
            cols, both = pl.ds(c * CH, CH), pl.ds(2 * c * CH, 2 * CH)
            for r in range(0, R, L):
                rows = pl.ds(r, L)
                u = gu[c, rows, CH:]
                a = ga[c, rows, :]
                g, dg = gelu_parts(gu[c, rows, :CH])
                act[rows, cols] = (g * u).astype(bf16)
                low[c, rows, :CH] = (a * u * dg).astype(bf16)
                low[c, rows, CH:] = (a * g).astype(bf16)
            if c == 0:
                gn[...] = nt(low[c], wgu[:, both])
            else:
                gn[...] += nt(low[c], wgu[:, both])
            ad[cols, :] += tn(act[:, cols], gb[...])
            agu[:, both] += tn(n2[...], low[c])
        if first:
            gpart_ref[...] = gn[...].astype(bf16)
        else:
            h = hid_ref[...]
            scale = inverse_rms(h)
            hs = h * scale
            g2 = gn[...] + gpart_ref[...].astype(f32)
            gf_ref[...] += row_sums(g2 * hs)
            g2 = g2 * gains_ref[1:2, :]
            dot = jnp.mean(g2 * hs, axis=-1, keepdims=True)
            gh = (gb[...].astype(f32) + scale * (g2 - hs * dot)).astype(bf16)
            gh_ref[...] = gh
            ao[...] += tn(mixed_ref[...], gh)
            gm_ref[...] = nt(gh, wo_in[...]).astype(bf16)

    @pl.when(step == last)
    def _():
        if first:
            put_grads(place, n_z, keep, send, agu, ad)
        elif is_ % 16 == 0:
            put_grads(place, n_z, keep, send, agu, ad, ao)
        else:
            for f in range(n_f):
                spread[f, :is_, :] = ao[f * is_ : (f + 1) * is_, :]
            put_grads(place, n_z, keep, send, agu, ad, spread)


def call_ffn_half(first, place, n_z, pieces, gains, arrays, S, L, D):
    G = GROUP
    R, n_f = G * L, 2 * n_z
    FW = D
    CH = FW // 2
    ds, fh, is_ = D // n_f, FW // n_f, INNER // n_f
    series = series_spec(G, (S, L, D))
    pack = (2, n_z, 2 * ds + fh + (0 if first else padded(is_)), CH)
    packs, act, wd = [sds(pack, bf16)] * 2, sds((S * L, FW), bf16), sds((FW, D), bf16)
    if first:
        tokens, ct, mixed = arrays
        operands = (*pieces, in_hbm(tokens), in_hbm(ct), mixed, gains)
        out_shape = [sds((S * L, D), f32), act, sds((S * L, D), bf16), wd, sds((INNER, D), bf16)] + packs
    else:
        hidden, ct, *arrays = arrays
        operands = (*pieces, hidden, in_hbm(ct), *arrays)
        out_shape = [sds((S * L, D), bf16), sds((S * L, INNER), bf16), act, wd] + packs + [sds((8, D), f32)]
    vm = pltpu.VMEM
    scratch = [
        vm((D, 2 * FW), f32), vm((FW, D), f32), vm((D, 2 * FW), bf16), vm((R, D), bf16), vm((R, D), bf16),
        vm((2, R, 2 * CH), f32), vm((2, R, CH), f32), vm((2, R, 2 * CH), bf16), vm((R, D), f32),
    ]
    scratch += [] if first else [vm((INNER, D), f32)]
    scratch += [vm((n_f, padded(is_), D) if is_ % 16 else (1, 16, 128), bf16 if first else f32)]
    return pl.pallas_call(
        functools.partial(ffn_half, G, L, n_z, first),
        out_shape=tuple(out_shape),
        grid_spec=pltpu.PrefetchScalarGridSpec(
            num_scalar_prefetch=1,
            grid=(S // G,),
            in_specs=[series if len(a.shape) == 3 and a.shape[0] == S else whole(a.shape) for a in operands],
            out_specs=[whole(shape.shape) for shape in out_shape],
            scratch_shapes=scratch,
        ),
        compiler_params=params(MIB_FFN),
        cost_estimate=cost(S * L, 9 * D * FW, S * L * 9000),
        name="ffn_first" if first else "ffn_second",
    )(place, *operands)


def layer_result(G, L, place_ref, hid_ref, act_0, act_1, wd_0, wd_1, gains_ref, out_ref, done_ref):
    step = pl.program_id(0)
    count = place_ref[0]
    R = G * L
    D = hid_ref.shape[-1]
    done_ref[...] = gains_ref[...]
    group = jnp.minimum(step, (count + G - 1) // G - 1)
    hid_ref, act_0, act_1 = (group_rows(ref, group, R) for ref in (hid_ref, act_0, act_1))

    @pl.when(step * G >= count)
    def _():
        out_ref[...] = jnp.zeros_like(out_ref)

    @pl.when(step * G < count)
    def _():
        live = (step * G + lax.broadcasted_iota(jnp.int32, (R, 1), 0) // L) < count
        out = hid_ref[...] + nn(act_0[...], wd_0[...]) + nn(act_1[...], wd_1[...])
        out_ref[...] = jnp.where(live, out, 0.0).astype(bf16).reshape(G, L, D)


def call_layer_result(place, hidden, act_0, act_1, wd_0, wd_1, gains, S, L):
    G, D = GROUP, hidden.shape[-1]
    operands = (hidden, act_0, act_1, wd_0, wd_1, gains)
    return pl.pallas_call(
        functools.partial(layer_result, G, L),
        out_shape=(pltpu.HBM((S, L, D), bf16), sds(gains.shape, f32)),
        grid_spec=pltpu.PrefetchScalarGridSpec(
            num_scalar_prefetch=1,
            grid=(S // G,),
            in_specs=[whole(a.shape) for a in operands],
            out_specs=(series_spec(G, (S, L, D), True), whole(gains.shape)),
        ),
        compiler_params=params(MIB_RESULT),
        cost_estimate=cost(S * L, 2 * D * act_0.shape[-1], S * L * 6000),
        name="layer_result",
    )(place, *operands)


def attention_backward(G, L, n_z, place_ref, tok_ref, qkv_ref, probs_ref, gm_ref, w_ref, gains_ref, gf_ref,
                       dqkv, keep, send, aw, ab, dp_ref, ds_ref, small):
    step = pl.program_id(0)
    last = pl.num_programs(0) - 1
    R = G * L
    D = tok_ref.shape[-1]
    place = Place(place_ref, n_z)
    count = place.count
    group = jnp.minimum(step, (count + G - 1) // G - 1)
    gm_ref, dqkv, qkv_ref = (group_rows(ref, group, R) for ref in (gm_ref, dqkv, qkv_ref))

    @pl.when(step == 0)
    def _():
        for ref in (aw, ab):
            ref[...] = jnp.zeros_like(ref)

    @pl.when(step * G < count)
    def _():
        cols = [[pl.ds(b * INNER + p * PAIR, PAIR) for b in range(3)] for p in range(PAIRS)]
        for p in range(PAIRS):
            for s in range(G):
                rows = pl.ds(s * L, L)
                dm = split_heads(gm_ref[rows, pl.ds(p * PAIR, PAIR)])
                dp_ref[s, p] = nt(qkv_ref[rows, cols[p][2]], dm)
                dqkv[rows, cols[p][2]] = nn(probs_ref[s, p], dm).astype(bf16)
        for p in range(PAIRS):
            total = ab[p]
            for s in range(G):
                prf = probs_ref[s, p].astype(f32)
                dp = dp_ref[s, p]
                ds = prf * (dp - jnp.sum(prf * dp, axis=0, keepdims=True))
                total = total + ds
                ds_ref[s, p] = ds.astype(bf16)
            ab[p] = total
        for p in range(PAIRS):
            for s in range(G):
                rows = pl.ds(s * L, L)
                low = ds_ref[s, p]
                dqkv[rows, cols[p][1]] = nn(low, split_heads(qkv_ref[rows, cols[p][0]])).astype(bf16)
                dqkv[rows, cols[p][0]] = join_heads(tn(low, qkv_ref[rows, cols[p][1]])).astype(bf16)
        x = tok_ref[...].reshape(R, D).astype(f32)
        aw[...] += tn((x * inverse_rms(x) * gains_ref[0:1, :]).astype(bf16), dqkv[...])

    @pl.when(step == last)
    def _():
        n_f = 2 * n_z
        ds, n_b, rest = D // n_f, BUCKETS // n_f, 3 * INNER - CUT
        ids = bucket_table(L)
        low = lane_low((1, PAIR))
        small[...] = jnp.zeros_like(small)
        for p in range(PAIRS):
            t = ab[p]
            for b in range(BUCKETS):
                by_lane = jnp.sum(jnp.where(ids == b, t, 0.0), axis=0, keepdims=True)
                one = jnp.sum(jnp.where(low, by_lane, 0.0), axis=1, keepdims=True)
                two = jnp.sum(jnp.where(low, 0.0, by_lane), axis=1, keepdims=True)
                row = b // n_b * ds + (b % n_b) * HEADS + 2 * p
                small[row : row + 1, :] = jnp.broadcast_to(one, (1, PAIR))
                small[row + 1 : row + 2, :] = jnp.broadcast_to(two, (1, PAIR))
        gain = jnp.transpose(gains_ref[...])[:, 0:1]
        one = jnp.sum(aw[...] * w_ref[...].astype(f32), axis=1, keepdims=True) / gain
        two = jnp.sum(jnp.transpose(gf_ref[...]), axis=1, keepdims=True)
        lane = lax.broadcasted_iota(jnp.int32, (D, PAIR), 1)
        small[...] = jnp.where(lane == 0, one, jnp.where(lane == 1, two, small[...]))

        def write(c):
            for xx, k, f in place.shards():
                one, two = keep.at[xx, k], send.at[xx, k]
                one, two = (one, two) if c == 0 else (two, one)
                one[...] = aw[at(f, ds), :CUT].astype(bf16)
                two[:, :rest] = aw[at(f, ds), CUT:].astype(bf16)
                two[:, rest:] = small[at(f, ds), :].astype(bf16)

        for c in range(2):
            pl.when(place.core == c)(functools.partial(write, c))


def call_attention_backward(place, n_z, tokens, qkv, probs, gm, w, gains, gf):
    S, L, D = tokens.shape
    G = GROUP
    pack = (2, n_z, D // (2 * n_z), CUT)
    vm = pltpu.VMEM
    return pl.pallas_call(
        functools.partial(attention_backward, G, L, n_z),
        out_shape=(sds((S * L, 3 * INNER), bf16), sds(pack, bf16), sds(pack, bf16)),
        grid_spec=pltpu.PrefetchScalarGridSpec(
            num_scalar_prefetch=1,
            grid=(S // G,),
            in_specs=[series_spec(G, tokens.shape), whole(qkv.shape), series_spec(G, probs.shape),
                      whole(gm.shape), whole(w.shape), whole(gains.shape), whole(gf.shape)],
            out_specs=[whole(pack)] * 3,
            scratch_shapes=[
                vm(w.shape, f32), vm((PAIRS, L, PAIR), f32),
                vm((G, PAIRS, L, PAIR), f32), vm((G, PAIRS, L, PAIR), bf16), vm((D, PAIR), f32),
            ],
        ),
        compiler_params=params(MIB_BACKWARD),
        cost_estimate=cost(S * L, D * 3 * INNER * 4, S * L * 6000),
        name="attention_backward",
    )(place, in_hbm(tokens), qkv, in_hbm(probs), gm, w, gains, gf)


def token_gradient(G, L, first_step, place_ref, tok_ref, dqkv_ref, gh_ref, w_ref, gains_ref, *refs):
    gt_ref, done_ref = refs[-2:]
    done_ref[...] = gains_ref[...]
    step = pl.program_id(0) + first_step
    D = tok_ref.shape[-1]
    group = jnp.minimum(step, (place_ref[0] + G - 1) // G - 1)
    dqkv_ref, gh_ref = group_rows(dqkv_ref, group, G * L), group_rows(gh_ref, group, G * L)

    @pl.when(step * G >= place_ref[0])
    def _():
        gt_ref[...] = jnp.zeros_like(gt_ref)

    @pl.when(step * G < place_ref[0])
    def _():
        x = tok_ref[...].reshape(G * L, D).astype(f32)
        scale = inverse_rms(x)
        xs = x * scale
        g = nt(dqkv_ref[...], w_ref[...]) * gains_ref[0:1, :]
        dot = jnp.mean(g * xs, axis=-1, keepdims=True)
        gt_ref[...] = (gh_ref[...].astype(f32) + scale * (g - xs * dot)).astype(bf16).reshape(G, L, D)


def call_token_gradient(place, tokens, dqkv, gh, w, gains, part, earlier=None):
    S, L, D = tokens.shape
    G = GROUP
    steps = S // G // 2 if part == 0 else S // G - S // G // 2
    shift = part * (S // G // 2)

    def rows(width):
        return pl.BlockSpec((G * L, width), lambda i, c: (live_group(i + shift, c, G), 0))

    def series(every):
        return pl.BlockSpec((G, L, D), lambda i, c: (i + shift if every else live_group(i + shift, c, G), 0, 0))

    more = [] if earlier is None else [earlier]
    return pl.pallas_call(
        functools.partial(token_gradient, G, L, shift),
        out_shape=(pltpu.HBM((S, L, D), bf16), sds(gains.shape, f32)),
        grid_spec=pltpu.PrefetchScalarGridSpec(
            num_scalar_prefetch=1,
            grid=(steps,),
            in_specs=[series(False), whole(dqkv.shape), whole(gh.shape), whole(w.shape), whole(gains.shape)]
            + [pl.BlockSpec(memory_space=pl.ANY)] * len(more),
            out_specs=(series(True), whole(gains.shape)),
        ),
        input_output_aliases={6: 0} if more else {},
        compiler_params=params(MIB_TOKENS),
        cost_estimate=cost(S * L // 2, D * 3 * INNER * 2, S * L * 2500),
        name="token_gradient",
    )(place, in_hbm(tokens), dqkv, gh, w, gains, *more)


def finish(n_f, place_ref, *refs):
    packs = [refs[2 * i : 2 * i + 2] for i in range(3)]
    gq, gk, gv, go, gg, gu, gd, ga, gf, gb = refs[7:]
    core = place_ref[1]
    ds, is_, fh = gq.shape[0], go.shape[0], gd.shape[0] // 2
    half = go.shape[1] // 2

    def halves(pack):
        here, there = pack[0][...].astype(f32), pack[1][...].astype(f32)
        return jnp.where(core == 0, here, there), jnp.where(core == 0, there, here)

    one, two = halves(packs[2])
    gq[...] = one[:, :INNER]
    gk[...] = jnp.concatenate([one[:, INNER:CUT], two[:, : 2 * INNER - CUT]], axis=1)
    gv[...] = two[:, 2 * INNER - CUT : 3 * INNER - CUT]
    small = jnp.transpose(two[:, 3 * INNER - CUT :])
    ga[...] = small[0]
    gf[...] = small[1]
    gb[...] = small[2, : BUCKETS // n_f * HEADS]
    chunks = [halves(packs[0]), halves(packs[1])]
    for which, ref in enumerate((gg, gu)):
        wide = [jnp.concatenate([c[which][:ds], c[which][ds : 2 * ds]], axis=1) for c in chunks]
        width = wide[0].shape[1] // n_f
        ref[...] = jnp.concatenate(
            [w[:, f * width : (f + 1) * width] for f in range(n_f) for w in wide], axis=1
        )
    for chunk, pair in enumerate(chunks):
        for which in range(2):
            gd[chunk * fh : (chunk + 1) * fh, which * half : (which + 1) * half] = pair[which][2 * ds : 2 * ds + fh]
    for which in range(2):
        go[:, which * half : (which + 1) * half] = chunks[1][which][2 * ds + fh : 2 * ds + fh + is_]


def call_finish(place, n_f, packs, shapes, after):
    vm, sm = pl.BlockSpec(memory_space=pltpu.VMEM), pl.BlockSpec(memory_space=pltpu.SMEM)
    flat = [piece for pack in packs for piece in pack]
    return pl.pallas_call(
        functools.partial(finish, n_f),
        out_shape=tuple(sds(shape, f32) for shape in shapes),
        in_specs=[sm] + [vm] * len(flat) + [vm],
        out_specs=[vm] * len(shapes),
        compiler_params=small_params(),
        name="finish",
    )(place, *flat, after)


def solution(mesh):
    n_r, n_f = mesh.shape["rep"], mesh.shape["fsdp"]
    n_z = n_f // 2

    def over_fsdp(value, distance):
        return lax.ppermute(value, "fsdp", [(i, i ^ distance) for i in range(n_f)])

    def over_rep(value, distance):
        return lax.ppermute(value, "rep", [(i, i ^ distance) for i in range(n_r)])

    def along_z(pack):
        return [pack] + [over_fsdp(pack, 2 * k) for k in range(1, n_z)]

    def halved(keep, got):
        away = (keep[1].astype(f32) + got[1].astype(f32)).astype(bf16)
        return keep[0].astype(f32) + got[0].astype(f32), away

    def joined(here, got):
        here = here + got.astype(f32)
        return here[0], [here[k].astype(bf16) for k in range(1, n_z)]

    def to_z(pieces):
        return [over_fsdp(piece, 2 * (k + 1)) for k, piece in enumerate(pieces)]

    def summed(own, got):
        for value in got:
            own = own + value.astype(f32)
        return own.astype(bf16)

    def replicas(own):
        distance = 2
        while distance < n_r:
            own = (own.astype(f32) + over_rep(own, distance).astype(f32)).astype(bf16)
            distance *= 2
        return own, over_rep(own, 1)

    together = lax.optimization_barrier

    def body(tokens, counts, attn_gain, wq, wk, wv, wo, rel_bias, ffn_gain, wg, wu, wd, cotangent):
        S, L, D = tokens.shape
        r, f = lax.axis_index("rep"), lax.axis_index("fsdp")
        place = in_hbm(jnp.stack([counts[0, 0], r % 2, f % 2, f // 2]).astype(jnp.int32))
        pack_a = call_prepare_attention(place, n_f, attn_gain, wq, wk, wv, rel_bias, ffn_gain)
        pack_0, pack_1 = call_prepare_ffn(place, n_f, wo, wg, wu, wd)

        z_0 = along_z(pack_0)
        z_a, pack_1 = together((along_z(pack_a), pack_1))
        near_a = jnp.stack(z_a)
        far_a, near_ac = over_fsdp(near_a, 1), over_rep(near_a, 1)
        far_a, near_ac, z_0, pack_1 = together((far_a, near_ac, z_0, pack_1))
        far_ac, near_0 = over_rep(far_a, 1), jnp.stack(z_0)
        far_ac, near_0 = together((far_ac, near_0))

        far_0, near_0c, z_1 = over_fsdp(near_0, 1), over_rep(near_0, 1), along_z(pack_1)
        qkv, probs, mixed, w_all, gains = call_attention_forward(place, tokens, (near_a, far_a, near_ac, far_ac))
        gains, far_0, near_0c, z_1 = together((gains, far_0, near_0c, z_1))
        far_0c, near_1 = over_rep(far_0, 1), jnp.stack(z_1)
        far_0c, near_1 = together((far_0c, near_1))

        far_1, near_1c = over_fsdp(near_1, 1), over_rep(near_1, 1)
        hidden, act_0, gpart, wd_0, wo_all, keep_0, send_0 = call_ffn_half(
            True, place, n_z, (near_0, far_0, near_0c, far_0c), gains, (tokens, cotangent, mixed), S, L, D
        )
        wo_all, keep_0, send_0, far_1, near_1c = together((wo_all, keep_0, send_0, far_1, near_1c))

        far_1c, got_0 = over_rep(far_1, 1), over_rep(send_0, 1)
        gh, gm, act_1, wd_1, keep_1, send_1, gf = call_ffn_half(
            False, place, n_z, (near_1, far_1, near_1c, far_1c), None, (hidden, cotangent, mixed, gpart, gains, wo_all), S, L, D
        )
        keep_1, send_1, gf, got_0 = together((keep_1, send_1, gf, got_0))
        here_0, away_0 = halved(keep_0, got_0)
        away_0, gf = together((away_0, gf))

        got_0, got_1 = over_fsdp(away_0, 1), over_rep(send_1, 1)
        dqkv, keep_2, send_2 = call_attention_backward(place, n_z, tokens, qkv, probs, gm, w_all, gains, gf)
        keep_2, send_2, got_0, got_1 = together((keep_2, send_2, got_0, got_1))
        own_0, z_0 = joined(here_0, got_0)
        here_1, away_1 = halved(keep_1, got_1)
        gains, z_0, away_1 = together((gains, z_0, away_1))

        z_0, got_1, got_2 = to_z(z_0), over_fsdp(away_1, 1), over_rep(send_2, 1)
        half_tokens, done = call_token_gradient(place, tokens, dqkv, gh, w_all, gains, 0)
        done, z_0, got_1, got_2 = together((done, z_0, got_1, got_2))
        sum_0 = summed(own_0, z_0)
        here_2, away_2 = halved(keep_2, got_2)
        own_1, z_1 = joined(here_1, got_1)
        done, away_2, z_1, sum_0 = together((done, away_2, z_1, sum_0))
        got_2, z_1 = over_fsdp(away_2, 1), to_z(z_1)
        grad_tokens, done = call_token_gradient(place, tokens, dqkv, gh, w_all, done, 1, half_tokens)
        done, got_2, z_1 = together((done, got_2, z_1))
        own_2, z_2 = joined(here_2, got_2)
        sum_1 = summed(own_1, z_1)
        done, z_2, sum_1 = together((done, z_2, sum_1))
        z_2 = to_z(z_2)
        layer_out, done = call_layer_result(place, hidden, act_0, act_1, wd_0, wd_1, done, S, L)
        done, z_2 = together((done, z_2))
        sum_2 = summed(own_2, z_2)
        gq, gk, gv, go, gg, gu, gd, grad_attn_gain, grad_ffn_gain, grad_bias = call_finish(
            place, n_f, [replicas(value) for value in (sum_0, sum_1, sum_2)],
            (wq.shape, wk.shape, wv.shape, wo.shape, wg.shape, wu.shape, wd.shape,
             attn_gain.shape, ffn_gain.shape, rel_bias.shape), done,
        )
        return (layer_out, grad_tokens, grad_attn_gain, gq, gk, gv, go, grad_bias, grad_ffn_gain, gg, gu, gd)

    rows, cols, flat = P(("rep", "fsdp"), None, None), P("fsdp", None), P("fsdp")
    return jax.shard_map(
        body,
        mesh=mesh,
        in_specs=(rows, P("rep", "fsdp"), flat, cols, cols, cols, cols, flat, flat, cols, cols, cols, rows),
        out_specs=(rows, rows, flat, cols, cols, cols, cols, flat, flat, cols, cols, cols),
        check_vma=False,
    )
```

```python
import functools

import jax
import jax.numpy as jnp
from jax import lax
from jax.experimental import pallas as pl
from jax.experimental.pallas import tpu as pltpu
from jax.sharding import PartitionSpec as P

HEADS, HDIM, BUCKETS = 6, 64, 32
INNER = HEADS * HDIM
PAIRS = HEADS // 2
PAIR = 2 * HDIM
CUT = 640
GROUP = 8
EPS = 1e-6
bf16, f32 = jnp.bfloat16, jnp.float32
sds = jax.ShapeDtypeStruct


def in_hbm(value):
    return pltpu.with_memory_space_constraint(value, pltpu.HBM)


def nn(a, b):
    return jnp.dot(a, b, preferred_element_type=f32)


def nt(a, b):
    return lax.dot_general(a, b, (((1,), (1,)), ((), ())), preferred_element_type=f32)


def tn(a, b):
    return lax.dot_general(a, b, (((0,), (0,)), ((), ())), preferred_element_type=f32)


def bucket_edges():
    half = BUCKETS // 2
    exact = half // 2
    power = half - exact
    return [
        min(m for m in range(exact, 129) if m**power * exact**k >= 128**k * exact**power) for k in range(1, power)
    ]


def bucket_table(length):
    half = BUCKETS // 2
    exact = half // 2
    shape = (length, PAIR)
    apart = lax.broadcasted_iota(jnp.int32, shape, 0) - lax.broadcasted_iota(jnp.int32, shape, 1) % HDIM
    distance = jnp.abs(apart)
    bucket = jnp.minimum(distance, exact)
    for edge in bucket_edges():
        bucket = bucket + (distance >= edge).astype(jnp.int32)
    return bucket + jnp.where(apart > 0, half, 0)


def lane_low(shape):
    return lax.broadcasted_iota(jnp.int32, shape, 1) < HDIM


def split_heads(pair):
    low, zero = lane_low(pair.shape), jnp.zeros_like(pair)
    return jnp.concatenate([jnp.where(low, pair, zero), jnp.where(low, zero, pair)], axis=0)


def join_heads(both):
    rows = both.shape[0] // 2
    return jnp.where(lane_low((rows, PAIR)), both[:rows], both[rows:])


def row_sums(values):
    rows, width = values.shape
    return jnp.sum(values.reshape(rows // 8, 8, width), axis=0)


def inverse_rms(values):
    return lax.rsqrt(jnp.mean(values * values, axis=-1, keepdims=True) + EPS)


class Place:
    def __init__(self, ref, n_z):
        self.count, self.core, self.x, self.z = ref[0], ref[1], ref[2], ref[3]
        self.n_z = n_z

    def shards(self):
        for xx in range(2):
            for k in range(self.n_z):
                yield xx, k, jnp.bitwise_xor(self.z, k) * 2 + jnp.bitwise_xor(self.x, xx)


def at(shard, size):
    return pl.ds(pl.multiple_of(shard * size, size), size)


def interleaved(values, n_f, chunk):
    width = values.shape[1] // n_f // 2
    return jnp.concatenate(
        [values[:, (2 * f + chunk) * width : (2 * f + chunk + 1) * width] for f in range(n_f)], axis=1
    )


def prepare_attention(n_f, place_ref, bias_ref, wq, wk, wv, ga, gf, a_ref):
    core = place_ref[1]
    ds = wq.shape[0]
    joined = jnp.concatenate([wq[...], wk[...], wv[...]], axis=1)
    row = lax.broadcasted_iota(jnp.int32, (ds, PAIR), 0)
    low = lane_low((1, PAIR))
    small = jnp.zeros((ds, PAIR), f32)
    n_b = BUCKETS // n_f
    for b in range(n_b):
        for p in range(PAIRS):
            value = jnp.where(low, bias_ref[b * HEADS + 2 * p], bias_ref[b * HEADS + 2 * p + 1])
            small = jnp.where(row == b * PAIRS + p, value, small)
    for i, gain in enumerate((ga, gf)):
        tiled = jnp.concatenate([gain[...]] * (PAIR // ds), axis=1)
        small = jnp.where(row == n_b * PAIRS + i, tiled, small)

    def write(c):
        if c == 0:
            a_ref[...] = joined[:, :CUT].astype(bf16)
        else:
            a_ref[:, : 3 * INNER - CUT] = joined[:, CUT:].astype(bf16)
            a_ref[:, 3 * INNER - CUT :] = small.astype(bf16)

    for c in range(2):
        pl.when(core == c)(functools.partial(write, c))


def prepare_ffn(n_f, place_ref, wo, wg, wu, wd, p0_ref, p1_ref):
    core = place_ref[1]
    ds, is_, fh = wg.shape[0], wo.shape[0], wd.shape[0] // 2
    half = wo.shape[1] // 2

    def write(c):
        cols = slice(c * half, (c + 1) * half)
        for chunk, ref in enumerate((p0_ref, p1_ref)):
            g = interleaved((wg, wu)[c][...], n_f, chunk).astype(bf16)
            ref[:ds, :] = g[:, :half]
            ref[ds : 2 * ds, :] = g[:, half:]
            ref[2 * ds : 2 * ds + fh, :] = wd[chunk * fh : (chunk + 1) * fh, cols].astype(bf16)
        tail = wo[:, cols]
        pad = p0_ref.shape[0] - (2 * ds + fh + is_)
        if pad:
            tail = jnp.concatenate([tail, jnp.zeros((pad, half), f32)], axis=0)
        p0_ref[2 * ds + fh :, :] = tail.astype(bf16)

    for c in range(2):
        pl.when(core == c)(functools.partial(write, c))


def small_params():
    return pltpu.CompilerParams(vmem_limit_bytes=12 * 1024 * 1024)


def padded(rows):
    return -(-rows // 16) * 16


def call_prepare_attention(place, n_f, attn_gain, wq, wk, wv, rel_bias, ffn_gain):
    vm, sm = pl.BlockSpec(memory_space=pltpu.VMEM), pl.BlockSpec(memory_space=pltpu.SMEM)
    return pl.pallas_call(
        functools.partial(prepare_attention, n_f),
        out_shape=sds((wq.shape[0], CUT), bf16),
        in_specs=[sm, sm] + [vm] * 5,
        out_specs=vm,
        name="prepare_attention",
    )(place, rel_bias, wq, wk, wv, attn_gain.reshape(1, -1), ffn_gain.reshape(1, -1))


def call_prepare_ffn(place, n_f, wo, wg, wu, wd):
    ds, fh, half = wg.shape[0], wd.shape[0] // 2, wo.shape[1] // 2
    vm, sm = pl.BlockSpec(memory_space=pltpu.VMEM), pl.BlockSpec(memory_space=pltpu.SMEM)
    return pl.pallas_call(
        functools.partial(prepare_ffn, n_f),
        out_shape=(sds((2 * ds + fh + padded(wo.shape[0]), half), bf16), sds((2 * ds + fh, half), bf16)),
        in_specs=[sm] + [vm] * 4,
        out_specs=[vm] * 2,
        name="prepare_ffn",
    )(place, wo, wg, wu, wd)


def keep_close(G, tok_ref, ct_ref, tok_out, ct_out, done_ref):
    series = pl.ds(pl.program_id(0) * G, G)
    tok_out[series] = tok_ref[...]
    ct_out[series] = ct_ref[...]
    done_ref[...] = jnp.zeros_like(done_ref)


def call_keep_close(tokens, ct):
    S, L, D = tokens.shape
    G = GROUP
    block = pl.BlockSpec((G, L, D), lambda i: (i, 0, 0))
    return pl.pallas_call(
        functools.partial(keep_close, G),
        out_shape=(sds(tokens.shape, bf16), sds(ct.shape, bf16), sds((8, PAIR), f32)),
        grid=(S // G,),
        in_specs=[block, block],
        out_specs=[whole(tokens.shape), whole(ct.shape), whole((8, PAIR))],
        compiler_params=params(MIB_TOKENS),
        cost_estimate=cost(S * L, 1, 8 * S * L * D),
        name="keep_close",
    )(in_hbm(tokens), in_hbm(ct))


def attention_forward(G, L, n_z, place_ref, tok_ref, after_ref, *refs):
    pieces, refs = refs[:4], refs[4:]
    all_qkv, all_probs, mixed_ref, w_ref, gains_ref, table_ref, st_ref, small_ref = refs
    step = pl.program_id(0)
    place = Place(place_ref, n_z)
    D = tok_ref.shape[-1]
    n_f = 2 * n_z
    ds = D // n_f
    rest = 3 * INNER - CUT

    def assemble(c):
        for xx, k, f in place.shards():
            one, two = pieces[xx].at[k], pieces[2 + xx].at[k]
            one, two = (one, two) if c == 0 else (two, one)
            w_ref[at(f, ds), :CUT] = one[...]
            w_ref[at(f, ds), CUT:] = two[:, :rest]
            small_ref[at(f, ds), :] = two[:, rest:].astype(f32)

    @pl.when(step == 0)
    def _():
        for c in range(2):
            pl.when(place.core == c)(functools.partial(assemble, c))
        n_b = BUCKETS // n_f
        ids = bucket_table(L)
        for p in range(PAIRS):
            total = jnp.zeros(ids.shape, f32)
            for b in range(BUCKETS):
                row = b // n_b * ds + (b % n_b) * PAIRS + p
                total = jnp.where(ids == b, small_ref[row : row + 1, :], total)
            table_ref[p] = total
        per = PAIR // ds
        lane = lax.broadcasted_iota(jnp.int32, (1, PAIR), 1) // ds
        gains_ref[...] = jnp.zeros_like(gains_ref)
        for i in range(2):
            for v in range(D // PAIR):
                total = jnp.zeros((1, PAIR), f32)
                for f in range(per):
                    row = (v * per + f) * ds + n_b * PAIRS + i
                    total = jnp.where(lane == f, small_ref[row : row + 1, :], total)
                gains_ref[i : i + 1, v * PAIR : (v + 1) * PAIR] = total

    @pl.when(step * G < place.count)
    def _():
        mixed, qkv_ref = group_rows(mixed_ref, step, G * L), group_rows(all_qkv, step, G * L)
        probs_ref = all_probs.at[pl.ds(step * G, G)]
        x = tok_ref[pl.ds(step * G, G)].reshape(G * L, D).astype(f32)
        normed = (x * inverse_rms(x) * gains_ref[0:1, :]).astype(bf16)
        qkv_ref[...] = nn(normed, w_ref[...]).astype(bf16)
        for s in range(G):
            rows = pl.ds(s * L, L)
            for p in range(PAIRS):
                q = qkv_ref[rows, pl.ds(p * PAIR, PAIR)]
                k = qkv_ref[rows, pl.ds(INNER + p * PAIR, PAIR)]
                st_ref[s, p] = nt(k, split_heads(q))
        for s in range(G):
            for p in range(PAIRS):
                st = st_ref[s, p] + table_ref[p]
                e = jnp.exp(st - jnp.max(st, axis=0, keepdims=True))
                probs_ref[s, p] = (e * (1.0 / jnp.sum(e, axis=0, keepdims=True))).astype(bf16)
        for s in range(G):
            rows = pl.ds(s * L, L)
            for p in range(PAIRS):
                v = qkv_ref[rows, pl.ds(2 * INNER + p * PAIR, PAIR)]
                mixed[rows, pl.ds(p * PAIR, PAIR)] = join_heads(tn(probs_ref[s, p], v)).astype(bf16)


MIB_FORWARD, MIB_FFN, MIB_BACKWARD, MIB_TOKENS, MIB_RESULT = 8, 14, 10, 6, 6


def params(mib):
    return pltpu.CompilerParams(dimension_semantics=("arbitrary",), vmem_limit_bytes=mib * 1024 * 1024)


def whole(shape):
    return pl.BlockSpec(memory_space=pltpu.VMEM)


def live_group(i, place, G):
    return jnp.minimum(i, jnp.maximum((place[0] + G - 1) // G - 1, 0))


def series_spec(G, shape, every=False):
    tail = (0,) * (len(shape) - 1)
    return pl.BlockSpec((G,) + shape[1:], lambda i, c: ((i if every else live_group(i, c, G)),) + tail)


def row_spec(G, L, width):
    return pl.BlockSpec((G * L, width), lambda i, c: (live_group(i, c, G), 0))


def group_rows(ref, step, rows):
    return ref.at[pl.ds(pl.multiple_of(step * rows, rows), rows), :]


def cost(rows, per_row, nbytes, exps=0):
    return pl.CostEstimate(flops=2 * rows * per_row, bytes_accessed=nbytes, transcendentals=exps)


def call_attention_forward(place, tokens, after, pieces):
    S, L, D = tokens.shape
    G, n_z = GROUP, pieces[0].shape[0]
    return pl.pallas_call(
        functools.partial(attention_forward, G, L, n_z),
        out_shape=(
            sds((S * L, 3 * INNER), bf16),
            sds((S, PAIRS, L, PAIR), bf16),
            sds((S * L, INNER), bf16),
            sds((D, 3 * INNER), bf16),
            sds((8, D), f32),
        ),
        grid_spec=pltpu.PrefetchScalarGridSpec(
            num_scalar_prefetch=1,
            grid=(S // G,),
            in_specs=[whole(tokens.shape), whole(after.shape)] + [whole(piece.shape) for piece in pieces],
            out_specs=[
                whole((S * L, 3 * INNER)),
                whole((S, PAIRS, L, PAIR)),
                whole((S * L, INNER)),
                whole((D, 3 * INNER)),
                whole((8, D)),
            ],
            scratch_shapes=[
                pltpu.VMEM((PAIRS, L, PAIR), f32),
                pltpu.VMEM((G, PAIRS, L, PAIR), f32),
                pltpu.VMEM((D, PAIR), f32),
            ],
        ),
        compiler_params=params(MIB_FORWARD),
        cost_estimate=cost(S * L, D * 3 * INNER * 4, S * L * 5000),
        name="attention_forward",
    )(place, tokens, after, *pieces)


def gelu_parts(v):
    c = 0.7978845608028654
    v2 = v * v
    t = jnp.tanh(v * (c + (c * 0.044715) * v2))
    half = 0.5 + 0.5 * t
    return v * half, half + (0.5 * v) * (1.0 - t * t) * (c + (3 * c * 0.044715) * v2)


def put_weights(place, pieces, wgu, wd, wo=None):
    FW, D = wd.shape

    def assemble(c):
        for f, here, there in pieces:
            for which, piece in enumerate((here, there) if c == 0 else (there, here)):
                n_f = len(pieces)
                ds, fh, half, is_ = D // n_f, FW // n_f, FW // 2, INNER // n_f
                for part in range(2):
                    start = (2 * part + which) * half
                    wgu[at(f, ds), start : start + half] = piece[part * ds : (part + 1) * ds, :]
                cols = slice(which * half, (which + 1) * half)
                wd[at(f, fh), cols] = piece[2 * ds : 2 * ds + fh, :]
                if wo is None:
                    continue
                if is_ % 16 == 0:
                    wo[at(f, is_), cols] = piece[2 * ds + fh : 2 * ds + fh + is_, :]
                else:
                    wo[f, :, cols] = piece[2 * ds + fh :, :]

    for c in range(2):
        pl.when(place.core == c)(functools.partial(assemble, c))


def put_grads(place, n_z, keep, send, agu, ad, ao=None):
    n_f = 2 * n_z
    FW, D = ad.shape
    ds, fh, half = D // n_f, FW // n_f, FW // 2

    def write(c):
        for xx, k, f in place.shards():
            for which, ref in enumerate((keep, send) if c == 0 else (send, keep)):
                for part in range(2):
                    start = (2 * part + which) * half
                    ref[xx, k, part * ds : (part + 1) * ds, :] = agu[at(f, ds), start : start + half].astype(bf16)
                cols = slice(which * half, (which + 1) * half)
                ref[xx, k, 2 * ds : 2 * ds + fh, :] = ad[at(f, fh), cols].astype(bf16)
                if ao is not None:
                    is_ = INNER // n_f
                    if is_ % 16 == 0:
                        ref[xx, k, 2 * ds + fh :, :] = ao[at(f, is_), cols].astype(bf16)
                    else:
                        ref[xx, k, 2 * ds + fh :, :] = ao[f, :, cols].astype(bf16)

    for c in range(2):
        pl.when(place.core == c)(functools.partial(write, c))


def ffn_half(G, L, n_z, stage, shift, place_ref, *refs):
    n_f = 2 * n_z
    place = Place(place_ref, n_z)
    first, begins, ends = stage == 0, stage < 2, stage != 1
    if begins:
        pieces, refs = refs[:4], refs[4:]
        pieces = [(f, pieces[xx].at[k], pieces[2 + xx].at[k]) for xx, k, f in place.shards()]
    if stage == 0:
        (tok_ref, ct_ref, mixed_ref, gains_ref,
         hid_ref, act, gpart_ref, wd, wo_out, keep, send,
         agu, ad, wgu, n2, gb, gu, ga, low, gn, spread) = refs
    elif stage == 1:
        hid_ref, ct_ref, gains_ref, wo_in, _, _ = refs[:6]
        gpart_ref, mixed_ref, act, agu, ad, ao, gf_ref, wd, wgu, n2, gb, gu, ga, low, gn = refs[6:]
    else:
        hid_ref, ct_ref, gains_ref, wo_in, wd, wgu = refs[:6]
        gpart_ref, mixed_ref, act, agu, ad, ao, gf_ref, keep, send, n2, gb, gu, ga, low, gn, spread = refs[13:]
    step = pl.program_id(0) + shift
    R = G * L
    FW, D = wd.shape
    CH = FW // 2
    is_ = INNER // n_f
    count = place.count
    group = jnp.minimum(step, (count + G - 1) // G - 1)
    hid_ref, mixed_ref, act, gpart_ref = (group_rows(ref, group, R) for ref in (hid_ref, mixed_ref, act, gpart_ref))

    if begins:

        @pl.when(step == 0)
        def _():
            wo = (wo_out if is_ % 16 == 0 else spread) if first else None
            put_weights(place, pieces, wgu, wd, wo)
            if first and is_ % 16:
                wo_out[...] = jnp.concatenate([spread[f, :is_, :].astype(f32) for f in range(n_f)], axis=0).astype(bf16)
            for ref in (agu, ad) if first else (agu, ad, ao, gf_ref):
                ref[...] = jnp.zeros_like(ref)

    @pl.when(step * G < count)
    def _():
        if first:
            h = tok_ref[pl.ds(group * G, G)].reshape(R, D).astype(f32) + nn(mixed_ref[...], wo_out[...])
            hid_ref[...] = h.astype(bf16)
        else:
            h = hid_ref[...].astype(f32)
        n2[...] = (h * inverse_rms(h) * gains_ref[1:2, :]).astype(bf16)
        live = (step * G + lax.broadcasted_iota(jnp.int32, (R, 1), 0) // L) < count
        gb[...] = jnp.where(live, ct_ref[pl.ds(group * G, G)].reshape(R, D), jnp.zeros((), bf16))
        for c in range(2):
            cols, both = pl.ds(c * CH, CH), pl.ds(2 * c * CH, 2 * CH)
            gu[c] = nn(n2[...], wgu[:, both])
            ga[c] = nt(gb[...], wd[cols, :])
        for c in range(2):
            cols, both = pl.ds(c * CH, CH), pl.ds(2 * c * CH, 2 * CH)
            for r in range(0, R, L):
                rows = pl.ds(r, L)
                u = gu[c, rows, CH:]
                a = ga[c, rows, :]
                g, dg = gelu_parts(gu[c, rows, :CH])
                act[rows, cols] = (g * u).astype(bf16)
                low[c, rows, :CH] = (a * u * dg).astype(bf16)
                low[c, rows, CH:] = (a * g).astype(bf16)
            if c == 0:
                gn[...] = nt(low[c], wgu[:, both])
            else:
                gn[...] += nt(low[c], wgu[:, both])
            ad[cols, :] += tn(act[:, cols], gb[...])
            agu[:, both] += tn(n2[...], low[c])
        if first:
            gpart_ref[...] = gn[...].astype(bf16)
        else:
            h = hid_ref[...].astype(f32)
            scale = inverse_rms(h)
            hs = h * scale
            g2 = gn[...] + gpart_ref[...].astype(f32)
            gf_ref[...] += row_sums(g2 * hs)
            g2 = g2 * gains_ref[1:2, :]
            dot = jnp.mean(g2 * hs, axis=-1, keepdims=True)
            gh = (gb[...].astype(f32) + scale * (g2 - hs * dot)).astype(bf16)
            gpart_ref[...] = gh
            ao[...] += tn(mixed_ref[...], gh)
            mixed_ref[...] = nt(gh, wo_in[...]).astype(bf16)

    if ends:

        @pl.when(pl.program_id(0) == pl.num_programs(0) - 1)
        def _():
            if first:
                put_grads(place, n_z, keep, send, agu, ad)
            elif is_ % 16 == 0:
                put_grads(place, n_z, keep, send, agu, ad, ao)
            else:
                for f in range(n_f):
                    spread[f, :is_, :] = ao[f * is_ : (f + 1) * is_, :]
                put_grads(place, n_z, keep, send, agu, ad, spread)


def call_ffn_half(stage, place, n_z, operands, S, L, D):
    G = GROUP
    R, n_f = G * L, 2 * n_z
    FW = D
    CH = FW // 2
    ds, fh, is_ = D // n_f, FW // n_f, INNER // n_f
    pack = (2, n_z, 2 * ds + fh + (padded(is_) if stage else 0), CH)
    packs, act = [sds(pack, bf16)] * 2, sds((S * L, FW), bf16)
    wd, wgu, rows = sds((FW, D), bf16), sds((D, 2 * FW), bf16), sds((S * L, D), bf16)
    agu, ad = sds((D, 2 * FW), f32), sds((FW, D), f32)
    running = [rows, sds((S * L, INNER), bf16), act, agu, ad, sds((INNER, D), f32), sds((8, D), f32)]
    vm = pltpu.VMEM
    work = [
        vm((R, D), bf16), vm((R, D), bf16),
        vm((2, R, 2 * CH), f32), vm((2, R, CH), f32), vm((2, R, 2 * CH), bf16), vm((R, D), f32),
    ]
    spread = [vm((n_f, padded(is_), D) if is_ % 16 else (1, 16, 128), f32 if stage else bf16)]
    half = S // G // 2
    steps, shift = ((S // G, 0), (half, 0), (S // G - half, half))[stage]
    if stage == 0:
        out_shape = [rows, act, rows, wd, sds((INNER, D), bf16)] + packs
        scratch = [vm(agu.shape, f32), vm(ad.shape, f32), vm(wgu.shape, bf16)] + work + spread
        aliases = {}
    elif stage == 1:
        out_shape, scratch = running + [wd, wgu], work
        aliases = {9: 0, 10: 1}
    else:
        out_shape, scratch = running + packs, work + spread
        aliases = {7 + i: i for i in range(7)}
    return pl.pallas_call(
        functools.partial(ffn_half, G, L, n_z, stage, shift),
        out_shape=tuple(out_shape),
        grid_spec=pltpu.PrefetchScalarGridSpec(
            num_scalar_prefetch=1,
            grid=(steps,),
            in_specs=[whole(a.shape) for a in operands],
            out_specs=[whole(shape.shape) for shape in out_shape],
            scratch_shapes=scratch,
        ),
        input_output_aliases=aliases,
        compiler_params=params(MIB_FFN),
        cost_estimate=cost(steps * R, 9 * D * FW, S * L * 9000),
        name=("ffn_first", "ffn_second", "ffn_third")[stage],
    )(place, *operands)


def layer_result(G, L, place_ref, hid_ref, act_0, act_1, wd_0, wd_1, gains_ref, out_ref, done_ref):
    step = pl.program_id(0)
    count = place_ref[0]
    R = G * L
    D = hid_ref.shape[-1]
    done_ref[...] = gains_ref[...]
    group = jnp.minimum(step, (count + G - 1) // G - 1)
    hid_ref, act_0, act_1 = (group_rows(ref, group, R) for ref in (hid_ref, act_0, act_1))

    @pl.when(step * G >= count)
    def _():
        out_ref[...] = jnp.zeros_like(out_ref)

    @pl.when(step * G < count)
    def _():
        live = (step * G + lax.broadcasted_iota(jnp.int32, (R, 1), 0) // L) < count
        out = hid_ref[...].astype(f32) + nn(act_0[...], wd_0[...]) + nn(act_1[...], wd_1[...])
        out_ref[...] = jnp.where(live, out, 0.0).astype(bf16).reshape(G, L, D)


def call_layer_result(place, hidden, act_0, act_1, wd_0, wd_1, gains, S, L):
    G, D = GROUP, hidden.shape[-1]
    operands = (hidden, act_0, act_1, wd_0, wd_1, gains)
    return pl.pallas_call(
        functools.partial(layer_result, G, L),
        out_shape=(pltpu.HBM((S, L, D), bf16), sds(gains.shape, f32)),
        grid_spec=pltpu.PrefetchScalarGridSpec(
            num_scalar_prefetch=1,
            grid=(S // G,),
            in_specs=[whole(a.shape) for a in operands],
            out_specs=(series_spec(G, (S, L, D), True), whole(gains.shape)),
        ),
        compiler_params=params(MIB_RESULT),
        cost_estimate=cost(S * L, 2 * D * act_0.shape[-1], S * L * 6000),
        name="layer_result",
    )(place, *operands)


def attention_backward(G, L, n_z, place_ref, tok_ref, _, probs_ref, gm_ref, w_ref, gains_ref, gf_ref,
                       dqkv, keep, send, aw, ab, dp_ref, ds_ref, small):
    step = pl.program_id(0)
    last = pl.num_programs(0) - 1
    R = G * L
    D = tok_ref.shape[-1]
    place = Place(place_ref, n_z)
    count = place.count
    group = jnp.minimum(step, (count + G - 1) // G - 1)
    probs_ref = probs_ref.at[pl.ds(group * G, G)]
    gm_ref, dqkv = group_rows(gm_ref, group, R), group_rows(dqkv, group, R)

    @pl.when(step == 0)
    def _():
        for ref in (aw, ab):
            ref[...] = jnp.zeros_like(ref)

    @pl.when(step * G < count)
    def _():
        cols = [[pl.ds(b * INNER + p * PAIR, PAIR) for b in range(3)] for p in range(PAIRS)]
        for p in range(PAIRS):
            for s in range(G):
                rows = pl.ds(s * L, L)
                dm = split_heads(gm_ref[rows, pl.ds(p * PAIR, PAIR)])
                dp_ref[s, p] = nt(dqkv[rows, cols[p][2]], dm)
                dqkv[rows, cols[p][2]] = nn(probs_ref[s, p], dm).astype(bf16)
        for p in range(PAIRS):
            total = ab[p]
            for s in range(G):
                prf = probs_ref[s, p].astype(f32)
                dp = dp_ref[s, p]
                ds = prf * (dp - jnp.sum(prf * dp, axis=0, keepdims=True))
                total = total + ds
                ds_ref[s, p] = ds.astype(bf16)
            ab[p] = total
        for p in range(PAIRS):
            for s in range(G):
                rows = pl.ds(s * L, L)
                low = ds_ref[s, p]
                q, k = dqkv[rows, cols[p][0]], dqkv[rows, cols[p][1]]
                dqkv[rows, cols[p][1]] = nn(low, split_heads(q)).astype(bf16)
                dqkv[rows, cols[p][0]] = join_heads(tn(low, k)).astype(bf16)
        x = tok_ref[pl.ds(group * G, G)].reshape(R, D).astype(f32)
        aw[...] += tn((x * inverse_rms(x) * gains_ref[0:1, :]).astype(bf16), dqkv[...])

    @pl.when(step == last)
    def _():
        n_f = 2 * n_z
        ds, n_b, rest = D // n_f, BUCKETS // n_f, 3 * INNER - CUT
        ids = bucket_table(L)
        low = lane_low((1, PAIR))
        small[...] = jnp.zeros_like(small)
        for p in range(PAIRS):
            t = ab[p]
            for b in range(BUCKETS):
                by_lane = jnp.sum(jnp.where(ids == b, t, 0.0), axis=0, keepdims=True)
                one = jnp.sum(jnp.where(low, by_lane, 0.0), axis=1, keepdims=True)
                two = jnp.sum(jnp.where(low, 0.0, by_lane), axis=1, keepdims=True)
                row = b // n_b * ds + (b % n_b) * HEADS + 2 * p
                small[row : row + 1, :] = jnp.broadcast_to(one, (1, PAIR))
                small[row + 1 : row + 2, :] = jnp.broadcast_to(two, (1, PAIR))
        gain = jnp.transpose(gains_ref[...])[:, 0:1]
        one = jnp.sum(aw[...] * w_ref[...].astype(f32), axis=1, keepdims=True) / gain
        two = jnp.sum(jnp.transpose(gf_ref[...]), axis=1, keepdims=True)
        lane = lax.broadcasted_iota(jnp.int32, (D, PAIR), 1)
        small[...] = jnp.where(lane == 0, one, jnp.where(lane == 1, two, small[...]))

        def write(c):
            for xx, k, f in place.shards():
                one, two = keep.at[xx, k], send.at[xx, k]
                one, two = (one, two) if c == 0 else (two, one)
                one[...] = aw[at(f, ds), :CUT].astype(bf16)
                two[:, :rest] = aw[at(f, ds), CUT:].astype(bf16)
                two[:, rest:] = small[at(f, ds), :].astype(bf16)

        for c in range(2):
            pl.when(place.core == c)(functools.partial(write, c))


def call_attention_backward(place, n_z, tokens, qkv, probs, gm, w, gains, gf):
    S, L, D = tokens.shape
    G = GROUP
    pack = (2, n_z, D // (2 * n_z), CUT)
    vm = pltpu.VMEM
    return pl.pallas_call(
        functools.partial(attention_backward, G, L, n_z),
        out_shape=(sds((S * L, 3 * INNER), bf16), sds(pack, bf16), sds(pack, bf16)),
        grid_spec=pltpu.PrefetchScalarGridSpec(
            num_scalar_prefetch=1,
            grid=(S // G,),
            in_specs=[whole(tokens.shape), whole(qkv.shape), whole(probs.shape),
                      whole(gm.shape), whole(w.shape), whole(gains.shape), whole(gf.shape)],
            out_specs=[whole(pack)] * 3,
            scratch_shapes=[
                vm(w.shape, f32), vm((PAIRS, L, PAIR), f32),
                vm((G, PAIRS, L, PAIR), f32), vm((G, PAIRS, L, PAIR), bf16), vm((D, PAIR), f32),
            ],
        ),
        input_output_aliases={2: 0},
        compiler_params=params(MIB_BACKWARD),
        cost_estimate=cost(S * L, D * 3 * INNER * 4, S * L * 6000),
        name="attention_backward",
    )(place, tokens, qkv, probs, gm, w, gains, gf)


def token_gradient(G, L, first_step, place_ref, tok_ref, dqkv_ref, gh_ref, w_ref, gains_ref, *refs):
    gt_ref, done_ref = refs[-2:]
    done_ref[...] = gains_ref[...]
    step = pl.program_id(0) + first_step
    D = tok_ref.shape[-1]
    group = jnp.minimum(step, (place_ref[0] + G - 1) // G - 1)
    dqkv_ref, gh_ref = group_rows(dqkv_ref, group, G * L), group_rows(gh_ref, group, G * L)

    @pl.when(step * G >= place_ref[0])
    def _():
        gt_ref[...] = jnp.zeros_like(gt_ref)

    @pl.when(step * G < place_ref[0])
    def _():
        x = tok_ref[pl.ds(group * G, G)].reshape(G * L, D).astype(f32)
        scale = inverse_rms(x)
        xs = x * scale
        g = nt(dqkv_ref[...], w_ref[...]) * gains_ref[0:1, :]
        dot = jnp.mean(g * xs, axis=-1, keepdims=True)
        gt_ref[...] = (gh_ref[...].astype(f32) + scale * (g - xs * dot)).astype(bf16).reshape(G, L, D)


def call_token_gradient(place, tokens, dqkv, gh, w, gains, part, earlier=None):
    S, L, D = tokens.shape
    G = GROUP
    steps = S // G // 2 if part == 0 else S // G - S // G // 2
    shift = part * (S // G // 2)

    def rows(width):
        return pl.BlockSpec((G * L, width), lambda i, c: (live_group(i + shift, c, G), 0))

    def series(every):
        return pl.BlockSpec((G, L, D), lambda i, c: (i + shift if every else live_group(i + shift, c, G), 0, 0))

    more = [] if earlier is None else [earlier]
    return pl.pallas_call(
        functools.partial(token_gradient, G, L, shift),
        out_shape=(pltpu.HBM((S, L, D), bf16), sds(gains.shape, f32)),
        grid_spec=pltpu.PrefetchScalarGridSpec(
            num_scalar_prefetch=1,
            grid=(steps,),
            in_specs=[whole(tokens.shape), whole(dqkv.shape), whole(gh.shape), whole(w.shape), whole(gains.shape)]
            + [pl.BlockSpec(memory_space=pl.ANY)] * len(more),
            out_specs=(series(True), whole(gains.shape)),
        ),
        input_output_aliases={6: 0} if more else {},
        compiler_params=params(MIB_TOKENS),
        cost_estimate=cost(S * L // 2, D * 3 * INNER * 2, S * L * 2500),
        name="token_gradient",
    )(place, tokens, dqkv, gh, w, gains, *more)


def finish(n_f, place_ref, *refs):
    packs = [refs[2 * i : 2 * i + 2] for i in range(3)]
    gq, gk, gv, go, gg, gu, gd, ga, gf, gb = refs[7:]
    core = place_ref[1]
    ds, is_, fh = gq.shape[0], go.shape[0], gd.shape[0] // 2
    half = go.shape[1] // 2

    def halves(pack):
        here, there = pack[0][...].astype(f32), pack[1][...].astype(f32)
        return jnp.where(core == 0, here, there), jnp.where(core == 0, there, here)

    one, two = halves(packs[2])
    gq[...] = one[:, :INNER]
    gk[...] = jnp.concatenate([one[:, INNER:CUT], two[:, : 2 * INNER - CUT]], axis=1)
    gv[...] = two[:, 2 * INNER - CUT : 3 * INNER - CUT]
    small = jnp.transpose(two[:, 3 * INNER - CUT :])
    ga[...] = small[0]
    gf[...] = small[1]
    gb[...] = small[2, : BUCKETS // n_f * HEADS]
    chunks = [halves(packs[0]), halves(packs[1])]
    for which, ref in enumerate((gg, gu)):
        wide = [jnp.concatenate([c[which][:ds], c[which][ds : 2 * ds]], axis=1) for c in chunks]
        width = wide[0].shape[1] // n_f
        ref[...] = jnp.concatenate(
            [w[:, f * width : (f + 1) * width] for f in range(n_f) for w in wide], axis=1
        )
    for chunk, pair in enumerate(chunks):
        for which in range(2):
            gd[chunk * fh : (chunk + 1) * fh, which * half : (which + 1) * half] = pair[which][2 * ds : 2 * ds + fh]
    for which in range(2):
        go[:, which * half : (which + 1) * half] = chunks[1][which][2 * ds + fh : 2 * ds + fh + is_]


def call_finish(place, n_f, packs, shapes, after):
    vm, sm = pl.BlockSpec(memory_space=pltpu.VMEM), pl.BlockSpec(memory_space=pltpu.SMEM)
    flat = [piece for pack in packs for piece in pack]
    return pl.pallas_call(
        functools.partial(finish, n_f),
        out_shape=tuple(sds(shape, f32) for shape in shapes),
        in_specs=[sm] + [vm] * len(flat) + [vm],
        out_specs=[vm] * len(shapes),
        compiler_params=small_params(),
        name="finish",
    )(place, *flat, after)


def solution(mesh):
    n_r, n_f = mesh.shape["rep"], mesh.shape["fsdp"]
    n_z = n_f // 2

    def over_fsdp(value, distance):
        return lax.ppermute(value, "fsdp", [(i, i ^ distance) for i in range(n_f)])

    def over_rep(value, distance):
        return lax.ppermute(value, "rep", [(i, i ^ distance) for i in range(n_r)])

    def along_z(pack):
        return [pack] + [over_fsdp(pack, 2 * k) for k in range(1, n_z)]

    def halved(keep, got):
        away = (keep[1].astype(f32) + got[1].astype(f32)).astype(bf16)
        return keep[0].astype(f32) + got[0].astype(f32), away

    def joined(here, got):
        here = here + got.astype(f32)
        return here[0], [here[k].astype(bf16) for k in range(1, n_z)]

    def to_z(pieces):
        return [over_fsdp(piece, 2 * (k + 1)) for k, piece in enumerate(pieces)]

    def summed(own, got):
        for value in got:
            own = own + value.astype(f32)
        return own.astype(bf16)

    def replicas(own):
        distance = 2
        while distance < n_r:
            own = (own.astype(f32) + over_rep(own, distance).astype(f32)).astype(bf16)
            distance *= 2
        return own, over_rep(own, 1)

    together = lax.optimization_barrier

    def body(tokens, counts, attn_gain, wq, wk, wv, wo, rel_bias, ffn_gain, wg, wu, wd, cotangent):
        S, L, D = tokens.shape
        r, f = lax.axis_index("rep"), lax.axis_index("fsdp")
        place = in_hbm(jnp.stack([counts[0, 0], r % 2, f % 2, f // 2]).astype(jnp.int32))
        pack_a = call_prepare_attention(place, n_f, attn_gain, wq, wk, wv, rel_bias, ffn_gain)
        pack_0, pack_1 = call_prepare_ffn(place, n_f, wo, wg, wu, wd)

        z_0 = along_z(pack_0)
        z_a, pack_1 = together((along_z(pack_a), pack_1))
        near_a = jnp.stack(z_a)
        far_a, near_ac = over_fsdp(near_a, 1), over_rep(near_a, 1)
        tokens, cotangent, done = call_keep_close(tokens, cotangent)
        done, far_a, near_ac, z_0, pack_1 = together((done, far_a, near_ac, z_0, pack_1))
        far_ac, near_0 = over_rep(far_a, 1), jnp.stack(z_0)
        far_ac, near_0 = together((far_ac, near_0))

        far_0, near_0c, z_1 = over_fsdp(near_0, 1), over_rep(near_0, 1), along_z(pack_1)
        qkv, probs, mixed, w_all, gains = call_attention_forward(place, tokens, done, (near_a, far_a, near_ac, far_ac))
        gains, far_0, near_0c, z_1 = together((gains, far_0, near_0c, z_1))
        far_0c, near_1 = over_rep(far_0, 1), jnp.stack(z_1)
        far_0c, near_1 = together((far_0c, near_1))

        far_1, near_1c = over_fsdp(near_1, 1), over_rep(near_1, 1)
        hidden, act_0, gpart, wd_0, wo_all, keep_0, send_0 = call_ffn_half(
            0, place, n_z, (near_0, far_0, near_0c, far_0c, tokens, cotangent, mixed, gains), S, L, D
        )
        wo_all, keep_0, send_0, far_1, near_1c = together((wo_all, keep_0, send_0, far_1, near_1c))

        far_1c, got_0 = over_rep(far_1, 1), over_rep(send_0, 1)
        *running, gf, wd_1, wgu = call_ffn_half(
            1, place, n_z, (near_1, far_1, near_1c, far_1c, hidden, cotangent, gains, wo_all, gpart, mixed), S, L, D
        )
        gf, got_0 = together((gf, got_0))
        here_0, away_0 = halved(keep_0, got_0)
        away_0, gf = together((away_0, gf))
        got_0 = over_fsdp(away_0, 1)
        gh, gm, act_1, _, _, _, gf, keep_1, send_1 = call_ffn_half(
            2, place, n_z, (hidden, cotangent, gains, wo_all, wd_1, wgu, *running, gf), S, L, D
        )
        keep_1, send_1, gf, got_0 = together((keep_1, send_1, gf, got_0))
        own_0, z_0 = joined(here_0, got_0)
        z_0, got_1 = to_z(z_0), over_rep(send_1, 1)
        here_1, away_1 = halved(keep_1, got_1)
        gf, away_1 = together((gf, away_1))
        got_1 = over_fsdp(away_1, 1)
        dqkv, keep_2, send_2 = call_attention_backward(place, n_z, tokens, qkv, probs, gm, w_all, gains, gf)
        keep_2, send_2, z_0, got_1 = together((keep_2, send_2, z_0, got_1))
        sum_0 = summed(own_0, z_0)
        own_1, z_1 = joined(here_1, got_1)

        z_1, got_2 = to_z(z_1), over_rep(send_2, 1)
        here_2, away_2 = halved(keep_2, got_2)
        gains, away_2, sum_0 = together((gains, away_2, sum_0))
        got_2 = over_fsdp(away_2, 1)
        half_tokens, done = call_token_gradient(place, tokens, dqkv, gh, w_all, gains, 0)
        grad_tokens, done = call_token_gradient(place, tokens, dqkv, gh, w_all, done, 1, half_tokens)
        done, got_2, z_1 = together((done, got_2, z_1))
        sum_1 = summed(own_1, z_1)
        own_2, z_2 = joined(here_2, got_2)
        done, z_2 = together((done, z_2))
        z_2 = to_z(z_2)
        layer_out, done = call_layer_result(place, hidden, act_0, act_1, wd_0, wd_1, done, S, L)
        done, z_2 = together((done, z_2))
        sum_2 = summed(own_2, z_2)
        gq, gk, gv, go, gg, gu, gd, grad_attn_gain, grad_ffn_gain, grad_bias = call_finish(
            place, n_f, [replicas(value) for value in (sum_0, sum_1, sum_2)],
            (wq.shape, wk.shape, wv.shape, wo.shape, wg.shape, wu.shape, wd.shape,
             attn_gain.shape, ffn_gain.shape, rel_bias.shape), done,
        )
        return (layer_out, grad_tokens, grad_attn_gain, gq, gk, gv, go, grad_bias, grad_ffn_gain, gg, gu, gd)

    rows, cols, flat = P(("rep", "fsdp"), None, None), P("fsdp", None), P("fsdp")
    return jax.shard_map(
        body,
        mesh=mesh,
        in_specs=(rows, P("rep", "fsdp"), flat, cols, cols, cols, cols, flat, flat, cols, cols, cols, rows),
        out_specs=(rows, rows, flat, cols, cols, cols, cols, flat, flat, cols, cols, cols),
        check_vma=False,
    )
```

```python
import functools

import jax
import jax.numpy as jnp
from jax import lax
from jax.experimental import pallas as pl
from jax.experimental.pallas import tpu as pltpu
from jax.sharding import PartitionSpec as P

HEADS, HDIM, BUCKETS = 6, 64, 32
INNER = HEADS * HDIM
PAIRS = HEADS // 2
PAIR = 2 * HDIM
CUT = 640
GROUP = 8
EPS = 1e-6
bf16, f32 = jnp.bfloat16, jnp.float32
sds = jax.ShapeDtypeStruct


def in_hbm(value):
    return pltpu.with_memory_space_constraint(value, pltpu.HBM)


def nn(a, b):
    return jnp.dot(a, b, preferred_element_type=f32)


def nt(a, b):
    return lax.dot_general(a, b, (((1,), (1,)), ((), ())), preferred_element_type=f32)


def tn(a, b):
    return lax.dot_general(a, b, (((0,), (0,)), ((), ())), preferred_element_type=f32)


def bucket_edges():
    half = BUCKETS // 2
    exact = half // 2
    power = half - exact
    return [
        min(m for m in range(exact, 129) if m**power * exact**k >= 128**k * exact**power) for k in range(1, power)
    ]


def bucket_table(length):
    half = BUCKETS // 2
    exact = half // 2
    shape = (length, PAIR)
    apart = lax.broadcasted_iota(jnp.int32, shape, 0) - lax.broadcasted_iota(jnp.int32, shape, 1) % HDIM
    distance = jnp.abs(apart)
    bucket = jnp.minimum(distance, exact)
    for edge in bucket_edges():
        bucket = bucket + (distance >= edge).astype(jnp.int32)
    return bucket + jnp.where(apart > 0, half, 0)


def lane_low(shape):
    return lax.broadcasted_iota(jnp.int32, shape, 1) < HDIM


def split_heads(pair):
    low, zero = lane_low(pair.shape), jnp.zeros_like(pair)
    return jnp.concatenate([jnp.where(low, pair, zero), jnp.where(low, zero, pair)], axis=0)


def join_heads(both):
    rows = both.shape[0] // 2
    return jnp.where(lane_low((rows, PAIR)), both[:rows], both[rows:])


def row_sums(values):
    rows, width = values.shape
    return jnp.sum(values.reshape(rows // 8, 8, width), axis=0)


def inverse_rms(values):
    return lax.rsqrt(jnp.mean(values * values, axis=-1, keepdims=True) + EPS)


class Place:
    def __init__(self, ref, n_z):
        self.count, self.core, self.x, self.z = ref[0], ref[1], ref[2], ref[3]
        self.n_z = n_z

    def shards(self):
        for xx in range(2):
            for k in range(self.n_z):
                yield xx, k, jnp.bitwise_xor(self.z, k) * 2 + jnp.bitwise_xor(self.x, xx)


def at(shard, size):
    return pl.ds(pl.multiple_of(shard * size, size), size)


def interleaved(values, n_f, chunk):
    width = values.shape[1] // n_f // 2
    return jnp.concatenate(
        [values[:, (2 * f + chunk) * width : (2 * f + chunk + 1) * width] for f in range(n_f)], axis=1
    )


def prepare_attention(n_f, place_ref, bias_ref, wq, wk, wv, ga, gf, a_ref):
    core = place_ref[1]
    ds = wq.shape[0]
    joined = jnp.concatenate([wq[...], wk[...], wv[...]], axis=1)
    row = lax.broadcasted_iota(jnp.int32, (ds, PAIR), 0)
    low = lane_low((1, PAIR))
    small = jnp.zeros((ds, PAIR), f32)
    n_b = BUCKETS // n_f
    for b in range(n_b):
        for p in range(PAIRS):
            value = jnp.where(low, bias_ref[b * HEADS + 2 * p], bias_ref[b * HEADS + 2 * p + 1])
            small = jnp.where(row == b * PAIRS + p, value, small)
    for i, gain in enumerate((ga, gf)):
        tiled = jnp.concatenate([gain[...]] * (PAIR // ds), axis=1)
        small = jnp.where(row == n_b * PAIRS + i, tiled, small)

    def write(c):
        if c == 0:
            a_ref[...] = joined[:, :CUT].astype(bf16)
        else:
            a_ref[:, : 3 * INNER - CUT] = joined[:, CUT:].astype(bf16)
            a_ref[:, 3 * INNER - CUT :] = small.astype(bf16)

    for c in range(2):
        pl.when(core == c)(functools.partial(write, c))


def prepare_ffn(n_f, place_ref, wo, wg, wu, wd, p0_ref, p1_ref):
    core = place_ref[1]
    ds, is_, fh = wg.shape[0], wo.shape[0], wd.shape[0] // 2
    half = wo.shape[1] // 2

    def write(c):
        cols = slice(c * half, (c + 1) * half)
        for chunk, ref in enumerate((p0_ref, p1_ref)):
            g = interleaved((wg, wu)[c][...], n_f, chunk).astype(bf16)
            ref[:ds, :] = g[:, :half]
            ref[ds : 2 * ds, :] = g[:, half:]
            ref[2 * ds : 2 * ds + fh, :] = wd[chunk * fh : (chunk + 1) * fh, cols].astype(bf16)
        tail = wo[:, cols]
        pad = p0_ref.shape[0] - (2 * ds + fh + is_)
        if pad:
            tail = jnp.concatenate([tail, jnp.zeros((pad, half), f32)], axis=0)
        p0_ref[2 * ds + fh :, :] = tail.astype(bf16)

    for c in range(2):
        pl.when(core == c)(functools.partial(write, c))


def small_params():
    return pltpu.CompilerParams(vmem_limit_bytes=12 * 1024 * 1024)


def padded(rows):
    return -(-rows // 16) * 16


def call_prepare_attention(place, n_f, attn_gain, wq, wk, wv, rel_bias, ffn_gain):
    vm, sm = pl.BlockSpec(memory_space=pltpu.VMEM), pl.BlockSpec(memory_space=pltpu.SMEM)
    return pl.pallas_call(
        functools.partial(prepare_attention, n_f),
        out_shape=sds((wq.shape[0], CUT), bf16),
        in_specs=[sm, sm] + [vm] * 5,
        out_specs=vm,
        name="prepare_attention",
    )(place, rel_bias, wq, wk, wv, attn_gain.reshape(1, -1), ffn_gain.reshape(1, -1))


def call_prepare_ffn(place, n_f, wo, wg, wu, wd):
    ds, fh, half = wg.shape[0], wd.shape[0] // 2, wo.shape[1] // 2
    vm, sm = pl.BlockSpec(memory_space=pltpu.VMEM), pl.BlockSpec(memory_space=pltpu.SMEM)
    return pl.pallas_call(
        functools.partial(prepare_ffn, n_f),
        out_shape=(sds((2 * ds + fh + padded(wo.shape[0]), half), bf16), sds((2 * ds + fh, half), bf16)),
        in_specs=[sm] + [vm] * 4,
        out_specs=[vm] * 2,
        name="prepare_ffn",
    )(place, wo, wg, wu, wd)


def keep_close(G, L, place_ref, tok_ref, ct_ref, tok_out, ct_out, done_ref):
    step = pl.program_id(0)
    R, D = G * L, tok_ref.shape[-1]
    live = (step * G + lax.broadcasted_iota(jnp.int32, (R, 1), 0) // L) < place_ref[0]
    group_rows(tok_out, step, R)[...] = tok_ref[...].reshape(R, D)
    group_rows(ct_out, step, R)[...] = jnp.where(live, ct_ref[...].reshape(R, D), jnp.zeros((), bf16))
    done_ref[...] = jnp.zeros_like(done_ref)


def call_keep_close(place, tokens, ct):
    S, L, D = tokens.shape
    G = GROUP
    block = pl.BlockSpec((G, L, D), lambda i, c: (i, 0, 0))
    return pl.pallas_call(
        functools.partial(keep_close, G, L),
        out_shape=(sds((S * L, D), bf16), sds((S * L, D), bf16), sds((8, PAIR), f32)),
        grid_spec=pltpu.PrefetchScalarGridSpec(
            num_scalar_prefetch=1, grid=(S // G,), in_specs=[block, block], out_specs=[whole(None)] * 3
        ),
        compiler_params=params(MIB_TOKENS),
        cost_estimate=cost(S * L, 1, 8 * S * L * D),
        name="keep_close",
    )(place, in_hbm(tokens), in_hbm(ct))


def attention_forward(G, L, n_z, place_ref, tok_ref, after_ref, *refs):
    pieces, refs = refs[:4], refs[4:]
    all_qkv, all_probs, mixed_ref, w_ref, gains_ref, table_ref, st_ref, small_ref = refs
    step = pl.program_id(0)
    place = Place(place_ref, n_z)
    D = tok_ref.shape[-1]
    n_f = 2 * n_z
    ds = D // n_f
    rest = 3 * INNER - CUT

    def assemble(c):
        for xx, k, f in place.shards():
            one, two = pieces[xx].at[k], pieces[2 + xx].at[k]
            one, two = (one, two) if c == 0 else (two, one)
            w_ref[at(f, ds), :CUT] = one[...]
            w_ref[at(f, ds), CUT:] = two[:, :rest]
            small_ref[at(f, ds), :] = two[:, rest:].astype(f32)

    @pl.when(step == 0)
    def _():
        for c in range(2):
            pl.when(place.core == c)(functools.partial(assemble, c))
        n_b = BUCKETS // n_f
        ids = bucket_table(L)
        for p in range(PAIRS):
            total = jnp.zeros(ids.shape, f32)
            for b in range(BUCKETS):
                row = b // n_b * ds + (b % n_b) * PAIRS + p
                total = jnp.where(ids == b, small_ref[row : row + 1, :], total)
            table_ref[p] = total
        per = PAIR // ds
        lane = lax.broadcasted_iota(jnp.int32, (1, PAIR), 1) // ds
        gains_ref[...] = jnp.zeros_like(gains_ref)
        for i in range(2):
            for v in range(D // PAIR):
                total = jnp.zeros((1, PAIR), f32)
                for f in range(per):
                    row = (v * per + f) * ds + n_b * PAIRS + i
                    total = jnp.where(lane == f, small_ref[row : row + 1, :], total)
                gains_ref[i : i + 1, v * PAIR : (v + 1) * PAIR] = total

    @pl.when(step * G < place.count)
    def _():
        mixed, qkv_ref = group_rows(mixed_ref, step, G * L), group_rows(all_qkv, step, G * L)
        probs_ref = all_probs.at[pl.ds(step * G, G)]
        x = group_rows(tok_ref, step, G * L)[...].astype(f32)
        normed = (x * inverse_rms(x) * gains_ref[0:1, :]).astype(bf16)
        qkv_ref[...] = nn(normed, w_ref[...]).astype(bf16)
        for s in range(G):
            rows = pl.ds(s * L, L)
            for p in range(PAIRS):
                q = qkv_ref[rows, pl.ds(p * PAIR, PAIR)]
                k = qkv_ref[rows, pl.ds(INNER + p * PAIR, PAIR)]
                st_ref[s, p] = nt(k, split_heads(q))
        for s in range(G):
            for p in range(PAIRS):
                st = st_ref[s, p] + table_ref[p]
                e = jnp.exp(st - jnp.max(st, axis=0, keepdims=True))
                probs_ref[s, p] = (e * (1.0 / jnp.sum(e, axis=0, keepdims=True))).astype(bf16)
        for s in range(G):
            rows = pl.ds(s * L, L)
            for p in range(PAIRS):
                v = qkv_ref[rows, pl.ds(2 * INNER + p * PAIR, PAIR)]
                mixed[rows, pl.ds(p * PAIR, PAIR)] = join_heads(tn(probs_ref[s, p], v)).astype(bf16)


MIB_FORWARD, MIB_FFN, MIB_BACKWARD, MIB_TOKENS, MIB_RESULT = 8, 14, 10, 6, 6


def params(mib):
    return pltpu.CompilerParams(dimension_semantics=("arbitrary",), vmem_limit_bytes=mib * 1024 * 1024)


def whole(shape):
    return pl.BlockSpec(memory_space=pltpu.VMEM)


def live_group(i, place, G):
    return jnp.minimum(i, jnp.maximum((place[0] + G - 1) // G - 1, 0))


def series_spec(G, shape, every=False):
    tail = (0,) * (len(shape) - 1)
    return pl.BlockSpec((G,) + shape[1:], lambda i, c: ((i if every else live_group(i, c, G)),) + tail)


def row_spec(G, L, width):
    return pl.BlockSpec((G * L, width), lambda i, c: (live_group(i, c, G), 0))


def group_rows(ref, step, rows):
    return ref.at[pl.ds(pl.multiple_of(step * rows, rows), rows), :]


def cost(rows, per_row, nbytes, exps=0):
    return pl.CostEstimate(flops=2 * rows * per_row, bytes_accessed=nbytes, transcendentals=exps)


def call_attention_forward(place, tokens, after, pieces, S, L, D):
    G, n_z = GROUP, pieces[0].shape[0]
    return pl.pallas_call(
        functools.partial(attention_forward, G, L, n_z),
        out_shape=(
            sds((S * L, 3 * INNER), bf16),
            sds((S, PAIRS, L, PAIR), bf16),
            sds((S * L, INNER), bf16),
            sds((D, 3 * INNER), bf16),
            sds((8, D), f32),
        ),
        grid_spec=pltpu.PrefetchScalarGridSpec(
            num_scalar_prefetch=1,
            grid=(S // G,),
            in_specs=[whole(tokens.shape), whole(after.shape)] + [whole(piece.shape) for piece in pieces],
            out_specs=[
                whole((S * L, 3 * INNER)),
                whole((S, PAIRS, L, PAIR)),
                whole((S * L, INNER)),
                whole((D, 3 * INNER)),
                whole((8, D)),
            ],
            scratch_shapes=[
                pltpu.VMEM((PAIRS, L, PAIR), f32),
                pltpu.VMEM((G, PAIRS, L, PAIR), f32),
                pltpu.VMEM((D, PAIR), f32),
            ],
        ),
        compiler_params=params(MIB_FORWARD),
        cost_estimate=cost(S * L, D * 3 * INNER * 4, S * L * 5000),
        name="attention_forward",
    )(place, tokens, after, *pieces)


def gelu_parts(v):
    c = 0.7978845608028654
    v2 = v * v
    t = jnp.tanh(v * (c + (c * 0.044715) * v2))
    half = 0.5 + 0.5 * t
    return v * half, half + (0.5 * v) * (1.0 - t * t) * (c + (3 * c * 0.044715) * v2)


def put_weights(place, pieces, wgu, wd, wo=None):
    FW, D = wd.shape

    def assemble(c):
        for f, here, there in pieces:
            for which, piece in enumerate((here, there) if c == 0 else (there, here)):
                n_f = len(pieces)
                ds, fh, half, is_ = D // n_f, FW // n_f, FW // 2, INNER // n_f
                for part in range(2):
                    start = (2 * part + which) * half
                    wgu[at(f, ds), start : start + half] = piece[part * ds : (part + 1) * ds, :]
                cols = slice(which * half, (which + 1) * half)
                wd[at(f, fh), cols] = piece[2 * ds : 2 * ds + fh, :]
                if wo is None:
                    continue
                if is_ % 16 == 0:
                    wo[at(f, is_), cols] = piece[2 * ds + fh : 2 * ds + fh + is_, :]
                else:
                    wo[f, :, cols] = piece[2 * ds + fh :, :]

    for c in range(2):
        pl.when(place.core == c)(functools.partial(assemble, c))


def put_grads(place, n_z, keep, send, agu, ad, ao=None):
    n_f = 2 * n_z
    FW, D = ad.shape
    ds, fh, half = D // n_f, FW // n_f, FW // 2

    def write(c):
        for xx, k, f in place.shards():
            for which, ref in enumerate((keep, send) if c == 0 else (send, keep)):
                for part in range(2):
                    start = (2 * part + which) * half
                    ref[xx, k, part * ds : (part + 1) * ds, :] = agu[at(f, ds), start : start + half].astype(bf16)
                cols = slice(which * half, (which + 1) * half)
                ref[xx, k, 2 * ds : 2 * ds + fh, :] = ad[at(f, fh), cols].astype(bf16)
                if ao is not None:
                    is_ = INNER // n_f
                    if is_ % 16 == 0:
                        ref[xx, k, 2 * ds + fh :, :] = ao[at(f, is_), cols].astype(bf16)
                    else:
                        ref[xx, k, 2 * ds + fh :, :] = ao[f, :, cols].astype(bf16)

    for c in range(2):
        pl.when(place.core == c)(functools.partial(write, c))


def ffn_half(G, L, n_z, stage, shift, place_ref, *refs):
    n_f = 2 * n_z
    place = Place(place_ref, n_z)
    first, begins, ends = stage == 0, stage < 2, stage != 1
    if begins:
        pieces, refs = refs[:4], refs[4:]
        pieces = [(f, pieces[xx].at[k], pieces[2 + xx].at[k]) for xx, k, f in place.shards()]
    if stage == 0:
        (tok_ref, ct_ref, mixed_ref, gains_ref,
         hid_ref, act_ref, gpart_ref, wd, wo_out, keep, send,
         agu, ad, wgu, n2, n2_next, gu, ga, low, gn, spread) = refs
    elif stage == 1:
        hid_ref, ct_ref, gains_ref, wo_in, _, _ = refs[:6]
        gpart_ref, mixed_ref, act_ref, agu, ad, ao, gf_ref, wd, wgu, n2, n2_next, gu, ga, low, gn = refs[6:]
    else:
        hid_ref, ct_ref, gains_ref, wo_in, wd, wgu = refs[:6]
        gpart_ref, mixed_ref, act_ref, agu, ad, ao, gf_ref, keep, send, n2, n2_next, gu, ga, low, gn, spread = refs[13:]
    step = pl.program_id(0) + shift
    R = G * L
    FW, D = wd.shape
    CH = FW // 2
    is_ = INNER // n_f
    count = place.count
    group = jnp.minimum(step, (count + G - 1) // G - 1)

    def normalise(group, into):
        if first:
            h = group_rows(tok_ref, group, R)[...].astype(f32) + nn(group_rows(mixed_ref, group, R)[...], wo_out[...])
            group_rows(hid_ref, group, R)[...] = h.astype(bf16)
        else:
            h = group_rows(hid_ref, group, R)[...].astype(f32)
        into[...] = (h * inverse_rms(h) * gains_ref[1:2, :]).astype(bf16)

    if begins:

        @pl.when(step == 0)
        def _():
            wo = (wo_out if is_ % 16 == 0 else spread) if first else None
            put_weights(place, pieces, wgu, wd, wo)
            if first and is_ % 16:
                wo_out[...] = jnp.concatenate([spread[f, :is_, :].astype(f32) for f in range(n_f)], axis=0).astype(bf16)
            for ref in (agu, ad) if first else (agu, ad, ao, gf_ref):
                ref[...] = jnp.zeros_like(ref)

    @pl.when(step * G < count)
    def _():
        normalise(group, n2)
        gb, act, gpart, hid = (group_rows(ref, group, R) for ref in (ct_ref, act_ref, gpart_ref, hid_ref))
        for c in range(2):
            cols, both = pl.ds(c * CH, CH), pl.ds(2 * c * CH, 2 * CH)
            gu[c] = nn(n2[...], wgu[:, both])
            ga[c] = nt(gb[...], wd[cols, :])
        for c in range(2):
            cols, both = pl.ds(c * CH, CH), pl.ds(2 * c * CH, 2 * CH)
            for r in range(0, R, L):
                rows = pl.ds(r, L)
                u = gu[c, rows, CH:]
                a = ga[c, rows, :]
                g, dg = gelu_parts(gu[c, rows, :CH])
                act[rows, cols] = (g * u).astype(bf16)
                low[c, rows, :CH] = (a * u * dg).astype(bf16)
                low[c, rows, CH:] = (a * g).astype(bf16)
            if c == 0:
                gn[...] = nt(low[c], wgu[:, both])
            else:
                gn[...] += nt(low[c], wgu[:, both])
            ad[cols, :] += tn(act[:, cols], gb[...])
            agu[:, both] += tn(n2[...], low[c])
        if first:
            gpart[...] = gn[...].astype(bf16)
        else:
            mixed = group_rows(mixed_ref, group, R)
            h = hid[...].astype(f32)
            scale = inverse_rms(h)
            hs = h * scale
            g2 = gn[...] + gpart[...].astype(f32)
            gf_ref[...] += row_sums(g2 * hs)
            g2 = g2 * gains_ref[1:2, :]
            dot = jnp.mean(g2 * hs, axis=-1, keepdims=True)
            gh = (gb[...].astype(f32) + scale * (g2 - hs * dot)).astype(bf16)
            gpart[...] = gh
            ao[...] += tn(mixed[...], gh)
            mixed[...] = nt(gh, wo_in[...]).astype(bf16)

    if ends:

        @pl.when(pl.program_id(0) == pl.num_programs(0) - 1)
        def _():
            if first:
                put_grads(place, n_z, keep, send, agu, ad)
            elif is_ % 16 == 0:
                put_grads(place, n_z, keep, send, agu, ad, ao)
            else:
                for f in range(n_f):
                    spread[f, :is_, :] = ao[f * is_ : (f + 1) * is_, :]
                put_grads(place, n_z, keep, send, agu, ad, spread)


def call_ffn_half(stage, place, n_z, operands, S, L, D):
    G = GROUP
    R, n_f = G * L, 2 * n_z
    FW = D
    CH = FW // 2
    ds, fh, is_ = D // n_f, FW // n_f, INNER // n_f
    pack = (2, n_z, 2 * ds + fh + (padded(is_) if stage else 0), CH)
    packs, act = [sds(pack, bf16)] * 2, sds((S * L, FW), bf16)
    wd, wgu, rows = sds((FW, D), bf16), sds((D, 2 * FW), bf16), sds((S * L, D), bf16)
    agu, ad = sds((D, 2 * FW), f32), sds((FW, D), f32)
    running = [rows, sds((S * L, INNER), bf16), act, agu, ad, sds((INNER, D), f32), sds((8, D), f32)]
    vm = pltpu.VMEM
    work = [
        vm((R, D), bf16), vm((R, D), bf16),
        vm((2, R, 2 * CH), f32), vm((2, R, CH), f32), vm((2, R, 2 * CH), bf16), vm((R, D), f32),
    ]
    spread = [vm((n_f, padded(is_), D) if is_ % 16 else (1, 16, 128), f32 if stage else bf16)]
    half = S // G // 2
    steps, shift = ((S // G, 0), (half, 0), (S // G - half, half))[stage]
    if stage == 0:
        out_shape = [rows, act, rows, wd, sds((INNER, D), bf16)] + packs
        scratch = [vm(agu.shape, f32), vm(ad.shape, f32), vm(wgu.shape, bf16)] + work + spread
        aliases = {}
    elif stage == 1:
        out_shape, scratch = running + [wd, wgu], work
        aliases = {9: 0, 10: 1}
    else:
        out_shape, scratch = running + packs, work + spread
        aliases = {7 + i: i for i in range(7)}
    return pl.pallas_call(
        functools.partial(ffn_half, G, L, n_z, stage, shift),
        out_shape=tuple(out_shape),
        grid_spec=pltpu.PrefetchScalarGridSpec(
            num_scalar_prefetch=1,
            grid=(steps,),
            in_specs=[whole(a.shape) for a in operands],
            out_specs=[whole(shape.shape) for shape in out_shape],
            scratch_shapes=scratch,
        ),
        input_output_aliases=aliases,
        compiler_params=params(MIB_FFN),
        cost_estimate=cost(steps * R, 9 * D * FW, S * L * 9000),
        name=("ffn_first", "ffn_second", "ffn_third")[stage],
    )(place, *operands)


def layer_result(G, L, shift, place_ref, hid_ref, act_0, act_1, wd_0, wd_1, gains_ref, *refs):
    out_ref, done_ref = refs[-2:]
    step = pl.program_id(0) + shift
    count = place_ref[0]
    R = G * L
    D = hid_ref.shape[-1]
    done_ref[...] = gains_ref[...]
    group = jnp.minimum(step, (count + G - 1) // G - 1)
    hid_ref, act_0, act_1 = (group_rows(ref, group, R) for ref in (hid_ref, act_0, act_1))

    @pl.when(step * G >= count)
    def _():
        out_ref[...] = jnp.zeros_like(out_ref)

    @pl.when(step * G < count)
    def _():
        live = (step * G + lax.broadcasted_iota(jnp.int32, (R, 1), 0) // L) < count
        out = hid_ref[...].astype(f32) + nn(act_0[...], wd_0[...]) + nn(act_1[...], wd_1[...])
        out_ref[...] = jnp.where(live, out, 0.0).astype(bf16).reshape(G, L, D)


def call_layer_result(place, hidden, act_0, act_1, wd_0, wd_1, gains, S, L, earlier=None):
    G, D = GROUP, hidden.shape[-1]
    operands = (hidden, act_0, act_1, wd_0, wd_1, gains)
    half = S // G // 2
    steps, shift = (half, 0) if earlier is None else (S // G - half, half)
    more = () if earlier is None else (earlier,)
    return pl.pallas_call(
        functools.partial(layer_result, G, L, shift),
        out_shape=(pltpu.HBM((S, L, D), bf16), sds(gains.shape, f32)),
        grid_spec=pltpu.PrefetchScalarGridSpec(
            num_scalar_prefetch=1,
            grid=(steps,),
            in_specs=[whole(a.shape) for a in operands] + [pl.BlockSpec(memory_space=pl.ANY)] * len(more),
            out_specs=(pl.BlockSpec((G, L, D), lambda i, c: (i + shift, 0, 0)), whole(gains.shape)),
        ),
        input_output_aliases={7: 0} if more else {},
        compiler_params=params(MIB_RESULT),
        cost_estimate=cost(S * L // 2, 2 * D * act_0.shape[-1], S * L * 3000),
        name="layer_result",
    )(place, *operands, *more)


def attention_backward(G, L, n_z, place_ref, tok_ref, _, probs_ref, gm_ref, w_ref, gains_ref, gf_ref,
                       dqkv, keep, send, aw, ab, dp_ref, ds_ref, small):
    step = pl.program_id(0)
    last = pl.num_programs(0) - 1
    R = G * L
    D = tok_ref.shape[-1]
    place = Place(place_ref, n_z)
    count = place.count
    group = jnp.minimum(step, (count + G - 1) // G - 1)
    probs_ref = probs_ref.at[pl.ds(group * G, G)]
    gm_ref, dqkv = group_rows(gm_ref, group, R), group_rows(dqkv, group, R)

    @pl.when(step == 0)
    def _():
        for ref in (aw, ab):
            ref[...] = jnp.zeros_like(ref)

    @pl.when(step * G < count)
    def _():
        cols = [[pl.ds(b * INNER + p * PAIR, PAIR) for b in range(3)] for p in range(PAIRS)]
        for p in range(PAIRS):
            for s in range(G):
                rows = pl.ds(s * L, L)
                dm = split_heads(gm_ref[rows, pl.ds(p * PAIR, PAIR)])
                dp_ref[s, p] = nt(dqkv[rows, cols[p][2]], dm)
                dqkv[rows, cols[p][2]] = nn(probs_ref[s, p], dm).astype(bf16)
        for p in range(PAIRS):
            total = ab[p]
            for s in range(G):
                prf = probs_ref[s, p].astype(f32)
                dp = dp_ref[s, p]
                ds = prf * (dp - jnp.sum(prf * dp, axis=0, keepdims=True))
                total = total + ds
                ds_ref[s, p] = ds.astype(bf16)
            ab[p] = total
        for p in range(PAIRS):
            for s in range(G):
                rows = pl.ds(s * L, L)
                low = ds_ref[s, p]
                q, k = dqkv[rows, cols[p][0]], dqkv[rows, cols[p][1]]
                dqkv[rows, cols[p][1]] = nn(low, split_heads(q)).astype(bf16)
                dqkv[rows, cols[p][0]] = join_heads(tn(low, k)).astype(bf16)
        x = group_rows(tok_ref, group, R)[...].astype(f32)
        aw[...] += tn((x * inverse_rms(x) * gains_ref[0:1, :]).astype(bf16), dqkv[...])

    @pl.when(step == last)
    def _():
        n_f = 2 * n_z
        ds, n_b, rest = D // n_f, BUCKETS // n_f, 3 * INNER - CUT
        ids = bucket_table(L)
        low = lane_low((1, PAIR))
        small[...] = jnp.zeros_like(small)
        for p in range(PAIRS):
            t = ab[p]
            for b in range(BUCKETS):
                by_lane = jnp.sum(jnp.where(ids == b, t, 0.0), axis=0, keepdims=True)
                one = jnp.sum(jnp.where(low, by_lane, 0.0), axis=1, keepdims=True)
                two = jnp.sum(jnp.where(low, 0.0, by_lane), axis=1, keepdims=True)
                row = b // n_b * ds + (b % n_b) * HEADS + 2 * p
                small[row : row + 1, :] = jnp.broadcast_to(one, (1, PAIR))
                small[row + 1 : row + 2, :] = jnp.broadcast_to(two, (1, PAIR))
        gain = jnp.transpose(gains_ref[...])[:, 0:1]
        one = jnp.sum(aw[...] * w_ref[...].astype(f32), axis=1, keepdims=True) / gain
        two = jnp.sum(jnp.transpose(gf_ref[...]), axis=1, keepdims=True)
        lane = lax.broadcasted_iota(jnp.int32, (D, PAIR), 1)
        small[...] = jnp.where(lane == 0, one, jnp.where(lane == 1, two, small[...]))

        def write(c):
            for xx, k, f in place.shards():
                one, two = keep.at[xx, k], send.at[xx, k]
                one, two = (one, two) if c == 0 else (two, one)
                one[...] = aw[at(f, ds), :CUT].astype(bf16)
                two[:, :rest] = aw[at(f, ds), CUT:].astype(bf16)
                two[:, rest:] = small[at(f, ds), :].astype(bf16)

        for c in range(2):
            pl.when(place.core == c)(functools.partial(write, c))


def call_attention_backward(place, n_z, tokens, qkv, probs, gm, w, gains, gf, S, L, D):
    G = GROUP
    pack = (2, n_z, D // (2 * n_z), CUT)
    vm = pltpu.VMEM
    return pl.pallas_call(
        functools.partial(attention_backward, G, L, n_z),
        out_shape=(sds((S * L, 3 * INNER), bf16), sds(pack, bf16), sds(pack, bf16)),
        grid_spec=pltpu.PrefetchScalarGridSpec(
            num_scalar_prefetch=1,
            grid=(S // G,),
            in_specs=[whole(tokens.shape), whole(qkv.shape), whole(probs.shape),
                      whole(gm.shape), whole(w.shape), whole(gains.shape), whole(gf.shape)],
            out_specs=[whole(pack)] * 3,
            scratch_shapes=[
                vm(w.shape, f32), vm((PAIRS, L, PAIR), f32),
                vm((G, PAIRS, L, PAIR), f32), vm((G, PAIRS, L, PAIR), bf16), vm((D, PAIR), f32),
            ],
        ),
        input_output_aliases={2: 0},
        compiler_params=params(MIB_BACKWARD),
        cost_estimate=cost(S * L, D * 3 * INNER * 4, S * L * 6000),
        name="attention_backward",
    )(place, tokens, qkv, probs, gm, w, gains, gf)


def token_gradient(G, L, place_ref, tok_ref, dqkv_ref, gh_ref, w_ref, gains_ref, gt_ref, done_ref):
    step = pl.program_id(0)
    D = tok_ref.shape[-1]
    done_ref[...] = gains_ref[...]
    group = jnp.minimum(step, (place_ref[0] + G - 1) // G - 1)
    tok_ref, dqkv_ref, gh_ref = (group_rows(ref, group, G * L) for ref in (tok_ref, dqkv_ref, gh_ref))

    @pl.when(step * G >= place_ref[0])
    def _():
        gt_ref[...] = jnp.zeros_like(gt_ref)

    @pl.when(step * G < place_ref[0])
    def _():
        half = G * L // 2
        parts = [pl.ds(i * half, half) for i in range(2)]
        products = [nt(dqkv_ref[rows, :], w_ref[...]) for rows in parts]
        for i, rows in enumerate(parts):
            x = tok_ref[rows, :].astype(f32)
            scale = inverse_rms(x)
            xs = x * scale
            g = products[i] * gains_ref[0:1, :]
            dot = jnp.mean(g * xs, axis=-1, keepdims=True)
            gt = gh_ref[rows, :].astype(f32) + scale * (g - xs * dot)
            gt_ref[pl.ds(i * G // 2, G // 2)] = gt.astype(bf16).reshape(G // 2, L, D)


def call_token_gradient(place, tokens, dqkv, gh, w, gains, S, L, D):
    G = GROUP
    operands = (tokens, dqkv, gh, w, gains)
    return pl.pallas_call(
        functools.partial(token_gradient, G, L),
        out_shape=(pltpu.HBM((S, L, D), bf16), sds(gains.shape, f32)),
        grid_spec=pltpu.PrefetchScalarGridSpec(
            num_scalar_prefetch=1,
            grid=(S // G,),
            in_specs=[whole(a.shape) for a in operands],
            out_specs=(series_spec(G, (S, L, D), True), whole(gains.shape)),
        ),
        compiler_params=params(MIB_TOKENS),
        cost_estimate=cost(S * L, D * 3 * INNER * 2, S * L * 5000),
        name="token_gradient",
    )(place, *operands)


def finish(n_f, place_ref, *refs):
    packs = [refs[2 * i : 2 * i + 2] for i in range(3)]
    gq, gk, gv, go, gg, gu, gd, ga, gf, gb = refs[7:]
    core = place_ref[1]
    ds, is_, fh = gq.shape[0], go.shape[0], gd.shape[0] // 2
    half = go.shape[1] // 2

    def halves(pack):
        here, there = pack[0][...].astype(f32), pack[1][...].astype(f32)
        return jnp.where(core == 0, here, there), jnp.where(core == 0, there, here)

    one, two = halves(packs[2])
    gq[...] = one[:, :INNER]
    gk[...] = jnp.concatenate([one[:, INNER:CUT], two[:, : 2 * INNER - CUT]], axis=1)
    gv[...] = two[:, 2 * INNER - CUT : 3 * INNER - CUT]
    small = jnp.transpose(two[:, 3 * INNER - CUT :])
    ga[...] = small[0]
    gf[...] = small[1]
    gb[...] = small[2, : BUCKETS // n_f * HEADS]
    chunks = [halves(packs[0]), halves(packs[1])]
    for which, ref in enumerate((gg, gu)):
        wide = [jnp.concatenate([c[which][:ds], c[which][ds : 2 * ds]], axis=1) for c in chunks]
        width = wide[0].shape[1] // n_f
        ref[...] = jnp.concatenate(
            [w[:, f * width : (f + 1) * width] for f in range(n_f) for w in wide], axis=1
        )
    for chunk, pair in enumerate(chunks):
        for which in range(2):
            gd[chunk * fh : (chunk + 1) * fh, which * half : (which + 1) * half] = pair[which][2 * ds : 2 * ds + fh]
    for which in range(2):
        go[:, which * half : (which + 1) * half] = chunks[1][which][2 * ds + fh : 2 * ds + fh + is_]


def call_finish(place, n_f, packs, shapes, after):
    vm, sm = pl.BlockSpec(memory_space=pltpu.VMEM), pl.BlockSpec(memory_space=pltpu.SMEM)
    flat = [piece for pack in packs for piece in pack]
    return pl.pallas_call(
        functools.partial(finish, n_f),
        out_shape=tuple(sds(shape, f32) for shape in shapes),
        in_specs=[sm] + [vm] * len(flat) + [vm],
        out_specs=[vm] * len(shapes),
        compiler_params=small_params(),
        name="finish",
    )(place, *flat, after)


def solution(mesh):
    n_r, n_f = mesh.shape["rep"], mesh.shape["fsdp"]
    n_z = n_f // 2

    def over_fsdp(value, distance):
        return lax.ppermute(value, "fsdp", [(i, i ^ distance) for i in range(n_f)])

    def over_rep(value, distance):
        return lax.ppermute(value, "rep", [(i, i ^ distance) for i in range(n_r)])

    def along_z(pack):
        return [pack] + [over_fsdp(pack, 2 * k) for k in range(1, n_z)]

    def halved(keep, got):
        away = (keep[1].astype(f32) + got[1].astype(f32)).astype(bf16)
        return keep[0].astype(f32) + got[0].astype(f32), away

    def joined(here, got):
        here = here + got.astype(f32)
        return here[0], [here[k].astype(bf16) for k in range(1, n_z)]

    def to_z(pieces):
        return [over_fsdp(piece, 2 * (k + 1)) for k, piece in enumerate(pieces)]

    def summed(own, got):
        for value in got:
            own = own + value.astype(f32)
        return own.astype(bf16)

    def replicas(own, got):
        distance = 2
        while distance < n_r:
            own = (own.astype(f32) + got.astype(f32)).astype(bf16)
            distance *= 2
            got = over_rep(own, distance) if distance < n_r else None
        return own, over_rep(own, 1)

    together = lax.optimization_barrier

    def body(tokens, counts, attn_gain, wq, wk, wv, wo, rel_bias, ffn_gain, wg, wu, wd, cotangent):
        S, L, D = tokens.shape
        r, f = lax.axis_index("rep"), lax.axis_index("fsdp")
        place = in_hbm(jnp.stack([counts[0, 0], r % 2, f % 2, f // 2]).astype(jnp.int32))
        pack_a = call_prepare_attention(place, n_f, attn_gain, wq, wk, wv, rel_bias, ffn_gain)
        pack_0, pack_1 = call_prepare_ffn(place, n_f, wo, wg, wu, wd)

        z_0 = along_z(pack_0)
        z_a, pack_1 = together((along_z(pack_a), pack_1))
        near_a = jnp.stack(z_a)
        far_a, near_ac = over_fsdp(near_a, 1), over_rep(near_a, 1)
        tokens, cotangent, done = call_keep_close(place, tokens, cotangent)
        done, far_a, near_ac, z_0, pack_1 = together((done, far_a, near_ac, z_0, pack_1))
        far_ac, near_0 = over_rep(far_a, 1), jnp.stack(z_0)
        far_ac, near_0 = together((far_ac, near_0))

        far_0, near_0c, z_1 = over_fsdp(near_0, 1), over_rep(near_0, 1), along_z(pack_1)
        qkv, probs, mixed, w_all, gains = call_attention_forward(place, tokens, done, (near_a, far_a, near_ac, far_ac), S, L, D)
        gains, far_0, near_0c, z_1 = together((gains, far_0, near_0c, z_1))
        far_0c, near_1 = over_rep(far_0, 1), jnp.stack(z_1)
        far_0c, near_1 = together((far_0c, near_1))

        far_1, near_1c = over_fsdp(near_1, 1), over_rep(near_1, 1)
        hidden, act_0, gpart, wd_0, wo_all, keep_0, send_0 = call_ffn_half(
            0, place, n_z, (near_0, far_0, near_0c, far_0c, tokens, cotangent, mixed, gains), S, L, D
        )
        wo_all, keep_0, send_0, far_1, near_1c = together((wo_all, keep_0, send_0, far_1, near_1c))

        far_1c, got_0 = over_rep(far_1, 1), over_rep(send_0, 1)
        *running, gf, wd_1, wgu = call_ffn_half(
            1, place, n_z, (near_1, far_1, near_1c, far_1c, hidden, cotangent, gains, wo_all, gpart, mixed), S, L, D
        )
        gf, got_0 = together((gf, got_0))
        here_0, away_0 = halved(keep_0, got_0)
        away_0, gf = together((away_0, gf))
        got_0 = over_fsdp(away_0, 1)
        gh, gm, act_1, _, _, _, gf, keep_1, send_1 = call_ffn_half(
            2, place, n_z, (hidden, cotangent, gains, wo_all, wd_1, wgu, *running, gf), S, L, D
        )
        keep_1, send_1, gf, got_0 = together((keep_1, send_1, gf, got_0))
        own_0, z_0 = joined(here_0, got_0)
        z_0, got_1 = to_z(z_0), over_rep(send_1, 1)
        here_1, away_1 = halved(keep_1, got_1)
        gf, away_1 = together((gf, away_1))
        got_1 = over_fsdp(away_1, 1)
        dqkv, keep_2, send_2 = call_attention_backward(place, n_z, tokens, qkv, probs, gm, w_all, gains, gf, S, L, D)
        keep_2, send_2, z_0, got_1 = together((keep_2, send_2, z_0, got_1))
        sum_0 = summed(own_0, z_0)
        own_1, z_1 = joined(here_1, got_1)

        z_1, got_2 = to_z(z_1), over_rep(send_2, 1)
        here_2, away_2 = halved(keep_2, got_2)
        gains, away_2, sum_0 = together((gains, away_2, sum_0))
        got_2 = over_fsdp(away_2, 1)
        grad_tokens, done = call_token_gradient(place, tokens, dqkv, gh, w_all, gains, S, L, D)
        done, got_2, z_1 = together((done, got_2, z_1))
        sum_1 = summed(own_1, z_1)
        own_2, z_2 = joined(here_2, got_2)
        done, z_2 = together((done, z_2))
        z_2 = to_z(z_2)
        half_out, done = call_layer_result(place, hidden, act_0, act_1, wd_0, wd_1, done, S, L)
        done, z_2 = together((done, z_2))
        sum_2 = summed(own_2, z_2)
        done, sum_2 = together((done, sum_2))
        got = [over_rep(value, 2) for value in (sum_0, sum_1, sum_2)]
        layer_out, done = call_layer_result(place, hidden, act_0, act_1, wd_0, wd_1, done, S, L, half_out)
        done, got = together((done, got))
        gq, gk, gv, go, gg, gu, gd, grad_attn_gain, grad_ffn_gain, grad_bias = call_finish(
            place, n_f, [replicas(own, y) for own, y in zip((sum_0, sum_1, sum_2), got)],
            (wq.shape, wk.shape, wv.shape, wo.shape, wg.shape, wu.shape, wd.shape,
             attn_gain.shape, ffn_gain.shape, rel_bias.shape), done,
        )
        return (layer_out, grad_tokens, grad_attn_gain, gq, gk, gv, go, grad_bias, grad_ffn_gain, gg, gu, gd)

    rows, cols, flat = P(("rep", "fsdp"), None, None), P("fsdp", None), P("fsdp")
    return jax.shard_map(
        body,
        mesh=mesh,
        in_specs=(rows, P("rep", "fsdp"), flat, cols, cols, cols, cols, flat, flat, cols, cols, cols, rows),
        out_specs=(rows, rows, flat, cols, cols, cols, cols, flat, flat, cols, cols, cols),
        check_vma=False,
    )
```

```python
import functools

import jax
import jax.numpy as jnp
from jax import lax
from jax.experimental import pallas as pl
from jax.experimental.pallas import tpu as pltpu
from jax.sharding import PartitionSpec as P

HEADS, HDIM, BUCKETS = 6, 64, 32
INNER = HEADS * HDIM
PAIRS = HEADS // 2
PAIR = 2 * HDIM
CUT = 640
GROUP = 8
EPS = 1e-6
bf16, f32 = jnp.bfloat16, jnp.float32
sds = jax.ShapeDtypeStruct


def in_hbm(value):
    return pltpu.with_memory_space_constraint(value, pltpu.HBM)


def nn(a, b):
    return jnp.dot(a, b, preferred_element_type=f32)


def nt(a, b):
    return lax.dot_general(a, b, (((1,), (1,)), ((), ())), preferred_element_type=f32)


def tn(a, b):
    return lax.dot_general(a, b, (((0,), (0,)), ((), ())), preferred_element_type=f32)


def bucket_edges():
    half = BUCKETS // 2
    exact = half // 2
    power = half - exact
    return [
        min(m for m in range(exact, 129) if m**power * exact**k >= 128**k * exact**power) for k in range(1, power)
    ]


def bucket_table(length):
    half = BUCKETS // 2
    exact = half // 2
    shape = (length, PAIR)
    apart = lax.broadcasted_iota(jnp.int32, shape, 0) - lax.broadcasted_iota(jnp.int32, shape, 1) % HDIM
    distance = jnp.abs(apart)
    bucket = jnp.minimum(distance, exact)
    for edge in bucket_edges():
        bucket = bucket + (distance >= edge).astype(jnp.int32)
    return bucket + jnp.where(apart > 0, half, 0)


def lane_low(shape):
    return lax.broadcasted_iota(jnp.int32, shape, 1) < HDIM


def split_heads(pair):
    low, zero = lane_low(pair.shape), jnp.zeros_like(pair)
    return jnp.concatenate([jnp.where(low, pair, zero), jnp.where(low, zero, pair)], axis=0)


def join_heads(both):
    rows = both.shape[0] // 2
    return jnp.where(lane_low((rows, PAIR)), both[:rows], both[rows:])


def side_by_side(one, two):
    zero = jnp.zeros_like(one)
    return jnp.concatenate([jnp.concatenate([one, zero], axis=1), jnp.concatenate([zero, two], axis=1)], axis=0)


def row_sums(values):
    rows, width = values.shape
    return jnp.sum(values.reshape(rows // 8, 8, width), axis=0)


def inverse_rms(values):
    return lax.rsqrt(jnp.mean(values * values, axis=-1, keepdims=True) + EPS)


class Place:
    def __init__(self, ref, n_z):
        self.count, self.core, self.x, self.z = ref[0], ref[1], ref[2], ref[3]
        self.n_z = n_z

    def shards(self):
        for xx in range(2):
            for k in range(self.n_z):
                yield xx, k, jnp.bitwise_xor(self.z, k) * 2 + jnp.bitwise_xor(self.x, xx)


def at(shard, size):
    return pl.ds(pl.multiple_of(shard * size, size), size)


def interleaved(values, n_f, chunk):
    width = values.shape[1] // n_f // 2
    return jnp.concatenate(
        [values[:, (2 * f + chunk) * width : (2 * f + chunk + 1) * width] for f in range(n_f)], axis=1
    )


def prepare_attention(n_f, bias_ref, wq, wk, wv, ga, gf, a_ref):
    core = lax.rem(lax.axis_index("rep"), 2)
    ds = wq.shape[0]
    joined = jnp.concatenate([wq[...], wk[...], wv[...]], axis=1)
    row = lax.broadcasted_iota(jnp.int32, (ds, PAIR), 0)
    low = lane_low((1, PAIR))
    small = jnp.zeros((ds, PAIR), f32)
    n_b = BUCKETS // n_f
    for b in range(n_b):
        for p in range(PAIRS):
            value = jnp.where(low, bias_ref[b * HEADS + 2 * p], bias_ref[b * HEADS + 2 * p + 1])
            small = jnp.where(row == b * PAIRS + p, value, small)
    for i, gain in enumerate((ga, gf)):
        tiled = jnp.concatenate([gain[...]] * (PAIR // ds), axis=1)
        small = jnp.where(row == n_b * PAIRS + i, tiled, small)

    def write(c):
        if c == 0:
            a_ref[...] = joined[:, :CUT].astype(bf16)
        else:
            a_ref[:, : 3 * INNER - CUT] = joined[:, CUT:].astype(bf16)
            a_ref[:, 3 * INNER - CUT :] = small.astype(bf16)

    for c in range(2):
        pl.when(core == c)(functools.partial(write, c))


def prepare_ffn(n_f, place_ref, wo, wg, wu, wd, p0_ref, p1_ref):
    core = place_ref[1]
    ds, is_, fh = wg.shape[0], wo.shape[0], wd.shape[0] // 2
    half = wo.shape[1] // 2

    def write(c):
        cols = slice(c * half, (c + 1) * half)
        for chunk, ref in enumerate((p0_ref, p1_ref)):
            g = interleaved((wg, wu)[c][...], n_f, chunk).astype(bf16)
            ref[:ds, :] = g[:, :half]
            ref[ds : 2 * ds, :] = g[:, half:]
            ref[2 * ds : 2 * ds + fh, :] = wd[chunk * fh : (chunk + 1) * fh, cols].astype(bf16)
        tail = wo[:, cols]
        pad = p0_ref.shape[0] - (2 * ds + fh + is_)
        if pad:
            tail = jnp.concatenate([tail, jnp.zeros((pad, half), f32)], axis=0)
        p0_ref[2 * ds + fh :, :] = tail.astype(bf16)

    for c in range(2):
        pl.when(core == c)(functools.partial(write, c))


def small_params():
    return pltpu.CompilerParams(vmem_limit_bytes=12 * 1024 * 1024)


def padded(rows):
    return -(-rows // 16) * 16


def call_prepare_attention(n_f, attn_gain, wq, wk, wv, rel_bias, ffn_gain):
    vm, sm = pl.BlockSpec(memory_space=pltpu.VMEM), pl.BlockSpec(memory_space=pltpu.SMEM)
    return pl.pallas_call(
        functools.partial(prepare_attention, n_f),
        out_shape=sds((wq.shape[0], CUT), bf16),
        in_specs=[sm] + [vm] * 5,
        out_specs=vm,
        name="prepare_attention",
    )(rel_bias, wq, wk, wv, attn_gain.reshape(1, -1), ffn_gain.reshape(1, -1))


def call_prepare_ffn(place, n_f, wo, wg, wu, wd):
    ds, fh, half = wg.shape[0], wd.shape[0] // 2, wo.shape[1] // 2
    vm, sm = pl.BlockSpec(memory_space=pltpu.VMEM), pl.BlockSpec(memory_space=pltpu.SMEM)
    return pl.pallas_call(
        functools.partial(prepare_ffn, n_f),
        out_shape=(sds((2 * ds + fh + padded(wo.shape[0]), half), bf16), sds((2 * ds + fh, half), bf16)),
        in_specs=[sm] + [vm] * 4,
        out_specs=[vm] * 2,
        name="prepare_ffn",
    )(place, wo, wg, wu, wd)


def keep_close(G, L, place_ref, tok_ref, ct_ref, tok_out, ct_out, done_ref):
    step = pl.program_id(0)
    R, D = G * L, tok_ref.shape[-1]
    live = (step * G + lax.broadcasted_iota(jnp.int32, (R, 1), 0) // L) < place_ref[0]
    group_rows(tok_out, step, R)[...] = tok_ref[...].reshape(R, D)
    group_rows(ct_out, step, R)[...] = jnp.where(live, ct_ref[...].reshape(R, D), jnp.zeros((), bf16))
    done_ref[...] = jnp.zeros_like(done_ref)


def call_keep_close(place, tokens, ct):
    S, L, D = tokens.shape
    G = GROUP
    block = pl.BlockSpec((G, L, D), lambda i, c: (i, 0, 0))
    return pl.pallas_call(
        functools.partial(keep_close, G, L),
        out_shape=(sds((S * L, D), bf16), sds((S * L, D), bf16), sds((8, PAIR), f32)),
        grid_spec=pltpu.PrefetchScalarGridSpec(
            num_scalar_prefetch=1, grid=(S // G,), in_specs=[block, block], out_specs=[whole(None)] * 3
        ),
        compiler_params=params(MIB_TOKENS),
        cost_estimate=cost(S * L, 1, 8 * S * L * D),
        name="keep_close",
    )(place, in_hbm(tokens), in_hbm(ct))


def attention_forward(G, L, n_z, place_ref, tok_ref, after_ref, *refs):
    pieces, refs = refs[:4], refs[4:]
    all_qkv, all_probs, mixed_ref, w_ref, gains_ref, table_ref, st_ref, small_ref = refs
    step = pl.program_id(0)
    place = Place(place_ref, n_z)
    D = tok_ref.shape[-1]
    n_f = 2 * n_z
    ds = D // n_f
    rest = 3 * INNER - CUT

    def assemble(c):
        for xx, k, f in place.shards():
            one, two = pieces[xx].at[k], pieces[2 + xx].at[k]
            one, two = (one, two) if c == 0 else (two, one)
            w_ref[at(f, ds), :CUT] = one[...]
            w_ref[at(f, ds), CUT:] = two[:, :rest]
            small_ref[at(f, ds), :] = two[:, rest:].astype(f32)

    @pl.when(step == 0)
    def _():
        for c in range(2):
            pl.when(place.core == c)(functools.partial(assemble, c))
        n_b = BUCKETS // n_f
        ids = bucket_table(L)
        for p in range(PAIRS):
            total = jnp.zeros(ids.shape, f32)
            for b in range(BUCKETS):
                row = b // n_b * ds + (b % n_b) * PAIRS + p
                total = jnp.where(ids == b, small_ref[row : row + 1, :], total)
            table_ref[p] = total
        per = PAIR // ds
        lane = lax.broadcasted_iota(jnp.int32, (1, PAIR), 1) // ds
        gains_ref[...] = jnp.zeros_like(gains_ref)
        for i in range(2):
            for v in range(D // PAIR):
                total = jnp.zeros((1, PAIR), f32)
                for f in range(per):
                    row = (v * per + f) * ds + n_b * PAIRS + i
                    total = jnp.where(lane == f, small_ref[row : row + 1, :], total)
                gains_ref[i : i + 1, v * PAIR : (v + 1) * PAIR] = total

    @pl.when(step * G < place.count)
    def _():
        mixed, qkv_ref = group_rows(mixed_ref, step, G * L), group_rows(all_qkv, step, G * L)
        probs_ref = all_probs.at[pl.ds(step * G, G)]
        x = group_rows(tok_ref, step, G * L)[...].astype(f32)
        normed = (x * inverse_rms(x) * gains_ref[0:1, :]).astype(bf16)
        qkv_ref[...] = nn(normed, w_ref[...]).astype(bf16)
        for s in range(0, G, 2):
            for p in range(PAIRS):
                q, k = (
                    [qkv_ref[pl.ds((s + i) * L, L), pl.ds(b * INNER + p * PAIR, PAIR)] for i in range(2)] for b in range(2)
                )
                st = nt(jnp.concatenate(k, axis=1), side_by_side(split_heads(q[0]), split_heads(q[1])))
                st_ref[s, p], st_ref[s + 1, p] = st[:, :PAIR], st[:, PAIR:]
        for s in range(G):
            for p in range(PAIRS):
                st = st_ref[s, p] + table_ref[p]
                e = jnp.exp(st - jnp.max(st, axis=0, keepdims=True))
                probs_ref[s, p] = (e * (1.0 / jnp.sum(e, axis=0, keepdims=True))).astype(bf16)
        for s in range(G):
            rows = pl.ds(s * L, L)
            for p in range(PAIRS):
                v = qkv_ref[rows, pl.ds(2 * INNER + p * PAIR, PAIR)]
                mixed[rows, pl.ds(p * PAIR, PAIR)] = join_heads(tn(probs_ref[s, p], v)).astype(bf16)


MIB_FORWARD, MIB_FFN, MIB_BACKWARD, MIB_TOKENS, MIB_RESULT = 8, 14, 10, 6, 6


def params(mib):
    return pltpu.CompilerParams(dimension_semantics=("arbitrary",), vmem_limit_bytes=mib * 1024 * 1024)


def whole(shape):
    return pl.BlockSpec(memory_space=pltpu.VMEM)


def live_group(i, place, G):
    return jnp.minimum(i, jnp.maximum((place[0] + G - 1) // G - 1, 0))


def series_spec(G, shape, every=False):
    tail = (0,) * (len(shape) - 1)
    return pl.BlockSpec((G,) + shape[1:], lambda i, c: ((i if every else live_group(i, c, G)),) + tail)


def row_spec(G, L, width):
    return pl.BlockSpec((G * L, width), lambda i, c: (live_group(i, c, G), 0))


def group_rows(ref, step, rows):
    return ref.at[pl.ds(pl.multiple_of(step * rows, rows), rows), :]


def cost(rows, per_row, nbytes, exps=0):
    return pl.CostEstimate(flops=2 * rows * per_row, bytes_accessed=nbytes, transcendentals=exps)


def call_attention_forward(place, tokens, after, pieces, S, L, D):
    G, n_z = GROUP, pieces[0].shape[0]
    return pl.pallas_call(
        functools.partial(attention_forward, G, L, n_z),
        out_shape=(
            sds((S * L, 3 * INNER), bf16),
            sds((S, PAIRS, L, PAIR), bf16),
            sds((S * L, INNER), bf16),
            sds((D, 3 * INNER), bf16),
            sds((8, D), f32),
        ),
        grid_spec=pltpu.PrefetchScalarGridSpec(
            num_scalar_prefetch=1,
            grid=(S // G,),
            in_specs=[whole(tokens.shape), whole(after.shape)] + [whole(piece.shape) for piece in pieces],
            out_specs=[
                whole((S * L, 3 * INNER)),
                whole((S, PAIRS, L, PAIR)),
                whole((S * L, INNER)),
                whole((D, 3 * INNER)),
                whole((8, D)),
            ],
            scratch_shapes=[
                pltpu.VMEM((PAIRS, L, PAIR), f32),
                pltpu.VMEM((G, PAIRS, L, PAIR), f32),
                pltpu.VMEM((D, PAIR), f32),
            ],
        ),
        compiler_params=params(MIB_FORWARD),
        cost_estimate=cost(S * L, D * 3 * INNER * 4, S * L * 5000),
        name="attention_forward",
    )(place, tokens, after, *pieces)


def gelu_parts(v):
    c = 0.7978845608028654
    v2 = v * v
    t = jnp.tanh(v * (c + (c * 0.044715) * v2))
    half = 0.5 + 0.5 * t
    return v * half, half + (0.5 * v) * (1.0 - t * t) * (c + (3 * c * 0.044715) * v2)


def put_weights(place, pieces, wgu, wd, wo=None):
    FW, D = wd.shape

    def assemble(c):
        for f, here, there in pieces:
            for which, piece in enumerate((here, there) if c == 0 else (there, here)):
                n_f = len(pieces)
                ds, fh, half, is_ = D // n_f, FW // n_f, FW // 2, INNER // n_f
                for part in range(2):
                    start = (2 * part + which) * half
                    wgu[at(f, ds), start : start + half] = piece[part * ds : (part + 1) * ds, :]
                cols = slice(which * half, (which + 1) * half)
                wd[at(f, fh), cols] = piece[2 * ds : 2 * ds + fh, :]
                if wo is None:
                    continue
                if is_ % 16 == 0:
                    wo[at(f, is_), cols] = piece[2 * ds + fh : 2 * ds + fh + is_, :]
                else:
                    wo[f, :, cols] = piece[2 * ds + fh :, :]

    for c in range(2):
        pl.when(place.core == c)(functools.partial(assemble, c))


def put_grads(place, n_z, keep, send, agu, ad, ao=None):
    n_f = 2 * n_z
    FW, D = ad.shape
    ds, fh, half = D // n_f, FW // n_f, FW // 2

    def write(c):
        for xx, k, f in place.shards():
            for which, ref in enumerate((keep, send) if c == 0 else (send, keep)):
                for part in range(2):
                    start = (2 * part + which) * half
                    ref[xx, k, part * ds : (part + 1) * ds, :] = agu[at(f, ds), start : start + half].astype(bf16)
                cols = slice(which * half, (which + 1) * half)
                ref[xx, k, 2 * ds : 2 * ds + fh, :] = ad[at(f, fh), cols].astype(bf16)
                if ao is not None:
                    is_ = INNER // n_f
                    if is_ % 16 == 0:
                        ref[xx, k, 2 * ds + fh :, :] = ao[at(f, is_), cols].astype(bf16)
                    else:
                        ref[xx, k, 2 * ds + fh :, :] = ao[f, :, cols].astype(bf16)

    for c in range(2):
        pl.when(place.core == c)(functools.partial(write, c))


def ffn_half(G, L, n_z, stage, shift, place_ref, *refs):
    n_f = 2 * n_z
    place = Place(place_ref, n_z)
    first, begins, ends = stage == 0, stage < 2, stage != 1
    if first:
        (near, own_far, far, near_c, own_far_c, far_c), refs = refs[:6], refs[6:]
        here, there = ([near.at[k] for k in range(n_z)] for near in (near, near_c))
        here, there = (
            side + [own] + [rest.at[k] for k in range(n_z - 1)]
            for side, own, rest in ((here, own_far, far), (there, own_far_c, far_c))
        )
        pieces = [(f, *pair) for (_, _, f), pair in zip(place.shards(), zip(here, there))]
    elif begins:
        pieces, refs = refs[:4], refs[4:]
        pieces = [(f, pieces[xx].at[k], pieces[2 + xx].at[k]) for xx, k, f in place.shards()]
    if stage == 0:
        (tok_ref, ct_ref, mixed_ref, gains_ref,
         hid_ref, act_ref, gpart_ref, wd, wo_out, keep, send,
         agu, ad, wgu, n2, n2_next, gu, ga, low, gn, spread) = refs
    elif stage == 1:
        hid_ref, ct_ref, gains_ref, wo_in, _, _ = refs[:6]
        gpart_ref, mixed_ref, act_ref, agu, ad, ao, gf_ref, wd, wgu, n2, n2_next, gu, ga, low, gn = refs[6:]
    else:
        hid_ref, ct_ref, gains_ref, wo_in, wd, wgu = refs[:6]
        gpart_ref, mixed_ref, act_ref, agu, ad, ao, gf_ref, keep, send, n2, n2_next, gu, ga, low, gn, spread = refs[13:]
    step = pl.program_id(0) + shift
    R = G * L
    FW, D = wd.shape
    CH = FW // 2
    is_ = INNER // n_f
    count = place.count
    group = jnp.minimum(step, (count + G - 1) // G - 1)

    def normalise(group, into):
        if first:
            h = group_rows(tok_ref, group, R)[...].astype(f32) + nn(group_rows(mixed_ref, group, R)[...], wo_out[...])
            group_rows(hid_ref, group, R)[...] = h.astype(bf16)
        else:
            h = group_rows(hid_ref, group, R)[...].astype(f32)
        into[...] = (h * inverse_rms(h) * gains_ref[1:2, :]).astype(bf16)

    if begins:

        @pl.when(step == 0)
        def _():
            wo = (wo_out if is_ % 16 == 0 else spread) if first else None
            put_weights(place, pieces, wgu, wd, wo)
            if first and is_ % 16:
                wo_out[...] = jnp.concatenate([spread[f, :is_, :].astype(f32) for f in range(n_f)], axis=0).astype(bf16)
            for ref in (agu, ad) if first else (agu, ad, ao, gf_ref):
                ref[...] = jnp.zeros_like(ref)

    @pl.when(step * G < count)
    def _():
        normalise(group, n2)
        gb, act, gpart, hid = (group_rows(ref, group, R) for ref in (ct_ref, act_ref, gpart_ref, hid_ref))
        for c in range(2):
            cols, both = pl.ds(c * CH, CH), pl.ds(2 * c * CH, 2 * CH)
            gu[c] = nn(n2[...], wgu[:, both])
            ga[c] = nt(gb[...], wd[cols, :])
        for c in range(2):
            cols, both = pl.ds(c * CH, CH), pl.ds(2 * c * CH, 2 * CH)
            for r in range(0, R, L):
                rows = pl.ds(r, L)
                u = gu[c, rows, CH:]
                a = ga[c, rows, :]
                g, dg = gelu_parts(gu[c, rows, :CH])
                act[rows, cols] = (g * u).astype(bf16)
                low[c, rows, :CH] = (a * u * dg).astype(bf16)
                low[c, rows, CH:] = (a * g).astype(bf16)
            if c == 0:
                gn[...] = nt(low[c], wgu[:, both])
            else:
                gn[...] += nt(low[c], wgu[:, both])
            ad[cols, :] += tn(act[:, cols], gb[...])
            agu[:, both] += tn(n2[...], low[c])
        if first:
            gpart[...] = gn[...].astype(bf16)
        else:
            mixed = group_rows(mixed_ref, group, R)
            h = hid[...].astype(f32)
            scale = inverse_rms(h)
            hs = h * scale
            g2 = gn[...] + gpart[...].astype(f32)
            gf_ref[...] += row_sums(g2 * hs)
            g2 = g2 * gains_ref[1:2, :]
            dot = jnp.mean(g2 * hs, axis=-1, keepdims=True)
            gh = (gb[...].astype(f32) + scale * (g2 - hs * dot)).astype(bf16)
            gpart[...] = gh
            ao[...] += tn(mixed[...], gh)
            mixed[...] = nt(gh, wo_in[...]).astype(bf16)

    if ends:

        @pl.when(pl.program_id(0) == pl.num_programs(0) - 1)
        def _():
            if first:
                put_grads(place, n_z, keep, send, agu, ad)
            elif is_ % 16 == 0:
                put_grads(place, n_z, keep, send, agu, ad, ao)
            else:
                for f in range(n_f):
                    spread[f, :is_, :] = ao[f * is_ : (f + 1) * is_, :]
                put_grads(place, n_z, keep, send, agu, ad, spread)


def call_ffn_half(stage, place, n_z, operands, S, L, D):
    G = GROUP
    R, n_f = G * L, 2 * n_z
    FW = D
    CH = FW // 2
    ds, fh, is_ = D // n_f, FW // n_f, INNER // n_f
    pack = (2, n_z, 2 * ds + fh + (padded(is_) if stage else 0), CH)
    packs, act = [sds(pack, bf16)] * 2, sds((S * L, FW), bf16)
    wd, wgu, rows = sds((FW, D), bf16), sds((D, 2 * FW), bf16), sds((S * L, D), bf16)
    agu, ad = sds((D, 2 * FW), f32), sds((FW, D), f32)
    running = [rows, sds((S * L, INNER), bf16), act, agu, ad, sds((INNER, D), f32), sds((8, D), f32)]
    vm = pltpu.VMEM
    work = [
        vm((R, D), bf16), vm((R, D), bf16),
        vm((2, R, 2 * CH), f32), vm((2, R, CH), f32), vm((2, R, 2 * CH), bf16), vm((R, D), f32),
    ]
    spread = [vm((n_f, padded(is_), D) if is_ % 16 else (1, 16, 128), f32 if stage else bf16)]
    half = S // G // 2
    steps, shift = ((S // G, 0), (half, 0), (S // G - half, half))[stage]
    if stage == 0:
        out_shape = [rows, act, rows, wd, sds((INNER, D), bf16)] + packs
        scratch = [vm(agu.shape, f32), vm(ad.shape, f32), vm(wgu.shape, bf16)] + work + spread
        aliases = {}
    elif stage == 1:
        out_shape, scratch = running + [wd, wgu], work
        aliases = {9: 0, 10: 1}
    else:
        out_shape, scratch = running + packs, work + spread
        aliases = {7 + i: i for i in range(7)}
    return pl.pallas_call(
        functools.partial(ffn_half, G, L, n_z, stage, shift),
        out_shape=tuple(out_shape),
        grid_spec=pltpu.PrefetchScalarGridSpec(
            num_scalar_prefetch=1,
            grid=(steps,),
            in_specs=[whole(a.shape) for a in operands],
            out_specs=[whole(shape.shape) for shape in out_shape],
            scratch_shapes=scratch,
        ),
        input_output_aliases=aliases,
        compiler_params=params(MIB_FFN),
        cost_estimate=cost(steps * R, 9 * D * FW, S * L * 9000),
        name=("ffn_first", "ffn_second", "ffn_third")[stage],
    )(place, *operands)


def layer_result(G, L, shift, place_ref, hid_ref, act_0, act_1, wd_0, wd_1, gains_ref, *refs):
    out_ref, done_ref = refs[-2:]
    step = pl.program_id(0) + shift
    count = place_ref[0]
    R = G * L
    D = hid_ref.shape[-1]
    done_ref[...] = gains_ref[...]
    group = jnp.minimum(step, (count + G - 1) // G - 1)
    hid_ref, act_0, act_1 = (group_rows(ref, group, R) for ref in (hid_ref, act_0, act_1))

    @pl.when(step * G >= count)
    def _():
        out_ref[...] = jnp.zeros_like(out_ref)

    @pl.when(step * G < count)
    def _():
        live = (step * G + lax.broadcasted_iota(jnp.int32, (R, 1), 0) // L) < count
        out = hid_ref[...].astype(f32) + nn(act_0[...], wd_0[...]) + nn(act_1[...], wd_1[...])
        out_ref[...] = jnp.where(live, out, 0.0).astype(bf16).reshape(G, L, D)


def call_layer_result(place, hidden, act_0, act_1, wd_0, wd_1, gains, S, L, earlier=None):
    G, D = GROUP, hidden.shape[-1]
    operands = (hidden, act_0, act_1, wd_0, wd_1, gains)
    half = S // G // 2
    steps, shift = (half, 0) if earlier is None else (S // G - half, half)
    more = () if earlier is None else (earlier,)
    return pl.pallas_call(
        functools.partial(layer_result, G, L, shift),
        out_shape=(pltpu.HBM((S, L, D), bf16), sds(gains.shape, f32)),
        grid_spec=pltpu.PrefetchScalarGridSpec(
            num_scalar_prefetch=1,
            grid=(steps,),
            in_specs=[whole(a.shape) for a in operands] + [pl.BlockSpec(memory_space=pl.ANY)] * len(more),
            out_specs=(pl.BlockSpec((G, L, D), lambda i, c: (i + shift, 0, 0)), whole(gains.shape)),
        ),
        input_output_aliases={7: 0} if more else {},
        compiler_params=params(MIB_RESULT),
        cost_estimate=cost(S * L // 2, 2 * D * act_0.shape[-1], S * L * 3000),
        name="layer_result",
    )(place, *operands, *more)


def attention_backward(G, L, n_z, place_ref, tok_ref, _, probs_ref, gm_ref, w_ref, gains_ref, gf_ref,
                       dqkv, keep, send, aw, ab, dp_ref, ds_ref, small):
    step = pl.program_id(0)
    last = pl.num_programs(0) - 1
    R = G * L
    D = tok_ref.shape[-1]
    place = Place(place_ref, n_z)
    count = place.count
    group = jnp.minimum(step, (count + G - 1) // G - 1)
    probs_ref = probs_ref.at[pl.ds(group * G, G)]
    gm_ref, dqkv = group_rows(gm_ref, group, R), group_rows(dqkv, group, R)

    @pl.when(step == 0)
    def _():
        for ref in (aw, ab):
            ref[...] = jnp.zeros_like(ref)

    @pl.when(step * G < count)
    def _():
        cols = [[pl.ds(b * INNER + p * PAIR, PAIR) for b in range(3)] for p in range(PAIRS)]
        for s in range(G):
            for p in range(PAIRS):
                rows = pl.ds(s * L, L)
                dm = split_heads(gm_ref[rows, pl.ds(p * PAIR, PAIR)])
                dp_ref[s, p] = nt(dqkv[rows, cols[p][2]], dm)
                dqkv[rows, cols[p][2]] = nn(probs_ref[s, p], dm).astype(bf16)
        for p in range(PAIRS):
            total = ab[p]
            for s in range(G):
                prf = probs_ref[s, p].astype(f32)
                dp = dp_ref[s, p]
                ds = prf * (dp - jnp.sum(prf * dp, axis=0, keepdims=True))
                total = total + ds
                ds_ref[s, p] = ds.astype(bf16)
            ab[p] = total
        for s in range(G):
            for p in range(PAIRS):
                rows = pl.ds(s * L, L)
                low = ds_ref[s, p]
                q, k = dqkv[rows, cols[p][0]], dqkv[rows, cols[p][1]]
                dqkv[rows, cols[p][1]] = nn(low, split_heads(q)).astype(bf16)
                dqkv[rows, cols[p][0]] = join_heads(tn(low, k)).astype(bf16)
        x = group_rows(tok_ref, group, R)[...].astype(f32)
        aw[...] += tn((x * inverse_rms(x) * gains_ref[0:1, :]).astype(bf16), dqkv[...])

    @pl.when(step == last)
    def _():
        n_f = 2 * n_z
        ds, n_b, rest = D // n_f, BUCKETS // n_f, 3 * INNER - CUT
        ids = bucket_table(L)
        low = lane_low((1, PAIR))
        small[...] = jnp.zeros_like(small)
        for p in range(PAIRS):
            t = ab[p]
            for b in range(BUCKETS):
                by_lane = jnp.sum(jnp.where(ids == b, t, 0.0), axis=0, keepdims=True)
                one = jnp.sum(jnp.where(low, by_lane, 0.0), axis=1, keepdims=True)
                two = jnp.sum(jnp.where(low, 0.0, by_lane), axis=1, keepdims=True)
                row = b // n_b * ds + (b % n_b) * HEADS + 2 * p
                small[row : row + 1, :] = jnp.broadcast_to(one, (1, PAIR))
                small[row + 1 : row + 2, :] = jnp.broadcast_to(two, (1, PAIR))
        gain = jnp.transpose(gains_ref[...])[:, 0:1]
        one = jnp.sum(aw[...] * w_ref[...].astype(f32), axis=1, keepdims=True) / gain
        two = jnp.sum(jnp.transpose(gf_ref[...]), axis=1, keepdims=True)
        lane = lax.broadcasted_iota(jnp.int32, (D, PAIR), 1)
        small[...] = jnp.where(lane == 0, one, jnp.where(lane == 1, two, small[...]))

        def write(c):
            for xx, k, f in place.shards():
                one, two = keep.at[xx, k], send.at[xx, k]
                one, two = (one, two) if c == 0 else (two, one)
                one[...] = aw[at(f, ds), :CUT].astype(bf16)
                two[:, :rest] = aw[at(f, ds), CUT:].astype(bf16)
                two[:, rest:] = small[at(f, ds), :].astype(bf16)

        for c in range(2):
            pl.when(place.core == c)(functools.partial(write, c))


def call_attention_backward(place, n_z, tokens, qkv, probs, gm, w, gains, gf, S, L, D):
    G = GROUP
    pack = (2, n_z, D // (2 * n_z), CUT)
    vm = pltpu.VMEM
    return pl.pallas_call(
        functools.partial(attention_backward, G, L, n_z),
        out_shape=(sds((S * L, 3 * INNER), bf16), sds(pack, bf16), sds(pack, bf16)),
        grid_spec=pltpu.PrefetchScalarGridSpec(
            num_scalar_prefetch=1,
            grid=(S // G,),
            in_specs=[whole(tokens.shape), whole(qkv.shape), whole(probs.shape),
                      whole(gm.shape), whole(w.shape), whole(gains.shape), whole(gf.shape)],
            out_specs=[whole(pack)] * 3,
            scratch_shapes=[
                vm(w.shape, f32), vm((PAIRS, L, PAIR), f32),
                vm((G, PAIRS, L, PAIR), f32), vm((G, PAIRS, L, PAIR), bf16), vm((D, PAIR), f32),
            ],
        ),
        input_output_aliases={2: 0},
        compiler_params=params(MIB_BACKWARD),
        cost_estimate=cost(S * L, D * 3 * INNER * 4, S * L * 6000),
        name="attention_backward",
    )(place, tokens, qkv, probs, gm, w, gains, gf)


def token_gradient(G, L, place_ref, tok_ref, dqkv_ref, gh_ref, w_ref, gains_ref, gt_ref, done_ref):
    step = pl.program_id(0)
    D = tok_ref.shape[-1]
    done_ref[...] = gains_ref[...]
    group = jnp.minimum(step, (place_ref[0] + G - 1) // G - 1)
    tok_ref, dqkv_ref, gh_ref = (group_rows(ref, group, G * L) for ref in (tok_ref, dqkv_ref, gh_ref))

    @pl.when(step * G >= place_ref[0])
    def _():
        gt_ref[...] = jnp.zeros_like(gt_ref)

    @pl.when(step * G < place_ref[0])
    def _():
        half = G * L // 2
        parts = [pl.ds(i * half, half) for i in range(2)]
        products = [nt(dqkv_ref[rows, :], w_ref[...]) for rows in parts]
        for i, rows in enumerate(parts):
            x = tok_ref[rows, :].astype(f32)
            scale = inverse_rms(x)
            xs = x * scale
            g = products[i] * gains_ref[0:1, :]
            dot = jnp.mean(g * xs, axis=-1, keepdims=True)
            gt = gh_ref[rows, :].astype(f32) + scale * (g - xs * dot)
            gt_ref[pl.ds(i * G // 2, G // 2)] = gt.astype(bf16).reshape(G // 2, L, D)


def call_token_gradient(place, tokens, dqkv, gh, w, gains, S, L, D):
    G = GROUP
    operands = (tokens, dqkv, gh, w, gains)
    return pl.pallas_call(
        functools.partial(token_gradient, G, L),
        out_shape=(pltpu.HBM((S, L, D), bf16), sds(gains.shape, f32)),
        grid_spec=pltpu.PrefetchScalarGridSpec(
            num_scalar_prefetch=1,
            grid=(S // G,),
            in_specs=[whole(a.shape) for a in operands],
            out_specs=(series_spec(G, (S, L, D), True), whole(gains.shape)),
        ),
        compiler_params=params(MIB_TOKENS),
        cost_estimate=cost(S * L, D * 3 * INNER * 2, S * L * 5000),
        name="token_gradient",
    )(place, *operands)


def finish(n_f, place_ref, *refs):
    packs = [refs[2 * i : 2 * i + 2] for i in range(3)]
    gq, gk, gv, go, gg, gu, gd, ga, gf, gb = refs[7:]
    core = place_ref[1]
    ds, is_, fh = gq.shape[0], go.shape[0], gd.shape[0] // 2
    half = go.shape[1] // 2

    def halves(pack):
        here, there = pack[0][...].astype(f32), pack[1][...].astype(f32)
        return jnp.where(core == 0, here, there), jnp.where(core == 0, there, here)

    one, two = halves(packs[2])
    gq[...] = one[:, :INNER]
    gk[...] = jnp.concatenate([one[:, INNER:CUT], two[:, : 2 * INNER - CUT]], axis=1)
    gv[...] = two[:, 2 * INNER - CUT : 3 * INNER - CUT]
    small = jnp.transpose(two[:, 3 * INNER - CUT :])
    ga[...] = small[0]
    gf[...] = small[1]
    gb[...] = small[2, : BUCKETS // n_f * HEADS]
    chunks = [halves(packs[0]), halves(packs[1])]
    for which, ref in enumerate((gg, gu)):
        wide = [jnp.concatenate([c[which][:ds], c[which][ds : 2 * ds]], axis=1) for c in chunks]
        width = wide[0].shape[1] // n_f
        ref[...] = jnp.concatenate(
            [w[:, f * width : (f + 1) * width] for f in range(n_f) for w in wide], axis=1
        )
    for chunk, pair in enumerate(chunks):
        for which in range(2):
            gd[chunk * fh : (chunk + 1) * fh, which * half : (which + 1) * half] = pair[which][2 * ds : 2 * ds + fh]
    for which in range(2):
        go[:, which * half : (which + 1) * half] = chunks[1][which][2 * ds + fh : 2 * ds + fh + is_]


def call_finish(place, n_f, packs, shapes, after):
    vm, sm = pl.BlockSpec(memory_space=pltpu.VMEM), pl.BlockSpec(memory_space=pltpu.SMEM)
    flat = [piece for pack in packs for piece in pack]
    return pl.pallas_call(
        functools.partial(finish, n_f),
        out_shape=tuple(sds(shape, f32) for shape in shapes),
        in_specs=[sm] + [vm] * len(flat) + [vm],
        out_specs=[vm] * len(shapes),
        compiler_params=small_params(),
        name="finish",
    )(place, *flat, after)


def solution(mesh):
    n_r, n_f = mesh.shape["rep"], mesh.shape["fsdp"]
    n_z = n_f // 2

    def over_fsdp(value, distance):
        return lax.ppermute(value, "fsdp", [(i, i ^ distance) for i in range(n_f)])

    def over_rep(value, distance):
        return lax.ppermute(value, "rep", [(i, i ^ distance) for i in range(n_r)])

    def along_z(pack):
        return [pack] + [over_fsdp(pack, 2 * k) for k in range(1, n_z)]

    def halved(keep, got):
        away = (keep[1].astype(f32) + got[1].astype(f32)).astype(bf16)
        return keep[0].astype(f32) + got[0].astype(f32), away

    def joined(here, got):
        here = here + got.astype(f32)
        return here[0], [here[k].astype(bf16) for k in range(1, n_z)]

    def to_z(pieces):
        return [over_fsdp(piece, 2 * (k + 1)) for k, piece in enumerate(pieces)]

    def summed(own, got):
        for value in got:
            own = own + value.astype(f32)
        return own.astype(bf16)

    def replicas(own, got):
        distance = 2
        while distance < n_r:
            own = (own.astype(f32) + got.astype(f32)).astype(bf16)
            distance *= 2
            got = over_rep(own, distance) if distance < n_r else None
        return own, over_rep(own, 1)

    together = lax.optimization_barrier

    def body(tokens, counts, attn_gain, wq, wk, wv, wo, rel_bias, ffn_gain, wg, wu, wd, cotangent):
        S, L, D = tokens.shape
        r, f = lax.axis_index("rep"), lax.axis_index("fsdp")
        place = in_hbm(jnp.stack([counts[0, 0], r % 2, f % 2, f // 2]).astype(jnp.int32))
        pack_a = call_prepare_attention(n_f, attn_gain, wq, wk, wv, rel_bias, ffn_gain)
        pack_0, pack_1 = call_prepare_ffn(place, n_f, wo, wg, wu, wd)

        z_0 = along_z(pack_0)
        z_a, pack_1 = together((along_z(pack_a), pack_1))
        near_a = jnp.stack(z_a)
        far_a, own_far_0 = over_fsdp(near_a, 1), over_fsdp(pack_0, 1)
        tokens, cotangent, done = call_keep_close(place, tokens, cotangent)
        done, far_a, own_far_0, z_0, pack_1 = together((done, far_a, own_far_0, z_0, pack_1))
        near_ac, far_ac, near_0 = over_rep(near_a, 1), over_rep(far_a, 1), jnp.stack(z_0)
        far_ac, near_0 = together((far_ac, near_0))

        far_0, near_0c, z_1 = over_fsdp(near_0[1:], 1), over_rep(near_0, 1), along_z(pack_1)
        qkv, probs, mixed, w_all, gains = call_attention_forward(place, tokens, done, (near_a, far_a, near_ac, far_ac), S, L, D)
        gains, far_0, near_0c, own_far_0, z_1 = together((gains, far_0, near_0c, own_far_0, z_1))
        own_far_0c, far_0c, near_1 = over_rep(own_far_0, 1), over_rep(far_0, 1), jnp.stack(z_1)
        far_0c, near_1 = together((far_0c, near_1))

        far_1, near_1c = over_fsdp(near_1, 1), over_rep(near_1, 1)
        hidden, act_0, gpart, wd_0, wo_all, keep_0, send_0 = call_ffn_half(
            0, place, n_z, (near_0, own_far_0, far_0, near_0c, own_far_0c, far_0c, tokens, cotangent, mixed, gains), S, L, D
        )
        wo_all, keep_0, send_0, far_1, near_1c = together((wo_all, keep_0, send_0, far_1, near_1c))

        far_1c, got_0 = over_rep(far_1, 1), over_rep(send_0, 1)
        *running, gf, wd_1, wgu = call_ffn_half(
            1, place, n_z, (near_1, far_1, near_1c, far_1c, hidden, cotangent, gains, wo_all, gpart, mixed), S, L, D
        )
        gf, got_0 = together((gf, got_0))
        here_0, away_0 = halved(keep_0, got_0)
        away_0, gf = together((away_0, gf))
        got_0 = over_fsdp(away_0, 1)
        gh, gm, act_1, _, _, _, gf, keep_1, send_1 = call_ffn_half(
            2, place, n_z, (hidden, cotangent, gains, wo_all, wd_1, wgu, *running, gf), S, L, D
        )
        keep_1, send_1, gf, got_0 = together((keep_1, send_1, gf, got_0))
        own_0, z_0 = joined(here_0, got_0)
        z_0, got_1 = to_z(z_0), over_rep(send_1, 1)
        here_1, away_1 = halved(keep_1, got_1)
        gf, away_1 = together((gf, away_1))
        got_1 = over_fsdp(away_1, 1)
        dqkv, keep_2, send_2 = call_attention_backward(place, n_z, tokens, qkv, probs, gm, w_all, gains, gf, S, L, D)
        keep_2, send_2, z_0, got_1 = together((keep_2, send_2, z_0, got_1))
        sum_0 = summed(own_0, z_0)
        own_1, z_1 = joined(here_1, got_1)

        z_1, got_2 = to_z(z_1), over_rep(send_2, 1)
        here_2, away_2 = halved(keep_2, got_2)
        gains, away_2, sum_0 = together((gains, away_2, sum_0))
        got_2 = over_fsdp(away_2, 1)
        grad_tokens, done = call_token_gradient(place, tokens, dqkv, gh, w_all, gains, S, L, D)
        done, got_2, z_1 = together((done, got_2, z_1))
        sum_1 = summed(own_1, z_1)
        own_2, z_2 = joined(here_2, got_2)
        done, z_2 = together((done, z_2))
        z_2 = to_z(z_2)
        half_out, done = call_layer_result(place, hidden, act_0, act_1, wd_0, wd_1, done, S, L)
        done, z_2 = together((done, z_2))
        sum_2 = summed(own_2, z_2)
        done, sum_2 = together((done, sum_2))
        got = [over_rep(value, 2) for value in (sum_0, sum_1, sum_2)]
        layer_out, done = call_layer_result(place, hidden, act_0, act_1, wd_0, wd_1, done, S, L, half_out)
        done, got = together((done, got))
        gq, gk, gv, go, gg, gu, gd, grad_attn_gain, grad_ffn_gain, grad_bias = call_finish(
            place, n_f, [replicas(own, y) for own, y in zip((sum_0, sum_1, sum_2), got)],
            (wq.shape, wk.shape, wv.shape, wo.shape, wg.shape, wu.shape, wd.shape,
             attn_gain.shape, ffn_gain.shape, rel_bias.shape), done,
        )
        return (layer_out, grad_tokens, grad_attn_gain, gq, gk, gv, go, grad_bias, grad_ffn_gain, gg, gu, gd)

    rows, cols, flat = P(("rep", "fsdp"), None, None), P("fsdp", None), P("fsdp")
    return jax.shard_map(
        body,
        mesh=mesh,
        in_specs=(rows, P("rep", "fsdp"), flat, cols, cols, cols, cols, flat, flat, cols, cols, cols, rows),
        out_specs=(rows, rows, flat, cols, cols, cols, cols, flat, flat, cols, cols, cols),
        check_vma=False,
    )
```

```python
import functools

import jax
import jax.numpy as jnp
from jax import lax
from jax.experimental import pallas as pl
from jax.experimental.pallas import tpu as pltpu
from jax.sharding import PartitionSpec as P

HEADS, HDIM, BUCKETS = 6, 64, 32
INNER = HEADS * HDIM
PAIRS = HEADS // 2
PAIR = 2 * HDIM
CUT = 640
GROUP = 8
EPS = 1e-6
bf16, f32 = jnp.bfloat16, jnp.float32
sds = jax.ShapeDtypeStruct


def in_hbm(value):
    return pltpu.with_memory_space_constraint(value, pltpu.HBM)


def nn(a, b):
    return jnp.dot(a, b, preferred_element_type=f32)


def nt(a, b):
    return lax.dot_general(a, b, (((1,), (1,)), ((), ())), preferred_element_type=f32)


def tn(a, b):
    return lax.dot_general(a, b, (((0,), (0,)), ((), ())), preferred_element_type=f32)


def bucket_edges():
    half = BUCKETS // 2
    exact = half // 2
    power = half - exact
    return [
        min(m for m in range(exact, 129) if m**power * exact**k >= 128**k * exact**power) for k in range(1, power)
    ]


def bucket_table(length):
    half = BUCKETS // 2
    exact = half // 2
    shape = (length, PAIR)
    apart = lax.broadcasted_iota(jnp.int32, shape, 0) - lax.broadcasted_iota(jnp.int32, shape, 1) % HDIM
    distance = jnp.abs(apart)
    bucket = jnp.minimum(distance, exact)
    for edge in bucket_edges():
        bucket = bucket + (distance >= edge).astype(jnp.int32)
    return bucket + jnp.where(apart > 0, half, 0)


def lane_low(shape):
    return lax.broadcasted_iota(jnp.int32, shape, 1) < HDIM


def split_heads(pair):
    low, zero = lane_low(pair.shape), jnp.zeros_like(pair)
    return jnp.concatenate([jnp.where(low, pair, zero), jnp.where(low, zero, pair)], axis=0)


def join_heads(both):
    rows = both.shape[0] // 2
    return jnp.where(lane_low((rows, PAIR)), both[:rows], both[rows:])


def side_by_side(one, two):
    zero = jnp.zeros_like(one)
    return jnp.concatenate([jnp.concatenate([one, zero], axis=1), jnp.concatenate([zero, two], axis=1)], axis=0)


def row_sums(values):
    rows, width = values.shape
    return jnp.sum(values.reshape(rows // 8, 8, width), axis=0)


def inverse_rms(values):
    return lax.rsqrt(jnp.mean(values * values, axis=-1, keepdims=True) + EPS)


class Place:
    def __init__(self, ref, n_z):
        self.count, self.core, self.x, self.z = ref[0], ref[1], ref[2], ref[3]
        self.n_z = n_z

    def shards(self):
        for xx in range(2):
            for k in range(self.n_z):
                yield xx, k, jnp.bitwise_xor(self.z, k) * 2 + jnp.bitwise_xor(self.x, xx)


def at(shard, size):
    return pl.ds(pl.multiple_of(shard * size, size), size)


def interleaved(values, n_f, chunk):
    width = values.shape[1] // n_f // 2
    return jnp.concatenate(
        [values[:, (2 * f + chunk) * width : (2 * f + chunk + 1) * width] for f in range(n_f)], axis=1
    )


def prepare_attention(n_f, bias_ref, wq, wk, wv, ga, gf, a_ref):
    core = lax.rem(lax.axis_index("rep"), 2)
    ds = wq.shape[0]
    joined = jnp.concatenate([wq[...], wk[...], wv[...]], axis=1)
    row = lax.broadcasted_iota(jnp.int32, (ds, PAIR), 0)
    low = lane_low((1, PAIR))
    small = jnp.zeros((ds, PAIR), f32)
    n_b = BUCKETS // n_f
    for b in range(n_b):
        for p in range(PAIRS):
            value = jnp.where(low, bias_ref[b * HEADS + 2 * p], bias_ref[b * HEADS + 2 * p + 1])
            small = jnp.where(row == b * PAIRS + p, value, small)
    for i, gain in enumerate((ga, gf)):
        tiled = jnp.concatenate([gain[...]] * (PAIR // ds), axis=1)
        small = jnp.where(row == n_b * PAIRS + i, tiled, small)

    def write(c):
        if c == 0:
            a_ref[...] = joined[:, :CUT].astype(bf16)
        else:
            a_ref[:, : 3 * INNER - CUT] = joined[:, CUT:].astype(bf16)
            a_ref[:, 3 * INNER - CUT :] = small.astype(bf16)

    for c in range(2):
        pl.when(core == c)(functools.partial(write, c))


def prepare_ffn(n_f, place_ref, wo, wg, wu, wd, p0_ref, p1_ref):
    core = place_ref[1]
    ds, is_, fh = wg.shape[0], wo.shape[0], wd.shape[0] // 2
    half = wo.shape[1] // 2

    def write(c):
        cols = slice(c * half, (c + 1) * half)
        for chunk, ref in enumerate((p0_ref, p1_ref)):
            g = interleaved((wg, wu)[c][...], n_f, chunk).astype(bf16)
            ref[:ds, :] = g[:, :half]
            ref[ds : 2 * ds, :] = g[:, half:]
            ref[2 * ds : 2 * ds + fh, :] = wd[chunk * fh : (chunk + 1) * fh, cols].astype(bf16)
        tail = wo[:, cols]
        pad = p0_ref.shape[0] - (2 * ds + fh + is_)
        if pad:
            tail = jnp.concatenate([tail, jnp.zeros((pad, half), f32)], axis=0)
        p0_ref[2 * ds + fh :, :] = tail.astype(bf16)

    for c in range(2):
        pl.when(core == c)(functools.partial(write, c))


def small_params():
    return pltpu.CompilerParams(vmem_limit_bytes=12 * 1024 * 1024)


def padded(rows):
    return -(-rows // 16) * 16


def call_prepare_attention(n_f, attn_gain, wq, wk, wv, rel_bias, ffn_gain):
    vm, sm = pl.BlockSpec(memory_space=pltpu.VMEM), pl.BlockSpec(memory_space=pltpu.SMEM)
    return pl.pallas_call(
        functools.partial(prepare_attention, n_f),
        out_shape=sds((wq.shape[0], CUT), bf16),
        in_specs=[sm] + [pl.BlockSpec()] * 5,
        out_specs=vm,
        compiler_params=small_params(),
        name="prepare_attention",
    )(*(in_hbm(a) for a in (rel_bias, wq, wk, wv, attn_gain.reshape(1, -1), ffn_gain.reshape(1, -1))))


def call_prepare_ffn(place, n_f, wo, wg, wu, wd):
    ds, fh, half = wg.shape[0], wd.shape[0] // 2, wo.shape[1] // 2
    vm, sm = pl.BlockSpec(memory_space=pltpu.VMEM), pl.BlockSpec(memory_space=pltpu.SMEM)
    return pl.pallas_call(
        functools.partial(prepare_ffn, n_f),
        out_shape=(sds((2 * ds + fh + padded(wo.shape[0]), half), bf16), sds((2 * ds + fh, half), bf16)),
        in_specs=[sm] + [pl.BlockSpec()] * 4,
        out_specs=[vm] * 2,
        compiler_params=small_params(),
        name="prepare_ffn",
    )(place, *(in_hbm(a) for a in (wo, wg, wu, wd)))


def keep_close(G, L, place_ref, tok_ref, ct_ref, tok_out, ct_out, done_ref):
    step = pl.program_id(0)
    R, D = G * L, tok_ref.shape[-1]
    live = (step * G + lax.broadcasted_iota(jnp.int32, (R, 1), 0) // L) < place_ref[0]
    group_rows(tok_out, step, R)[...] = tok_ref[...].reshape(R, D)
    group_rows(ct_out, step, R)[...] = jnp.where(live, ct_ref[...].reshape(R, D), jnp.zeros((), bf16))
    done_ref[...] = jnp.zeros_like(done_ref)


def call_keep_close(place, tokens, ct):
    S, L, D = tokens.shape
    G = GROUP
    block = pl.BlockSpec((G, L, D), lambda i, c: (i, 0, 0))
    return pl.pallas_call(
        functools.partial(keep_close, G, L),
        out_shape=(sds((S * L, D), bf16), sds((S * L, D), bf16), sds((8, PAIR), f32)),
        grid_spec=pltpu.PrefetchScalarGridSpec(
            num_scalar_prefetch=1, grid=(S // G,), in_specs=[block, block], out_specs=[whole(None)] * 3
        ),
        compiler_params=params(MIB_TOKENS),
        cost_estimate=cost(S * L, 1, 8 * S * L * D),
        name="keep_close",
    )(place, in_hbm(tokens), in_hbm(ct))


def attention_forward(G, L, n_z, place_ref, tok_ref, after_ref, *refs):
    pieces, refs = refs[:4], refs[4:]
    all_qkv, all_probs, mixed_ref, w_ref, gains_ref, table_ref, st_ref, small_ref = refs
    step = pl.program_id(0)
    place = Place(place_ref, n_z)
    D = tok_ref.shape[-1]
    n_f = 2 * n_z
    ds = D // n_f
    rest = 3 * INNER - CUT

    def assemble(c):
        for xx, k, f in place.shards():
            one, two = pieces[xx].at[k], pieces[2 + xx].at[k]
            one, two = (one, two) if c == 0 else (two, one)
            w_ref[at(f, ds), :CUT] = one[...]
            w_ref[at(f, ds), CUT:] = two[:, :rest]
            small_ref[at(f, ds), :] = two[:, rest:].astype(f32)

    @pl.when(step == 0)
    def _():
        for c in range(2):
            pl.when(place.core == c)(functools.partial(assemble, c))
        n_b = BUCKETS // n_f
        ids = bucket_table(L)
        for p in range(PAIRS):
            total = jnp.zeros(ids.shape, f32)
            for b in range(BUCKETS):
                row = b // n_b * ds + (b % n_b) * PAIRS + p
                total = jnp.where(ids == b, small_ref[row : row + 1, :], total)
            table_ref[p] = total
        per = PAIR // ds
        lane = lax.broadcasted_iota(jnp.int32, (1, PAIR), 1) // ds
        gains_ref[...] = jnp.zeros_like(gains_ref)
        for i in range(2):
            for v in range(D // PAIR):
                total = jnp.zeros((1, PAIR), f32)
                for f in range(per):
                    row = (v * per + f) * ds + n_b * PAIRS + i
                    total = jnp.where(lane == f, small_ref[row : row + 1, :], total)
                gains_ref[i : i + 1, v * PAIR : (v + 1) * PAIR] = total

    @pl.when(step * G < place.count)
    def _():
        mixed, qkv_ref = group_rows(mixed_ref, step, G * L), group_rows(all_qkv, step, G * L)
        probs_ref = all_probs.at[pl.ds(step * G, G)]
        x = group_rows(tok_ref, step, G * L)[...].astype(f32)
        normed = (x * inverse_rms(x) * gains_ref[0:1, :]).astype(bf16)
        qkv_ref[...] = nn(normed, w_ref[...]).astype(bf16)
        for s in range(0, G, 2):
            for p in range(PAIRS):
                q, k = (
                    [qkv_ref[pl.ds((s + i) * L, L), pl.ds(b * INNER + p * PAIR, PAIR)] for i in range(2)] for b in range(2)
                )
                st = nt(jnp.concatenate(k, axis=1), side_by_side(split_heads(q[0]), split_heads(q[1])))
                st_ref[s, p], st_ref[s + 1, p] = st[:, :PAIR], st[:, PAIR:]
        for s in range(G):
            for p in range(PAIRS):
                st = st_ref[s, p] + table_ref[p]
                e = jnp.exp(st - jnp.max(st, axis=0, keepdims=True))
                probs_ref[s, p] = (e * (1.0 / jnp.sum(e, axis=0, keepdims=True))).astype(bf16)
        for s in range(G):
            rows = pl.ds(s * L, L)
            for p in range(PAIRS):
                v = qkv_ref[rows, pl.ds(2 * INNER + p * PAIR, PAIR)]
                mixed[rows, pl.ds(p * PAIR, PAIR)] = join_heads(tn(probs_ref[s, p], v)).astype(bf16)


MIB_FORWARD, MIB_FFN, MIB_BACKWARD, MIB_TOKENS, MIB_RESULT = 8, 14, 10, 6, 6


def params(mib):
    return pltpu.CompilerParams(dimension_semantics=("arbitrary",), vmem_limit_bytes=mib * 1024 * 1024)


def whole(shape):
    return pl.BlockSpec(memory_space=pltpu.VMEM)


def live_group(i, place, G):
    return jnp.minimum(i, jnp.maximum((place[0] + G - 1) // G - 1, 0))


def series_spec(G, shape, every=False):
    tail = (0,) * (len(shape) - 1)
    return pl.BlockSpec((G,) + shape[1:], lambda i, c: ((i if every else live_group(i, c, G)),) + tail)


def row_spec(G, L, width):
    return pl.BlockSpec((G * L, width), lambda i, c: (live_group(i, c, G), 0))


def group_rows(ref, step, rows):
    return ref.at[pl.ds(pl.multiple_of(step * rows, rows), rows), :]


def cost(rows, per_row, nbytes, exps=0):
    return pl.CostEstimate(flops=2 * rows * per_row, bytes_accessed=nbytes, transcendentals=exps)


def call_attention_forward(place, tokens, after, pieces, S, L, D):
    G, n_z = GROUP, pieces[0].shape[0]
    return pl.pallas_call(
        functools.partial(attention_forward, G, L, n_z),
        out_shape=(
            sds((S * L, 3 * INNER), bf16),
            sds((S, PAIRS, L, PAIR), bf16),
            sds((S * L, INNER), bf16),
            sds((D, 3 * INNER), bf16),
            sds((8, D), f32),
        ),
        grid_spec=pltpu.PrefetchScalarGridSpec(
            num_scalar_prefetch=1,
            grid=(S // G,),
            in_specs=[whole(tokens.shape), whole(after.shape)] + [whole(piece.shape) for piece in pieces],
            out_specs=[
                whole((S * L, 3 * INNER)),
                whole((S, PAIRS, L, PAIR)),
                whole((S * L, INNER)),
                whole((D, 3 * INNER)),
                whole((8, D)),
            ],
            scratch_shapes=[
                pltpu.VMEM((PAIRS, L, PAIR), f32),
                pltpu.VMEM((G, PAIRS, L, PAIR), f32),
                pltpu.VMEM((D, PAIR), f32),
            ],
        ),
        compiler_params=params(MIB_FORWARD),
        cost_estimate=cost(S * L, D * 3 * INNER * 4, S * L * 5000),
        name="attention_forward",
    )(place, tokens, after, *pieces)


def gelu_parts(v):
    c = 0.7978845608028654
    v2 = v * v
    t = jnp.tanh(v * (c + (c * 0.044715) * v2))
    half = 0.5 + 0.5 * t
    return v * half, half + (0.5 * v) * (1.0 - t * t) * (c + (3 * c * 0.044715) * v2)


def put_weights(place, pieces, wgu, wd, wo=None):
    FW, D = wd.shape

    def assemble(c):
        for f, here, there in pieces:
            for which, piece in enumerate((here, there) if c == 0 else (there, here)):
                n_f = len(pieces)
                ds, fh, half, is_ = D // n_f, FW // n_f, FW // 2, INNER // n_f
                for part in range(2):
                    start = (2 * part + which) * half
                    wgu[at(f, ds), start : start + half] = piece[part * ds : (part + 1) * ds, :]
                cols = slice(which * half, (which + 1) * half)
                wd[at(f, fh), cols] = piece[2 * ds : 2 * ds + fh, :]
                if wo is None:
                    continue
                if is_ % 16 == 0:
                    wo[at(f, is_), cols] = piece[2 * ds + fh : 2 * ds + fh + is_, :]
                else:
                    wo[f, :, cols] = piece[2 * ds + fh :, :]

    for c in range(2):
        pl.when(place.core == c)(functools.partial(assemble, c))


def put_grads(place, n_z, keep, send, agu, ad, ao=None):
    n_f = 2 * n_z
    FW, D = ad.shape
    ds, fh, half = D // n_f, FW // n_f, FW // 2

    def write(c):
        for xx, k, f in place.shards():
            for which, ref in enumerate((keep, send) if c == 0 else (send, keep)):
                for part in range(2):
                    start = (2 * part + which) * half
                    ref[xx, k, part * ds : (part + 1) * ds, :] = agu[at(f, ds), start : start + half].astype(bf16)
                cols = slice(which * half, (which + 1) * half)
                ref[xx, k, 2 * ds : 2 * ds + fh, :] = ad[at(f, fh), cols].astype(bf16)
                if ao is not None:
                    is_ = INNER // n_f
                    if is_ % 16 == 0:
                        ref[xx, k, 2 * ds + fh :, :] = ao[at(f, is_), cols].astype(bf16)
                    else:
                        ref[xx, k, 2 * ds + fh :, :] = ao[f, :, cols].astype(bf16)

    for c in range(2):
        pl.when(place.core == c)(functools.partial(write, c))


def ffn_half(G, L, n_z, stage, shift, place_ref, *refs):
    n_f = 2 * n_z
    place = Place(place_ref, n_z)
    first, begins, ends = stage == 0, stage < 2, stage != 1
    if first:
        (near, own_far, far, near_c, own_far_c, far_c), refs = refs[:6], refs[6:]
        here, there = ([near.at[k] for k in range(n_z)] for near in (near, near_c))
        here, there = (
            side + [own] + [rest.at[k] for k in range(n_z - 1)]
            for side, own, rest in ((here, own_far, far), (there, own_far_c, far_c))
        )
        pieces = [(f, *pair) for (_, _, f), pair in zip(place.shards(), zip(here, there))]
    elif begins:
        pieces, refs = refs[:4], refs[4:]
        pieces = [(f, pieces[xx].at[k], pieces[2 + xx].at[k]) for xx, k, f in place.shards()]
    if stage == 0:
        (tok_ref, ct_ref, mixed_ref, gains_ref,
         hid_ref, act_ref, gpart_ref, wd, wo_out, keep, send,
         agu, ad, wgu, n2, n2_next, gu, ga, low, gn, spread) = refs
    elif stage == 1:
        hid_ref, ct_ref, gains_ref, wo_in, _, _ = refs[:6]
        gpart_ref, mixed_ref, act_ref, agu, ad, ao, gf_ref, wd, wgu, n2, n2_next, gu, ga, low, gn = refs[6:]
    else:
        hid_ref, ct_ref, gains_ref, wo_in, wd, wgu = refs[:6]
        gpart_ref, mixed_ref, act_ref, agu, ad, ao, gf_ref, keep, send, n2, n2_next, gu, ga, low, gn, spread = refs[13:]
    step = pl.program_id(0) + shift
    R = G * L
    FW, D = wd.shape
    CH = FW // 2
    is_ = INNER // n_f
    count = place.count
    group = jnp.minimum(step, (count + G - 1) // G - 1)

    def normalise(group, into):
        if first:
            h = group_rows(tok_ref, group, R)[...].astype(f32) + nn(group_rows(mixed_ref, group, R)[...], wo_out[...])
            group_rows(hid_ref, group, R)[...] = h.astype(bf16)
        else:
            h = group_rows(hid_ref, group, R)[...].astype(f32)
        into[...] = (h * inverse_rms(h) * gains_ref[1:2, :]).astype(bf16)

    if begins:

        @pl.when(step == 0)
        def _():
            wo = (wo_out if is_ % 16 == 0 else spread) if first else None
            put_weights(place, pieces, wgu, wd, wo)
            if first and is_ % 16:
                wo_out[...] = jnp.concatenate([spread[f, :is_, :].astype(f32) for f in range(n_f)], axis=0).astype(bf16)
            for ref in (agu, ad) if first else (agu, ad, ao, gf_ref):
                ref[...] = jnp.zeros_like(ref)

    @pl.when(step * G < count)
    def _():
        normalise(group, n2)
        gb, act, gpart, hid = (group_rows(ref, group, R) for ref in (ct_ref, act_ref, gpart_ref, hid_ref))
        for c in range(2):
            cols, both = pl.ds(c * CH, CH), pl.ds(2 * c * CH, 2 * CH)
            gu[c] = nn(n2[...], wgu[:, both])
            ga[c] = nt(gb[...], wd[cols, :])
        for c in range(2):
            cols, both = pl.ds(c * CH, CH), pl.ds(2 * c * CH, 2 * CH)
            for r in range(0, R, L):
                rows = pl.ds(r, L)
                u = gu[c, rows, CH:]
                a = ga[c, rows, :]
                g, dg = gelu_parts(gu[c, rows, :CH])
                act[rows, cols] = (g * u).astype(bf16)
                low[c, rows, :CH] = (a * u * dg).astype(bf16)
                low[c, rows, CH:] = (a * g).astype(bf16)
            if c == 0:
                gn[...] = nt(low[c], wgu[:, both])
            else:
                gn[...] += nt(low[c], wgu[:, both])
            ad[cols, :] += tn(act[:, cols], gb[...])
            agu[:, both] += tn(n2[...], low[c])
        if first:
            gpart[...] = gn[...].astype(bf16)
        else:
            mixed = group_rows(mixed_ref, group, R)
            h = hid[...].astype(f32)
            scale = inverse_rms(h)
            hs = h * scale
            g2 = gn[...] + gpart[...].astype(f32)
            gf_ref[...] += row_sums(g2 * hs)
            g2 = g2 * gains_ref[1:2, :]
            dot = jnp.mean(g2 * hs, axis=-1, keepdims=True)
            gh = (gb[...].astype(f32) + scale * (g2 - hs * dot)).astype(bf16)
            gpart[...] = gh
            ao[...] += tn(mixed[...], gh)
            mixed[...] = nt(gh, wo_in[...]).astype(bf16)

    if ends:

        @pl.when(pl.program_id(0) == pl.num_programs(0) - 1)
        def _():
            if first:
                put_grads(place, n_z, keep, send, agu, ad)
            elif is_ % 16 == 0:
                put_grads(place, n_z, keep, send, agu, ad, ao)
            else:
                for f in range(n_f):
                    spread[f, :is_, :] = ao[f * is_ : (f + 1) * is_, :]
                put_grads(place, n_z, keep, send, agu, ad, spread)


def call_ffn_half(stage, place, n_z, operands, S, L, D):
    G = GROUP
    R, n_f = G * L, 2 * n_z
    FW = D
    CH = FW // 2
    ds, fh, is_ = D // n_f, FW // n_f, INNER // n_f
    pack = (2, n_z, 2 * ds + fh + (padded(is_) if stage else 0), CH)
    packs, act = [sds(pack, bf16)] * 2, sds((S * L, FW), bf16)
    wd, wgu, rows = sds((FW, D), bf16), sds((D, 2 * FW), bf16), sds((S * L, D), bf16)
    agu, ad = sds((D, 2 * FW), f32), sds((FW, D), f32)
    running = [rows, sds((S * L, INNER), bf16), act, agu, ad, sds((INNER, D), f32), sds((8, D), f32)]
    vm = pltpu.VMEM
    work = [
        vm((R, D), bf16), vm((R, D), bf16),
        vm((2, R, 2 * CH), f32), vm((2, R, CH), f32), vm((2, R, 2 * CH), bf16), vm((R, D), f32),
    ]
    spread = [vm((n_f, padded(is_), D) if is_ % 16 else (1, 16, 128), f32 if stage else bf16)]
    half = S // G // 2
    steps, shift = ((S // G, 0), (half, 0), (S // G - half, half))[stage]
    if stage == 0:
        out_shape = [rows, act, rows, wd, sds((INNER, D), bf16)] + packs
        scratch = [vm(agu.shape, f32), vm(ad.shape, f32), vm(wgu.shape, bf16)] + work + spread
        aliases = {}
    elif stage == 1:
        out_shape, scratch = running + [wd, wgu], work
        aliases = {9: 0, 10: 1}
    else:
        out_shape, scratch = running + packs, work + spread
        aliases = {7 + i: i for i in range(7)}
    return pl.pallas_call(
        functools.partial(ffn_half, G, L, n_z, stage, shift),
        out_shape=tuple(out_shape),
        grid_spec=pltpu.PrefetchScalarGridSpec(
            num_scalar_prefetch=1,
            grid=(steps,),
            in_specs=[whole(a.shape) for a in operands],
            out_specs=[whole(shape.shape) for shape in out_shape],
            scratch_shapes=scratch,
        ),
        input_output_aliases=aliases,
        compiler_params=params(MIB_FFN),
        cost_estimate=cost(steps * R, 9 * D * FW, S * L * 9000),
        name=("ffn_first", "ffn_second", "ffn_third")[stage],
    )(place, *operands)


def layer_result(G, L, shift, place_ref, hid_ref, act_0, act_1, wd_0, wd_1, gains_ref, *refs):
    out_ref, done_ref = refs[-2:]
    step = pl.program_id(0) + shift
    count = place_ref[0]
    R = G * L
    D = hid_ref.shape[-1]
    done_ref[...] = gains_ref[...]
    group = jnp.minimum(step, (count + G - 1) // G - 1)
    hid_ref, act_0, act_1 = (group_rows(ref, group, R) for ref in (hid_ref, act_0, act_1))

    @pl.when(step * G >= count)
    def _():
        out_ref[...] = jnp.zeros_like(out_ref)

    @pl.when(step * G < count)
    def _():
        live = (step * G + lax.broadcasted_iota(jnp.int32, (R, 1), 0) // L) < count
        out = hid_ref[...].astype(f32) + nn(act_0[...], wd_0[...]) + nn(act_1[...], wd_1[...])
        out_ref[...] = jnp.where(live, out, 0.0).astype(bf16).reshape(G, L, D)


def call_layer_result(place, hidden, act_0, act_1, wd_0, wd_1, gains, S, L, earlier=None):
    G, D = GROUP, hidden.shape[-1]
    operands = (hidden, act_0, act_1, wd_0, wd_1, gains)
    half = S // G // 2
    steps, shift = (half, 0) if earlier is None else (S // G - half, half)
    more = () if earlier is None else (earlier,)
    return pl.pallas_call(
        functools.partial(layer_result, G, L, shift),
        out_shape=(pltpu.HBM((S, L, D), bf16), sds(gains.shape, f32)),
        grid_spec=pltpu.PrefetchScalarGridSpec(
            num_scalar_prefetch=1,
            grid=(steps,),
            in_specs=[whole(a.shape) for a in operands] + [pl.BlockSpec(memory_space=pl.ANY)] * len(more),
            out_specs=(pl.BlockSpec((G, L, D), lambda i, c: (i + shift, 0, 0)), whole(gains.shape)),
        ),
        input_output_aliases={7: 0} if more else {},
        compiler_params=params(MIB_RESULT),
        cost_estimate=cost(S * L // 2, 2 * D * act_0.shape[-1], S * L * 3000),
        name="layer_result",
    )(place, *operands, *more)


def attention_backward(G, L, n_z, place_ref, tok_ref, _, probs_ref, gm_ref, w_ref, gains_ref, gf_ref,
                       dqkv, keep, send, aw, ab, dp_ref, ds_ref, small):
    step = pl.program_id(0)
    last = pl.num_programs(0) - 1
    R = G * L
    D = tok_ref.shape[-1]
    place = Place(place_ref, n_z)
    count = place.count
    group = jnp.minimum(step, (count + G - 1) // G - 1)
    probs_ref = probs_ref.at[pl.ds(group * G, G)]
    gm_ref, dqkv = group_rows(gm_ref, group, R), group_rows(dqkv, group, R)

    @pl.when(step == 0)
    def _():
        for ref in (aw, ab):
            ref[...] = jnp.zeros_like(ref)

    @pl.when(step * G < count)
    def _():
        cols = [[pl.ds(b * INNER + p * PAIR, PAIR) for b in range(3)] for p in range(PAIRS)]
        for s in range(G):
            for p in range(PAIRS):
                rows = pl.ds(s * L, L)
                dm = split_heads(gm_ref[rows, pl.ds(p * PAIR, PAIR)])
                dp_ref[s, p] = nt(dqkv[rows, cols[p][2]], dm)
                dqkv[rows, cols[p][2]] = nn(probs_ref[s, p], dm).astype(bf16)
        for p in range(PAIRS):
            total = ab[p]
            for s in range(G):
                prf = probs_ref[s, p].astype(f32)
                dp = dp_ref[s, p]
                ds = prf * (dp - jnp.sum(prf * dp, axis=0, keepdims=True))
                total = total + ds
                ds_ref[s, p] = ds.astype(bf16)
            ab[p] = total
        for s in range(G):
            for p in range(PAIRS):
                rows = pl.ds(s * L, L)
                low = ds_ref[s, p]
                q, k = dqkv[rows, cols[p][0]], dqkv[rows, cols[p][1]]
                dqkv[rows, cols[p][1]] = nn(low, split_heads(q)).astype(bf16)
                dqkv[rows, cols[p][0]] = join_heads(tn(low, k)).astype(bf16)
        x = group_rows(tok_ref, group, R)[...].astype(f32)
        aw[...] += tn((x * inverse_rms(x) * gains_ref[0:1, :]).astype(bf16), dqkv[...])

    @pl.when(step == last)
    def _():
        n_f = 2 * n_z
        ds, n_b, rest = D // n_f, BUCKETS // n_f, 3 * INNER - CUT
        ids = bucket_table(L)
        low = lane_low((1, PAIR))
        small[...] = jnp.zeros_like(small)
        for p in range(PAIRS):
            t = ab[p]
            for b in range(BUCKETS):
                by_lane = jnp.sum(jnp.where(ids == b, t, 0.0), axis=0, keepdims=True)
                one = jnp.sum(jnp.where(low, by_lane, 0.0), axis=1, keepdims=True)
                two = jnp.sum(jnp.where(low, 0.0, by_lane), axis=1, keepdims=True)
                row = b // n_b * ds + (b % n_b) * HEADS + 2 * p
                small[row : row + 1, :] = jnp.broadcast_to(one, (1, PAIR))
                small[row + 1 : row + 2, :] = jnp.broadcast_to(two, (1, PAIR))
        gain = jnp.transpose(gains_ref[...])[:, 0:1]
        one = jnp.sum(aw[...] * w_ref[...].astype(f32), axis=1, keepdims=True) / gain
        two = jnp.sum(jnp.transpose(gf_ref[...]), axis=1, keepdims=True)
        lane = lax.broadcasted_iota(jnp.int32, (D, PAIR), 1)
        small[...] = jnp.where(lane == 0, one, jnp.where(lane == 1, two, small[...]))

        def write(c):
            for xx, k, f in place.shards():
                one, two = keep.at[xx, k], send.at[xx, k]
                one, two = (one, two) if c == 0 else (two, one)
                one[...] = aw[at(f, ds), :CUT].astype(bf16)
                two[:, :rest] = aw[at(f, ds), CUT:].astype(bf16)
                two[:, rest:] = small[at(f, ds), :].astype(bf16)

        for c in range(2):
            pl.when(place.core == c)(functools.partial(write, c))


def call_attention_backward(place, n_z, tokens, qkv, probs, gm, w, gains, gf, S, L, D):
    G = GROUP
    pack = (2, n_z, D // (2 * n_z), CUT)
    vm = pltpu.VMEM
    return pl.pallas_call(
        functools.partial(attention_backward, G, L, n_z),
        out_shape=(sds((S * L, 3 * INNER), bf16), sds(pack, bf16), sds(pack, bf16)),
        grid_spec=pltpu.PrefetchScalarGridSpec(
            num_scalar_prefetch=1,
            grid=(S // G,),
            in_specs=[whole(tokens.shape), whole(qkv.shape), whole(probs.shape),
                      whole(gm.shape), whole(w.shape), whole(gains.shape), whole(gf.shape)],
            out_specs=[whole(pack)] * 3,
            scratch_shapes=[
                vm(w.shape, f32), vm((PAIRS, L, PAIR), f32),
                vm((G, PAIRS, L, PAIR), f32), vm((G, PAIRS, L, PAIR), bf16), vm((D, PAIR), f32),
            ],
        ),
        input_output_aliases={2: 0},
        compiler_params=params(MIB_BACKWARD),
        cost_estimate=cost(S * L, D * 3 * INNER * 4, S * L * 6000),
        name="attention_backward",
    )(place, tokens, qkv, probs, gm, w, gains, gf)


def token_gradient(G, L, place_ref, tok_ref, dqkv_ref, gh_ref, w_ref, gains_ref, gt_ref, done_ref):
    step = pl.program_id(0)
    D = tok_ref.shape[-1]
    done_ref[...] = gains_ref[...]
    group = jnp.minimum(step, (place_ref[0] + G - 1) // G - 1)
    tok_ref, dqkv_ref, gh_ref = (group_rows(ref, group, G * L) for ref in (tok_ref, dqkv_ref, gh_ref))

    @pl.when(step * G >= place_ref[0])
    def _():
        gt_ref[...] = jnp.zeros_like(gt_ref)

    @pl.when(step * G < place_ref[0])
    def _():
        half = G * L // 2
        parts = [pl.ds(i * half, half) for i in range(2)]
        products = [nt(dqkv_ref[rows, :], w_ref[...]) for rows in parts]
        for i, rows in enumerate(parts):
            x = tok_ref[rows, :].astype(f32)
            scale = inverse_rms(x)
            xs = x * scale
            g = products[i] * gains_ref[0:1, :]
            dot = jnp.mean(g * xs, axis=-1, keepdims=True)
            gt = gh_ref[rows, :].astype(f32) + scale * (g - xs * dot)
            gt_ref[pl.ds(i * G // 2, G // 2)] = gt.astype(bf16).reshape(G // 2, L, D)


def call_token_gradient(place, tokens, dqkv, gh, w, gains, S, L, D):
    G = GROUP
    operands = (tokens, dqkv, gh, w, gains)
    return pl.pallas_call(
        functools.partial(token_gradient, G, L),
        out_shape=(pltpu.HBM((S, L, D), bf16), sds(gains.shape, f32)),
        grid_spec=pltpu.PrefetchScalarGridSpec(
            num_scalar_prefetch=1,
            grid=(S // G,),
            in_specs=[whole(a.shape) for a in operands],
            out_specs=(series_spec(G, (S, L, D), True), whole(gains.shape)),
        ),
        compiler_params=params(MIB_TOKENS),
        cost_estimate=cost(S * L, D * 3 * INNER * 2, S * L * 5000),
        name="token_gradient",
    )(place, *operands)


def finish(n_f, place_ref, *refs):
    packs = [refs[2 * i : 2 * i + 2] for i in range(3)]
    gq, gk, gv, go, gg, gu, gd, ga, gf, gb = refs[7:]
    core = place_ref[1]
    ds, is_, fh = gq.shape[0], go.shape[0], gd.shape[0] // 2
    half = go.shape[1] // 2

    def halves(pack):
        here, there = pack[0][...].astype(f32), pack[1][...].astype(f32)
        return jnp.where(core == 0, here, there), jnp.where(core == 0, there, here)

    one, two = halves(packs[2])
    gq[...] = one[:, :INNER]
    gk[...] = jnp.concatenate([one[:, INNER:CUT], two[:, : 2 * INNER - CUT]], axis=1)
    gv[...] = two[:, 2 * INNER - CUT : 3 * INNER - CUT]
    small = jnp.transpose(two[:, 3 * INNER - CUT :])
    ga[...] = small[0]
    gf[...] = small[1]
    gb[...] = small[2, : BUCKETS // n_f * HEADS]
    chunks = [halves(packs[0]), halves(packs[1])]
    for which, ref in enumerate((gg, gu)):
        wide = [jnp.concatenate([c[which][:ds], c[which][ds : 2 * ds]], axis=1) for c in chunks]
        width = wide[0].shape[1] // n_f
        ref[...] = jnp.concatenate(
            [w[:, f * width : (f + 1) * width] for f in range(n_f) for w in wide], axis=1
        )
    for chunk, pair in enumerate(chunks):
        for which in range(2):
            gd[chunk * fh : (chunk + 1) * fh, which * half : (which + 1) * half] = pair[which][2 * ds : 2 * ds + fh]
    for which in range(2):
        go[:, which * half : (which + 1) * half] = chunks[1][which][2 * ds + fh : 2 * ds + fh + is_]


def call_finish(place, n_f, packs, shapes, after):
    vm, sm = pl.BlockSpec(memory_space=pltpu.VMEM), pl.BlockSpec(memory_space=pltpu.SMEM)
    flat = [piece for pack in packs for piece in pack]
    return pl.pallas_call(
        functools.partial(finish, n_f),
        out_shape=tuple(sds(shape, f32) for shape in shapes),
        in_specs=[sm] + [vm] * len(flat) + [vm],
        out_specs=[vm] * len(shapes),
        compiler_params=small_params(),
        name="finish",
    )(place, *flat, after)


def solution(mesh):
    n_r, n_f = mesh.shape["rep"], mesh.shape["fsdp"]
    n_z = n_f // 2

    def over_fsdp(value, distance):
        return lax.ppermute(value, "fsdp", [(i, i ^ distance) for i in range(n_f)])

    def over_rep(value, distance):
        return lax.ppermute(value, "rep", [(i, i ^ distance) for i in range(n_r)])

    def along_z(pack):
        return [pack] + [over_fsdp(pack, 2 * k) for k in range(1, n_z)]

    def halved(keep, got):
        away = (keep[1].astype(f32) + got[1].astype(f32)).astype(bf16)
        return keep[0].astype(f32) + got[0].astype(f32), away

    def joined(here, got):
        here = here + got.astype(f32)
        return here[0], [here[k].astype(bf16) for k in range(1, n_z)]

    def to_z(pieces):
        return [over_fsdp(piece, 2 * (k + 1)) for k, piece in enumerate(pieces)]

    def summed(own, got):
        for value in got:
            own = own + value.astype(f32)
        return own.astype(bf16)

    def replicas(own, got):
        distance = 2
        while distance < n_r:
            own = (own.astype(f32) + got.astype(f32)).astype(bf16)
            distance *= 2
            got = over_rep(own, distance) if distance < n_r else None
        return own, over_rep(own, 1)

    together = lax.optimization_barrier

    def body(tokens, counts, attn_gain, wq, wk, wv, wo, rel_bias, ffn_gain, wg, wu, wd, cotangent):
        S, L, D = tokens.shape
        r, f = lax.axis_index("rep"), lax.axis_index("fsdp")
        place = in_hbm(jnp.stack([counts[0, 0], r % 2, f % 2, f // 2]).astype(jnp.int32))
        pack_a = call_prepare_attention(n_f, attn_gain, wq, wk, wv, rel_bias, ffn_gain)
        pack_0, pack_1 = call_prepare_ffn(place, n_f, wo, wg, wu, wd)

        z_0 = along_z(pack_0)
        z_a, pack_1 = together((along_z(pack_a), pack_1))
        near_a = jnp.stack(z_a)
        far_a, own_far_0 = over_fsdp(near_a, 1), over_fsdp(pack_0, 1)
        tokens, cotangent, done = call_keep_close(place, tokens, cotangent)
        done, far_a, own_far_0, z_0, pack_1 = together((done, far_a, own_far_0, z_0, pack_1))
        near_ac, far_ac, near_0 = over_rep(near_a, 1), over_rep(far_a, 1), jnp.stack(z_0)
        far_ac, near_0 = together((far_ac, near_0))

        far_0, near_0c, z_1 = over_fsdp(near_0[1:], 1), over_rep(near_0, 1), along_z(pack_1)
        qkv, probs, mixed, w_all, gains = call_attention_forward(place, tokens, done, (near_a, far_a, near_ac, far_ac), S, L, D)
        gains, far_0, near_0c, own_far_0, z_1 = together((gains, far_0, near_0c, own_far_0, z_1))
        own_far_0c, far_0c, near_1 = over_rep(own_far_0, 1), over_rep(far_0, 1), jnp.stack(z_1)
        far_0c, near_1 = together((far_0c, near_1))

        far_1, near_1c = over_fsdp(near_1, 1), over_rep(near_1, 1)
        hidden, act_0, gpart, wd_0, wo_all, keep_0, send_0 = call_ffn_half(
            0, place, n_z, (near_0, own_far_0, far_0, near_0c, own_far_0c, far_0c, tokens, cotangent, mixed, gains), S, L, D
        )
        wo_all, keep_0, send_0, far_1, near_1c = together((wo_all, keep_0, send_0, far_1, near_1c))

        far_1c, got_0 = over_rep(far_1, 1), over_rep(send_0, 1)
        *running, gf, wd_1, wgu = call_ffn_half(
            1, place, n_z, (near_1, far_1, near_1c, far_1c, hidden, cotangent, gains, wo_all, gpart, mixed), S, L, D
        )
        gf, got_0 = together((gf, got_0))
        here_0, away_0 = halved(keep_0, got_0)
        away_0, gf = together((away_0, gf))
        got_0 = over_fsdp(away_0, 1)
        gh, gm, act_1, _, _, _, gf, keep_1, send_1 = call_ffn_half(
            2, place, n_z, (hidden, cotangent, gains, wo_all, wd_1, wgu, *running, gf), S, L, D
        )
        keep_1, send_1, gf, got_0 = together((keep_1, send_1, gf, got_0))
        own_0, z_0 = joined(here_0, got_0)
        z_0, got_1 = to_z(z_0), over_rep(send_1, 1)
        here_1, away_1 = halved(keep_1, got_1)
        gf, away_1 = together((gf, away_1))
        got_1 = over_fsdp(away_1, 1)
        dqkv, keep_2, send_2 = call_attention_backward(place, n_z, tokens, qkv, probs, gm, w_all, gains, gf, S, L, D)
        keep_2, send_2, z_0, got_1 = together((keep_2, send_2, z_0, got_1))
        sum_0 = summed(own_0, z_0)
        own_1, z_1 = joined(here_1, got_1)

        z_1, got_2 = to_z(z_1), over_rep(send_2, 1)
        here_2, away_2 = halved(keep_2, got_2)
        gains, away_2, sum_0 = together((gains, away_2, sum_0))
        got_2 = over_fsdp(away_2, 1)
        grad_tokens, done = call_token_gradient(place, tokens, dqkv, gh, w_all, gains, S, L, D)
        done, got_2, z_1 = together((done, got_2, z_1))
        sum_1 = summed(own_1, z_1)
        own_2, z_2 = joined(here_2, got_2)
        done, z_2 = together((done, z_2))
        z_2 = to_z(z_2)
        half_out, done = call_layer_result(place, hidden, act_0, act_1, wd_0, wd_1, done, S, L)
        done, z_2 = together((done, z_2))
        sum_2 = summed(own_2, z_2)
        done, sum_2 = together((done, sum_2))
        got = [over_rep(value, 2) for value in (sum_0, sum_1, sum_2)]
        layer_out, done = call_layer_result(place, hidden, act_0, act_1, wd_0, wd_1, done, S, L, half_out)
        done, got = together((done, got))
        gq, gk, gv, go, gg, gu, gd, grad_attn_gain, grad_ffn_gain, grad_bias = call_finish(
            place, n_f, [replicas(own, y) for own, y in zip((sum_0, sum_1, sum_2), got)],
            (wq.shape, wk.shape, wv.shape, wo.shape, wg.shape, wu.shape, wd.shape,
             attn_gain.shape, ffn_gain.shape, rel_bias.shape), done,
        )
        return (layer_out, grad_tokens, grad_attn_gain, gq, gk, gv, go, grad_bias, grad_ffn_gain, gg, gu, gd)

    rows, cols, flat = P(("rep", "fsdp"), None, None), P("fsdp", None), P("fsdp")
    return jax.shard_map(
        body,
        mesh=mesh,
        in_specs=(rows, P("rep", "fsdp"), flat, cols, cols, cols, cols, flat, flat, cols, cols, cols, rows),
        out_specs=(rows, rows, flat, cols, cols, cols, cols, flat, flat, cols, cols, cols),
        check_vma=False,
    )
```

```python
import functools

import jax
import jax.numpy as jnp
from jax import lax
from jax.experimental import pallas as pl
from jax.experimental.pallas import tpu as pltpu
from jax.sharding import PartitionSpec as P

HEADS, HDIM, BUCKETS = 6, 64, 32
INNER = HEADS * HDIM
PAIRS = HEADS // 2
PAIR = 2 * HDIM
CUT = 640
GROUP = 8
EPS = 1e-6
bf16, f32 = jnp.bfloat16, jnp.float32
sds = jax.ShapeDtypeStruct


def in_hbm(value):
    return pltpu.with_memory_space_constraint(value, pltpu.HBM)


def nn(a, b):
    return jnp.dot(a, b, preferred_element_type=f32)


def nt(a, b):
    return lax.dot_general(a, b, (((1,), (1,)), ((), ())), preferred_element_type=f32)


def tn(a, b):
    return lax.dot_general(a, b, (((0,), (0,)), ((), ())), preferred_element_type=f32)


def bucket_edges():
    half = BUCKETS // 2
    exact = half // 2
    power = half - exact
    return [
        min(m for m in range(exact, 129) if m**power * exact**k >= 128**k * exact**power) for k in range(1, power)
    ]


def bucket_table(length):
    half = BUCKETS // 2
    exact = half // 2
    shape = (length, PAIR)
    apart = lax.broadcasted_iota(jnp.int32, shape, 0) - lax.broadcasted_iota(jnp.int32, shape, 1) % HDIM
    distance = jnp.abs(apart)
    bucket = jnp.minimum(distance, exact)
    for edge in bucket_edges():
        bucket = bucket + (distance >= edge).astype(jnp.int32)
    return bucket + jnp.where(apart > 0, half, 0)


def lane_low(shape):
    return lax.broadcasted_iota(jnp.int32, shape, 1) < HDIM


def split_heads(pair):
    low, zero = lane_low(pair.shape), jnp.zeros_like(pair)
    return jnp.concatenate([jnp.where(low, pair, zero), jnp.where(low, zero, pair)], axis=0)


def join_heads(both):
    rows = both.shape[0] // 2
    return jnp.where(lane_low((rows, PAIR)), both[:rows], both[rows:])


def side_by_side(one, two):
    zero = jnp.zeros_like(one)
    return jnp.concatenate([jnp.concatenate([one, zero], axis=1), jnp.concatenate([zero, two], axis=1)], axis=0)


def row_sums(values):
    rows, width = values.shape
    return jnp.sum(values.reshape(rows // 8, 8, width), axis=0)


def inverse_rms(values):
    return lax.rsqrt(jnp.mean(values * values, axis=-1, keepdims=True) + EPS)


class Place:
    def __init__(self, ref, n_z):
        self.count, self.core, self.x, self.z = ref[0], ref[1], ref[2], ref[3]
        self.n_z = n_z

    def shards(self):
        for xx in range(2):
            for k in range(self.n_z):
                yield xx, k, jnp.bitwise_xor(self.z, k) * 2 + jnp.bitwise_xor(self.x, xx)


def at(shard, size):
    return pl.ds(pl.multiple_of(shard * size, size), size)


def interleaved(values, n_f, chunk):
    width = values.shape[1] // n_f // 2
    return jnp.concatenate(
        [values[:, (2 * f + chunk) * width : (2 * f + chunk + 1) * width] for f in range(n_f)], axis=1
    )


def prepare_attention(n_f, bias_ref, wq, wk, wv, ga, gf, a_ref):
    core = lax.rem(lax.axis_index("rep"), 2)
    ds = wq.shape[0]
    joined = jnp.concatenate([wq[...], wk[...], wv[...]], axis=1)
    row = lax.broadcasted_iota(jnp.int32, (ds, PAIR), 0)
    low = lane_low((1, PAIR))
    small = jnp.zeros((ds, PAIR), f32)
    n_b = BUCKETS // n_f
    for b in range(n_b):
        for p in range(PAIRS):
            value = jnp.where(low, bias_ref[b * HEADS + 2 * p], bias_ref[b * HEADS + 2 * p + 1])
            small = jnp.where(row == b * PAIRS + p, value, small)
    for i, gain in enumerate((ga, gf)):
        tiled = jnp.concatenate([gain[...]] * (PAIR // ds), axis=1)
        small = jnp.where(row == n_b * PAIRS + i, tiled, small)

    def write(c):
        if c == 0:
            a_ref[...] = joined[:, :CUT].astype(bf16)
        else:
            a_ref[:, : 3 * INNER - CUT] = joined[:, CUT:].astype(bf16)
            a_ref[:, 3 * INNER - CUT :] = small.astype(bf16)

    for c in range(2):
        pl.when(core == c)(functools.partial(write, c))


def prepare_ffn(n_f, place_ref, wo, wg, wu, wd, p0_ref, p1_ref):
    core = place_ref[1]
    ds, is_, fh = wg.shape[0], wo.shape[0], wd.shape[0] // 2
    half = wo.shape[1] // 2

    def write(c):
        cols = slice(c * half, (c + 1) * half)
        for chunk, ref in enumerate((p0_ref, p1_ref)):
            g = interleaved((wg, wu)[c][...], n_f, chunk).astype(bf16)
            ref[:ds, :] = g[:, :half]
            ref[ds : 2 * ds, :] = g[:, half:]
            ref[2 * ds : 2 * ds + fh, :] = wd[chunk * fh : (chunk + 1) * fh, cols].astype(bf16)
        tail = wo[:, cols]
        pad = p0_ref.shape[0] - (2 * ds + fh + is_)
        if pad:
            tail = jnp.concatenate([tail, jnp.zeros((pad, half), f32)], axis=0)
        p0_ref[2 * ds + fh :, :] = tail.astype(bf16)

    for c in range(2):
        pl.when(core == c)(functools.partial(write, c))


def small_params():
    return pltpu.CompilerParams(vmem_limit_bytes=12 * 1024 * 1024)


def padded(rows):
    return -(-rows // 16) * 16


def call_prepare_attention(n_f, attn_gain, wq, wk, wv, rel_bias, ffn_gain):
    vm, sm = pl.BlockSpec(memory_space=pltpu.VMEM), pl.BlockSpec(memory_space=pltpu.SMEM)
    return pl.pallas_call(
        functools.partial(prepare_attention, n_f),
        out_shape=sds((wq.shape[0], CUT), bf16),
        in_specs=[sm] + [pl.BlockSpec()] * 5,
        out_specs=vm,
        compiler_params=small_params(),
        name="prepare_attention",
    )(*(in_hbm(a) for a in (rel_bias, wq, wk, wv, attn_gain.reshape(1, -1), ffn_gain.reshape(1, -1))))


def call_prepare_ffn(place, n_f, wo, wg, wu, wd):
    ds, fh, half = wg.shape[0], wd.shape[0] // 2, wo.shape[1] // 2
    vm, sm = pl.BlockSpec(memory_space=pltpu.VMEM), pl.BlockSpec(memory_space=pltpu.SMEM)
    return pl.pallas_call(
        functools.partial(prepare_ffn, n_f),
        out_shape=(sds((2 * ds + fh + padded(wo.shape[0]), half), bf16), sds((2 * ds + fh, half), bf16)),
        in_specs=[sm] + [pl.BlockSpec()] * 4,
        out_specs=[vm] * 2,
        compiler_params=small_params(),
        name="prepare_ffn",
    )(place, *(in_hbm(a) for a in (wo, wg, wu, wd)))


def keep_close(G, L, place_ref, tok_ref, ct_ref, tok_out, ct_out, done_ref):
    step = pl.program_id(0)
    R, D = G * L, tok_ref.shape[-1]
    live = (step * G + lax.broadcasted_iota(jnp.int32, (R, 1), 0) // L) < place_ref[0]
    group_rows(tok_out, step, R)[...] = tok_ref[...].reshape(R, D)
    group_rows(ct_out, step, R)[...] = jnp.where(live, ct_ref[...].reshape(R, D), jnp.zeros((), bf16))
    done_ref[...] = jnp.zeros_like(done_ref)


def call_keep_close(place, tokens, ct):
    S, L, D = tokens.shape
    G = GROUP
    block = pl.BlockSpec((G, L, D), lambda i, c: (i, 0, 0))
    return pl.pallas_call(
        functools.partial(keep_close, G, L),
        out_shape=(sds((S * L, D), bf16), sds((S * L, D), bf16), sds((8, PAIR), f32)),
        grid_spec=pltpu.PrefetchScalarGridSpec(
            num_scalar_prefetch=1, grid=(S // G,), in_specs=[block, block], out_specs=[whole(None)] * 3
        ),
        compiler_params=params(MIB_TOKENS),
        cost_estimate=cost(S * L, 1, 8 * S * L * D),
        name="keep_close",
    )(place, in_hbm(tokens), in_hbm(ct))


def attention_forward(G, L, n_z, place_ref, tok_ref, after_ref, *refs):
    pieces, refs = refs[:4], refs[4:]
    all_qkv, all_probs, mixed_ref, w_ref, gains_ref, table_ref, st_ref, small_ref = refs
    step = pl.program_id(0)
    place = Place(place_ref, n_z)
    D = tok_ref.shape[-1]
    n_f = 2 * n_z
    ds = D // n_f
    rest = 3 * INNER - CUT

    def assemble(c):
        for xx, k, f in place.shards():
            one, two = pieces[xx].at[k], pieces[2 + xx].at[k]
            one, two = (one, two) if c == 0 else (two, one)
            w_ref[at(f, ds), :CUT] = one[...]
            w_ref[at(f, ds), CUT:] = two[:, :rest]
            small_ref[at(f, ds), :] = two[:, rest:].astype(f32)

    @pl.when(step == 0)
    def _():
        for c in range(2):
            pl.when(place.core == c)(functools.partial(assemble, c))
        n_b = BUCKETS // n_f
        ids = bucket_table(L)
        for p in range(PAIRS):
            total = jnp.zeros(ids.shape, f32)
            for b in range(BUCKETS):
                row = b // n_b * ds + (b % n_b) * PAIRS + p
                total = jnp.where(ids == b, small_ref[row : row + 1, :], total)
            table_ref[p] = total
        per = PAIR // ds
        lane = lax.broadcasted_iota(jnp.int32, (1, PAIR), 1) // ds
        gains_ref[...] = jnp.zeros_like(gains_ref)
        for i in range(2):
            for v in range(D // PAIR):
                total = jnp.zeros((1, PAIR), f32)
                for f in range(per):
                    row = (v * per + f) * ds + n_b * PAIRS + i
                    total = jnp.where(lane == f, small_ref[row : row + 1, :], total)
                gains_ref[i : i + 1, v * PAIR : (v + 1) * PAIR] = total

    @pl.when(step * G < place.count)
    def _():
        mixed, qkv_ref = group_rows(mixed_ref, step, G * L), group_rows(all_qkv, step, G * L)
        probs_ref = all_probs.at[pl.ds(step * G, G)]
        x = group_rows(tok_ref, step, G * L)[...].astype(f32)
        normed = (x * inverse_rms(x) * gains_ref[0:1, :]).astype(bf16)
        qkv_ref[...] = nn(normed, w_ref[...]).astype(bf16)
        for s in range(0, G, 2):
            for p in range(PAIRS):
                q, k = (
                    [qkv_ref[pl.ds((s + i) * L, L), pl.ds(b * INNER + p * PAIR, PAIR)] for i in range(2)] for b in range(2)
                )
                st = nt(jnp.concatenate(k, axis=1), side_by_side(split_heads(q[0]), split_heads(q[1])))
                st_ref[s, p], st_ref[s + 1, p] = st[:, :PAIR], st[:, PAIR:]
        for s in range(G):
            for p in range(PAIRS):
                st = st_ref[s, p] + table_ref[p]
                e = jnp.exp(st - jnp.max(st, axis=0, keepdims=True))
                probs_ref[s, p] = (e * (1.0 / jnp.sum(e, axis=0, keepdims=True))).astype(bf16)
        for s in range(G):
            rows = pl.ds(s * L, L)
            for p in range(PAIRS):
                v = qkv_ref[rows, pl.ds(2 * INNER + p * PAIR, PAIR)]
                mixed[rows, pl.ds(p * PAIR, PAIR)] = join_heads(tn(probs_ref[s, p], v)).astype(bf16)


MIB_FORWARD, MIB_FFN, MIB_BACKWARD, MIB_TOKENS, MIB_RESULT = 8, 14, 10, 6, 6


def params(mib):
    return pltpu.CompilerParams(dimension_semantics=("arbitrary",), vmem_limit_bytes=mib * 1024 * 1024)


def whole(shape):
    return pl.BlockSpec(memory_space=pltpu.VMEM)


def live_group(i, place, G):
    return jnp.minimum(i, jnp.maximum((place[0] + G - 1) // G - 1, 0))


def series_spec(G, shape, every=False):
    tail = (0,) * (len(shape) - 1)
    return pl.BlockSpec((G,) + shape[1:], lambda i, c: ((i if every else live_group(i, c, G)),) + tail)


def row_spec(G, L, width):
    return pl.BlockSpec((G * L, width), lambda i, c: (live_group(i, c, G), 0))


def group_rows(ref, step, rows):
    return ref.at[pl.ds(pl.multiple_of(step * rows, rows), rows), :]


def cost(rows, per_row, nbytes, exps=0):
    return pl.CostEstimate(flops=2 * rows * per_row, bytes_accessed=nbytes, transcendentals=exps)


def call_attention_forward(place, tokens, after, pieces, S, L, D):
    G, n_z = GROUP, pieces[0].shape[0]
    return pl.pallas_call(
        functools.partial(attention_forward, G, L, n_z),
        out_shape=(
            sds((S * L, 3 * INNER), bf16),
            sds((S, PAIRS, L, PAIR), bf16),
            sds((S * L, INNER), bf16),
            sds((D, 3 * INNER), bf16),
            sds((8, D), f32),
        ),
        grid_spec=pltpu.PrefetchScalarGridSpec(
            num_scalar_prefetch=1,
            grid=(S // G,),
            in_specs=[whole(tokens.shape), whole(after.shape)] + [whole(piece.shape) for piece in pieces],
            out_specs=[
                whole((S * L, 3 * INNER)),
                whole((S, PAIRS, L, PAIR)),
                whole((S * L, INNER)),
                whole((D, 3 * INNER)),
                whole((8, D)),
            ],
            scratch_shapes=[
                pltpu.VMEM((PAIRS, L, PAIR), f32),
                pltpu.VMEM((G, PAIRS, L, PAIR), f32),
                pltpu.VMEM((D, PAIR), f32),
            ],
        ),
        compiler_params=params(MIB_FORWARD),
        cost_estimate=cost(S * L, D * 3 * INNER * 4, S * L * 5000),
        name="attention_forward",
    )(place, tokens, after, *pieces)


def gelu_parts(v):
    c = 0.7978845608028654
    v2 = v * v
    t = jnp.tanh(v * (c + (c * 0.044715) * v2))
    half = 0.5 + 0.5 * t
    g = v * half
    return g, half + g * (1.0 - t) * (c + (3 * c * 0.044715) * v2)


def put_weights(place, pieces, wgu, wd, wo=None):
    FW, D = wd.shape

    def assemble(c):
        for f, here, there in pieces:
            for which, piece in enumerate((here, there) if c == 0 else (there, here)):
                n_f = len(pieces)
                ds, fh, half, is_ = D // n_f, FW // n_f, FW // 2, INNER // n_f
                for part in range(2):
                    start = (2 * part + which) * half
                    wgu[at(f, ds), start : start + half] = piece[part * ds : (part + 1) * ds, :]
                cols = slice(which * half, (which + 1) * half)
                wd[at(f, fh), cols] = piece[2 * ds : 2 * ds + fh, :]
                if wo is None:
                    continue
                if is_ % 16 == 0:
                    wo[at(f, is_), cols] = piece[2 * ds + fh : 2 * ds + fh + is_, :]
                else:
                    wo[f, :, cols] = piece[2 * ds + fh :, :]

    for c in range(2):
        pl.when(place.core == c)(functools.partial(assemble, c))


def put_grads(place, n_z, keep, send, agu, ad, ao=None):
    n_f = 2 * n_z
    FW, D = ad.shape
    ds, fh, half = D // n_f, FW // n_f, FW // 2

    def write(c):
        for xx, k, f in place.shards():
            for which, ref in enumerate((keep, send) if c == 0 else (send, keep)):
                for part in range(2):
                    start = (2 * part + which) * half
                    ref[xx, k, part * ds : (part + 1) * ds, :] = agu[at(f, ds), start : start + half].astype(bf16)
                cols = slice(which * half, (which + 1) * half)
                ref[xx, k, 2 * ds : 2 * ds + fh, :] = ad[at(f, fh), cols].astype(bf16)
                if ao is not None:
                    is_ = INNER // n_f
                    if is_ % 16 == 0:
                        ref[xx, k, 2 * ds + fh :, :] = ao[at(f, is_), cols].astype(bf16)
                    else:
                        ref[xx, k, 2 * ds + fh :, :] = ao[f, :, cols].astype(bf16)

    for c in range(2):
        pl.when(place.core == c)(functools.partial(write, c))


def ffn_half(G, L, n_z, stage, shift, place_ref, *refs):
    n_f = 2 * n_z
    place = Place(place_ref, n_z)
    first, begins, ends = stage == 0, stage < 2, stage != 1
    if first:
        (near, own_far, far, near_c, own_far_c, far_c), refs = refs[:6], refs[6:]
        here, there = ([near.at[k] for k in range(n_z)] for near in (near, near_c))
        here, there = (
            side + [own] + [rest.at[k] for k in range(n_z - 1)]
            for side, own, rest in ((here, own_far, far), (there, own_far_c, far_c))
        )
        pieces = [(f, *pair) for (_, _, f), pair in zip(place.shards(), zip(here, there))]
    elif begins:
        pieces, refs = refs[:4], refs[4:]
        pieces = [(f, pieces[xx].at[k], pieces[2 + xx].at[k]) for xx, k, f in place.shards()]
    if stage == 0:
        (tok_ref, ct_ref, mixed_ref, gains_ref,
         hid_ref, act_ref, gpart_ref, wd, wo_out, keep, send,
         agu, ad, wgu, n2, n2_next, gu, ga, low, gn, spread) = refs
    elif stage == 1:
        hid_ref, ct_ref, gains_ref, wo_in, _, _ = refs[:6]
        gpart_ref, mixed_ref, act_ref, agu, ad, ao, gf_ref, wd, wgu, n2, n2_next, gu, ga, low, gn = refs[6:]
    else:
        hid_ref, ct_ref, gains_ref, wo_in, wd, wgu = refs[:6]
        gpart_ref, mixed_ref, act_ref, agu, ad, ao, gf_ref, keep, send, n2, n2_next, gu, ga, low, gn, spread = refs[13:]
    step = pl.program_id(0) + shift
    R = G * L
    FW, D = wd.shape
    CH = FW // 2
    is_ = INNER // n_f
    count = place.count
    group = jnp.minimum(step, (count + G - 1) // G - 1)

    def normalise(group, into):
        if first:
            h = group_rows(tok_ref, group, R)[...].astype(f32) + nn(group_rows(mixed_ref, group, R)[...], wo_out[...])
            group_rows(hid_ref, group, R)[...] = h.astype(bf16)
        else:
            h = group_rows(hid_ref, group, R)[...].astype(f32)
        into[...] = (h * inverse_rms(h) * gains_ref[1:2, :]).astype(bf16)

    if begins:

        @pl.when(step == 0)
        def _():
            wo = (wo_out if is_ % 16 == 0 else spread) if first else None
            put_weights(place, pieces, wgu, wd, wo)
            if first and is_ % 16:
                wo_out[...] = jnp.concatenate([spread[f, :is_, :].astype(f32) for f in range(n_f)], axis=0).astype(bf16)
            for ref in (agu, ad) if first else (agu, ad, ao, gf_ref):
                ref[...] = jnp.zeros_like(ref)

    @pl.when(step * G < count)
    def _():
        normalise(group, n2)
        gb, act, gpart, hid = (group_rows(ref, group, R) for ref in (ct_ref, act_ref, gpart_ref, hid_ref))
        for c in range(2):
            cols, both = pl.ds(c * CH, CH), pl.ds(2 * c * CH, 2 * CH)
            gu[c] = nn(n2[...], wgu[:, both])
            ga[c] = nt(gb[...], wd[cols, :])
        for c in range(2):
            cols, both = pl.ds(c * CH, CH), pl.ds(2 * c * CH, 2 * CH)
            for r in range(0, R, L):
                rows = pl.ds(r, L)
                u = gu[c, rows, CH:]
                a = ga[c, rows, :]
                g, dg = gelu_parts(gu[c, rows, :CH])
                act[rows, cols] = (g * u).astype(bf16)
                low[c, rows, :CH] = (a * u * dg).astype(bf16)
                low[c, rows, CH:] = (a * g).astype(bf16)
            if c == 0:
                gn[...] = nt(low[c], wgu[:, both])
            else:
                gn[...] += nt(low[c], wgu[:, both])
            ad[cols, :] += tn(act[:, cols], gb[...])
            agu[:, both] += tn(n2[...], low[c])
        if first:
            gpart[...] = gn[...].astype(bf16)
        else:
            mixed = group_rows(mixed_ref, group, R)
            h = hid[...].astype(f32)
            scale = inverse_rms(h)
            hs = h * scale
            g2 = gn[...] + gpart[...].astype(f32)
            gf_ref[...] += row_sums(g2 * hs)
            g2 = g2 * gains_ref[1:2, :]
            dot = jnp.mean(g2 * hs, axis=-1, keepdims=True)
            gh = (gb[...].astype(f32) + scale * (g2 - hs * dot)).astype(bf16)
            gpart[...] = gh
            ao[...] += tn(mixed[...], gh)
            mixed[...] = nt(gh, wo_in[...]).astype(bf16)

    if ends:

        @pl.when(pl.program_id(0) == pl.num_programs(0) - 1)
        def _():
            if first:
                put_grads(place, n_z, keep, send, agu, ad)
            elif is_ % 16 == 0:
                put_grads(place, n_z, keep, send, agu, ad, ao)
            else:
                for f in range(n_f):
                    spread[f, :is_, :] = ao[f * is_ : (f + 1) * is_, :]
                put_grads(place, n_z, keep, send, agu, ad, spread)


def call_ffn_half(stage, place, n_z, operands, S, L, D):
    G = GROUP
    R, n_f = G * L, 2 * n_z
    FW = D
    CH = FW // 2
    ds, fh, is_ = D // n_f, FW // n_f, INNER // n_f
    pack = (2, n_z, 2 * ds + fh + (padded(is_) if stage else 0), CH)
    packs, act = [sds(pack, bf16)] * 2, sds((S * L, FW), bf16)
    wd, wgu, rows = sds((FW, D), bf16), sds((D, 2 * FW), bf16), sds((S * L, D), bf16)
    agu, ad = sds((D, 2 * FW), f32), sds((FW, D), f32)
    running = [rows, sds((S * L, INNER), bf16), act, agu, ad, sds((INNER, D), f32), sds((8, D), f32)]
    vm = pltpu.VMEM
    work = [
        vm((R, D), bf16), vm((R, D), bf16),
        vm((2, R, 2 * CH), f32), vm((2, R, CH), f32), vm((2, R, 2 * CH), bf16), vm((R, D), f32),
    ]
    spread = [vm((n_f, padded(is_), D) if is_ % 16 else (1, 16, 128), f32 if stage else bf16)]
    half = S // G // 2
    steps, shift = ((S // G, 0), (half, 0), (S // G - half, half))[stage]
    if stage == 0:
        out_shape = [rows, act, rows, wd, sds((INNER, D), bf16)] + packs
        scratch = [vm(agu.shape, f32), vm(ad.shape, f32), vm(wgu.shape, bf16)] + work + spread
        aliases = {}
    elif stage == 1:
        out_shape, scratch = running + [wd, wgu], work
        aliases = {9: 0, 10: 1}
    else:
        out_shape, scratch = running + packs, work + spread
        aliases = {7 + i: i for i in range(7)}
    return pl.pallas_call(
        functools.partial(ffn_half, G, L, n_z, stage, shift),
        out_shape=tuple(out_shape),
        grid_spec=pltpu.PrefetchScalarGridSpec(
            num_scalar_prefetch=1,
            grid=(steps,),
            in_specs=[whole(a.shape) for a in operands],
            out_specs=[whole(shape.shape) for shape in out_shape],
            scratch_shapes=scratch,
        ),
        input_output_aliases=aliases,
        compiler_params=params(MIB_FFN),
        cost_estimate=cost(steps * R, 9 * D * FW, S * L * 9000),
        name=("ffn_first", "ffn_second", "ffn_third")[stage],
    )(place, *operands)


def layer_result(G, L, shift, place_ref, hid_ref, act_0, act_1, wd_0, wd_1, gains_ref, *refs):
    out_ref, done_ref = refs[-2:]
    step = pl.program_id(0) + shift
    count = place_ref[0]
    R = G * L
    D = hid_ref.shape[-1]
    done_ref[...] = gains_ref[...]
    group = jnp.minimum(step, (count + G - 1) // G - 1)
    hid_ref, act_0, act_1 = (group_rows(ref, group, R) for ref in (hid_ref, act_0, act_1))

    @pl.when(step * G >= count)
    def _():
        out_ref[...] = jnp.zeros_like(out_ref)

    @pl.when(step * G < count)
    def _():
        live = (step * G + lax.broadcasted_iota(jnp.int32, (R, 1), 0) // L) < count
        out = hid_ref[...].astype(f32) + nn(act_0[...], wd_0[...]) + nn(act_1[...], wd_1[...])
        out_ref[...] = jnp.where(live, out, 0.0).astype(bf16).reshape(G, L, D)


def call_layer_result(place, hidden, act_0, act_1, wd_0, wd_1, gains, S, L, earlier=None):
    G, D = GROUP, hidden.shape[-1]
    operands = (hidden, act_0, act_1, wd_0, wd_1, gains)
    half = S // G // 2
    steps, shift = (half, 0) if earlier is None else (S // G - half, half)
    more = () if earlier is None else (earlier,)
    return pl.pallas_call(
        functools.partial(layer_result, G, L, shift),
        out_shape=(pltpu.HBM((S, L, D), bf16), sds(gains.shape, f32)),
        grid_spec=pltpu.PrefetchScalarGridSpec(
            num_scalar_prefetch=1,
            grid=(steps,),
            in_specs=[whole(a.shape) for a in operands] + [pl.BlockSpec(memory_space=pl.ANY)] * len(more),
            out_specs=(pl.BlockSpec((G, L, D), lambda i, c: (i + shift, 0, 0)), whole(gains.shape)),
        ),
        input_output_aliases={7: 0} if more else {},
        compiler_params=params(MIB_RESULT),
        cost_estimate=cost(S * L // 2, 2 * D * act_0.shape[-1], S * L * 3000),
        name="layer_result",
    )(place, *operands, *more)


def attention_backward(G, L, n_z, place_ref, tok_ref, _, probs_ref, gm_ref, w_ref, gains_ref, gf_ref,
                       dqkv, keep, send, aw, ab, dp_ref, ds_ref, small):
    step = pl.program_id(0)
    last = pl.num_programs(0) - 1
    R = G * L
    D = tok_ref.shape[-1]
    place = Place(place_ref, n_z)
    count = place.count
    group = jnp.minimum(step, (count + G - 1) // G - 1)
    probs_ref = probs_ref.at[pl.ds(group * G, G)]
    gm_ref, dqkv = group_rows(gm_ref, group, R), group_rows(dqkv, group, R)

    @pl.when(step == 0)
    def _():
        for ref in (aw, ab):
            ref[...] = jnp.zeros_like(ref)

    @pl.when(step * G < count)
    def _():
        cols = [[pl.ds(b * INNER + p * PAIR, PAIR) for b in range(3)] for p in range(PAIRS)]
        for s in range(G):
            for p in range(PAIRS):
                rows = pl.ds(s * L, L)
                dm = split_heads(gm_ref[rows, pl.ds(p * PAIR, PAIR)])
                dp_ref[s, p] = nt(dqkv[rows, cols[p][2]], dm)
                dqkv[rows, cols[p][2]] = nn(probs_ref[s, p], dm).astype(bf16)
        for p in range(PAIRS):
            total = ab[p]
            for s in range(G):
                prf = probs_ref[s, p].astype(f32)
                dp = dp_ref[s, p]
                ds = prf * (dp - jnp.sum(prf * dp, axis=0, keepdims=True))
                total = total + ds
                ds_ref[s, p] = ds.astype(bf16)
            ab[p] = total
        for s in range(G):
            for p in range(PAIRS):
                rows = pl.ds(s * L, L)
                low = ds_ref[s, p]
                q, k = dqkv[rows, cols[p][0]], dqkv[rows, cols[p][1]]
                dqkv[rows, cols[p][1]] = nn(low, split_heads(q)).astype(bf16)
                dqkv[rows, cols[p][0]] = join_heads(tn(low, k)).astype(bf16)
        x = group_rows(tok_ref, group, R)[...].astype(f32)
        aw[...] += tn((x * inverse_rms(x) * gains_ref[0:1, :]).astype(bf16), dqkv[...])

    @pl.when(step == last)
    def _():
        n_f = 2 * n_z
        ds, n_b, rest = D // n_f, BUCKETS // n_f, 3 * INNER - CUT
        ids = bucket_table(L)
        small[...] = jnp.zeros_like(small)
        for p in range(PAIRS):
            t = ab[p]
            by_lane = [jnp.sum(jnp.where(ids == b, t, 0.0), axis=0, keepdims=True) for b in range(BUCKETS)]
            by_lane = jnp.concatenate(by_lane, axis=0)
            low = lane_low(by_lane.shape)
            halves = [jnp.sum(jnp.where(mask, by_lane, 0.0), axis=1, keepdims=True) for mask in (low, ~low)]
            for b in range(BUCKETS):
                row = b // n_b * ds + (b % n_b) * HEADS + 2 * p
                for side in range(2):
                    small[row + side : row + side + 1, :] = jnp.broadcast_to(halves[side][b : b + 1], (1, PAIR))
        gain = jnp.transpose(gains_ref[...])[:, 0:1]
        one = jnp.sum(aw[...] * w_ref[...].astype(f32), axis=1, keepdims=True) / gain
        two = jnp.sum(jnp.transpose(gf_ref[...]), axis=1, keepdims=True)
        lane = lax.broadcasted_iota(jnp.int32, (D, PAIR), 1)
        small[...] = jnp.where(lane == 0, one, jnp.where(lane == 1, two, small[...]))

        def write(c):
            for xx, k, f in place.shards():
                one, two = keep.at[xx, k], send.at[xx, k]
                one, two = (one, two) if c == 0 else (two, one)
                one[...] = aw[at(f, ds), :CUT].astype(bf16)
                two[:, :rest] = aw[at(f, ds), CUT:].astype(bf16)
                two[:, rest:] = small[at(f, ds), :].astype(bf16)

        for c in range(2):
            pl.when(place.core == c)(functools.partial(write, c))


def call_attention_backward(place, n_z, tokens, qkv, probs, gm, w, gains, gf, S, L, D):
    G = GROUP
    pack = (2, n_z, D // (2 * n_z), CUT)
    vm = pltpu.VMEM
    return pl.pallas_call(
        functools.partial(attention_backward, G, L, n_z),
        out_shape=(sds((S * L, 3 * INNER), bf16), sds(pack, bf16), sds(pack, bf16)),
        grid_spec=pltpu.PrefetchScalarGridSpec(
            num_scalar_prefetch=1,
            grid=(S // G,),
            in_specs=[whole(tokens.shape), whole(qkv.shape), whole(probs.shape),
                      whole(gm.shape), whole(w.shape), whole(gains.shape), whole(gf.shape)],
            out_specs=[whole(pack)] * 3,
            scratch_shapes=[
                vm(w.shape, f32), vm((PAIRS, L, PAIR), f32),
                vm((G, PAIRS, L, PAIR), f32), vm((G, PAIRS, L, PAIR), bf16), vm((D, PAIR), f32),
            ],
        ),
        input_output_aliases={2: 0},
        compiler_params=params(MIB_BACKWARD),
        cost_estimate=cost(S * L, D * 3 * INNER * 4, S * L * 6000),
        name="attention_backward",
    )(place, tokens, qkv, probs, gm, w, gains, gf)


def token_gradient(G, L, place_ref, tok_ref, dqkv_ref, gh_ref, w_ref, gains_ref, gt_ref, done_ref):
    step = pl.program_id(0)
    D = tok_ref.shape[-1]
    done_ref[...] = gains_ref[...]
    group = jnp.minimum(step, (place_ref[0] + G - 1) // G - 1)
    tok_ref, dqkv_ref, gh_ref = (group_rows(ref, group, G * L) for ref in (tok_ref, dqkv_ref, gh_ref))

    @pl.when(step * G >= place_ref[0])
    def _():
        gt_ref[...] = jnp.zeros_like(gt_ref)

    @pl.when(step * G < place_ref[0])
    def _():
        half = G * L // 2
        parts = [pl.ds(i * half, half) for i in range(2)]
        products = [nt(dqkv_ref[rows, :], w_ref[...]) for rows in parts]
        for i, rows in enumerate(parts):
            x = tok_ref[rows, :].astype(f32)
            scale = inverse_rms(x)
            xs = x * scale
            g = products[i] * gains_ref[0:1, :]
            dot = jnp.mean(g * xs, axis=-1, keepdims=True)
            gt = gh_ref[rows, :].astype(f32) + scale * (g - xs * dot)
            gt_ref[pl.ds(i * G // 2, G // 2)] = gt.astype(bf16).reshape(G // 2, L, D)


def call_token_gradient(place, tokens, dqkv, gh, w, gains, S, L, D):
    G = GROUP
    operands = (tokens, dqkv, gh, w, gains)
    return pl.pallas_call(
        functools.partial(token_gradient, G, L),
        out_shape=(pltpu.HBM((S, L, D), bf16), sds(gains.shape, f32)),
        grid_spec=pltpu.PrefetchScalarGridSpec(
            num_scalar_prefetch=1,
            grid=(S // G,),
            in_specs=[whole(a.shape) for a in operands],
            out_specs=(series_spec(G, (S, L, D), True), whole(gains.shape)),
        ),
        compiler_params=params(MIB_TOKENS),
        cost_estimate=cost(S * L, D * 3 * INNER * 2, S * L * 5000),
        name="token_gradient",
    )(place, *operands)


def finish(n_f, place_ref, *refs):
    packs = [refs[2 * i : 2 * i + 2] for i in range(3)]
    gq, gk, gv, go, gg, gu, gd, ga, gf, gb = refs[7:]
    core = place_ref[1]
    ds, is_, fh = gq.shape[0], go.shape[0], gd.shape[0] // 2
    half = go.shape[1] // 2

    def halves(pack):
        here, there = pack[0][...].astype(f32), pack[1][...].astype(f32)
        return jnp.where(core == 0, here, there), jnp.where(core == 0, there, here)

    one, two = halves(packs[2])
    gq[...] = one[:, :INNER]
    gk[...] = jnp.concatenate([one[:, INNER:CUT], two[:, : 2 * INNER - CUT]], axis=1)
    gv[...] = two[:, 2 * INNER - CUT : 3 * INNER - CUT]
    small = jnp.transpose(two[:, 3 * INNER - CUT :])
    ga[...] = small[0]
    gf[...] = small[1]
    gb[...] = small[2, : BUCKETS // n_f * HEADS]
    chunks = [halves(packs[0]), halves(packs[1])]
    for which, ref in enumerate((gg, gu)):
        wide = [jnp.concatenate([c[which][:ds], c[which][ds : 2 * ds]], axis=1) for c in chunks]
        width = wide[0].shape[1] // n_f
        ref[...] = jnp.concatenate(
            [w[:, f * width : (f + 1) * width] for f in range(n_f) for w in wide], axis=1
        )
    for chunk, pair in enumerate(chunks):
        for which in range(2):
            gd[chunk * fh : (chunk + 1) * fh, which * half : (which + 1) * half] = pair[which][2 * ds : 2 * ds + fh]
    for which in range(2):
        go[:, which * half : (which + 1) * half] = chunks[1][which][2 * ds + fh : 2 * ds + fh + is_]


def call_finish(place, n_f, packs, shapes, after):
    vm, sm = pl.BlockSpec(memory_space=pltpu.VMEM), pl.BlockSpec(memory_space=pltpu.SMEM)
    flat = [piece for pack in packs for piece in pack]
    return pl.pallas_call(
        functools.partial(finish, n_f),
        out_shape=tuple(sds(shape, f32) for shape in shapes),
        in_specs=[sm] + [vm] * len(flat) + [vm],
        out_specs=[vm] * len(shapes),
        compiler_params=small_params(),
        name="finish",
    )(place, *flat, after)


def solution(mesh):
    n_r, n_f = mesh.shape["rep"], mesh.shape["fsdp"]
    n_z = n_f // 2

    def over_fsdp(value, distance):
        return lax.ppermute(value, "fsdp", [(i, i ^ distance) for i in range(n_f)])

    def over_rep(value, distance):
        return lax.ppermute(value, "rep", [(i, i ^ distance) for i in range(n_r)])

    def along_z(pack):
        return [pack] + [over_fsdp(pack, 2 * k) for k in range(1, n_z)]

    def halved(keep, got):
        away = (keep[1].astype(f32) + got[1].astype(f32)).astype(bf16)
        return keep[0].astype(f32) + got[0].astype(f32), away

    def joined(here, got):
        here = here + got.astype(f32)
        return here[0], [here[k].astype(bf16) for k in range(1, n_z)]

    def to_z(pieces):
        return [over_fsdp(piece, 2 * (k + 1)) for k, piece in enumerate(pieces)]

    def summed(own, got):
        for value in got:
            own = own + value.astype(f32)
        return own.astype(bf16)

    def replicas(own, got):
        distance = 2
        while distance < n_r:
            own = (own.astype(f32) + got.astype(f32)).astype(bf16)
            distance *= 2
            got = over_rep(own, distance) if distance < n_r else None
        return own, over_rep(own, 1)

    together = lax.optimization_barrier

    def body(tokens, counts, attn_gain, wq, wk, wv, wo, rel_bias, ffn_gain, wg, wu, wd, cotangent):
        S, L, D = tokens.shape
        r, f = lax.axis_index("rep"), lax.axis_index("fsdp")
        place = in_hbm(jnp.stack([counts[0, 0], r % 2, f % 2, f // 2]).astype(jnp.int32))
        pack_a = call_prepare_attention(n_f, attn_gain, wq, wk, wv, rel_bias, ffn_gain)
        pack_0, pack_1 = call_prepare_ffn(place, n_f, wo, wg, wu, wd)

        z_0 = along_z(pack_0)
        z_a, pack_1 = together((along_z(pack_a), pack_1))
        near_a = jnp.stack(z_a)
        far_a, own_far_0 = over_fsdp(near_a, 1), over_fsdp(pack_0, 1)
        tokens, cotangent, done = call_keep_close(place, tokens, cotangent)
        done, far_a, own_far_0, z_0, pack_1 = together((done, far_a, own_far_0, z_0, pack_1))
        near_ac, far_ac, near_0 = over_rep(near_a, 1), over_rep(far_a, 1), jnp.stack(z_0)
        far_ac, near_0 = together((far_ac, near_0))

        far_0, near_0c, z_1 = over_fsdp(near_0[1:], 1), over_rep(near_0, 1), along_z(pack_1)
        qkv, probs, mixed, w_all, gains = call_attention_forward(place, tokens, done, (near_a, far_a, near_ac, far_ac), S, L, D)
        gains, far_0, near_0c, own_far_0, z_1 = together((gains, far_0, near_0c, own_far_0, z_1))
        own_far_0c, far_0c, near_1 = over_rep(own_far_0, 1), over_rep(far_0, 1), jnp.stack(z_1)
        far_0c, near_1 = together((far_0c, near_1))

        far_1, near_1c = over_fsdp(near_1, 1), over_rep(near_1, 1)
        hidden, act_0, gpart, wd_0, wo_all, keep_0, send_0 = call_ffn_half(
            0, place, n_z, (near_0, own_far_0, far_0, near_0c, own_far_0c, far_0c, tokens, cotangent, mixed, gains), S, L, D
        )
        wo_all, keep_0, send_0, far_1, near_1c = together((wo_all, keep_0, send_0, far_1, near_1c))

        far_1c, got_0 = over_rep(far_1, 1), over_rep(send_0, 1)
        *running, gf, wd_1, wgu = call_ffn_half(
            1, place, n_z, (near_1, far_1, near_1c, far_1c, hidden, cotangent, gains, wo_all, gpart, mixed), S, L, D
        )
        gf, got_0 = together((gf, got_0))
        here_0, away_0 = halved(keep_0, got_0)
        away_0, gf = together((away_0, gf))
        got_0 = over_fsdp(away_0, 1)
        gh, gm, act_1, _, _, _, gf, keep_1, send_1 = call_ffn_half(
            2, place, n_z, (hidden, cotangent, gains, wo_all, wd_1, wgu, *running, gf), S, L, D
        )
        keep_1, send_1, gf, got_0 = together((keep_1, send_1, gf, got_0))
        own_0, z_0 = joined(here_0, got_0)
        z_0, got_1 = to_z(z_0), over_rep(send_1, 1)
        here_1, away_1 = halved(keep_1, got_1)
        gf, away_1 = together((gf, away_1))
        got_1 = over_fsdp(away_1, 1)
        dqkv, keep_2, send_2 = call_attention_backward(place, n_z, tokens, qkv, probs, gm, w_all, gains, gf, S, L, D)
        keep_2, send_2, z_0, got_1 = together((keep_2, send_2, z_0, got_1))
        sum_0 = summed(own_0, z_0)
        own_1, z_1 = joined(here_1, got_1)

        z_1, got_2 = to_z(z_1), over_rep(send_2, 1)
        here_2, away_2 = halved(keep_2, got_2)
        gains, away_2, sum_0 = together((gains, away_2, sum_0))
        got_2 = over_fsdp(away_2, 1)
        grad_tokens, done = call_token_gradient(place, tokens, dqkv, gh, w_all, gains, S, L, D)
        done, got_2, z_1 = together((done, got_2, z_1))
        sum_1 = summed(own_1, z_1)
        own_2, z_2 = joined(here_2, got_2)
        done, z_2 = together((done, z_2))
        z_2 = to_z(z_2)
        half_out, done = call_layer_result(place, hidden, act_0, act_1, wd_0, wd_1, done, S, L)
        done, z_2 = together((done, z_2))
        sum_2 = summed(own_2, z_2)
        done, sum_2 = together((done, sum_2))
        got = [over_rep(value, 2) for value in (sum_0, sum_1, sum_2)]
        layer_out, done = call_layer_result(place, hidden, act_0, act_1, wd_0, wd_1, done, S, L, half_out)
        done, got = together((done, got))
        gq, gk, gv, go, gg, gu, gd, grad_attn_gain, grad_ffn_gain, grad_bias = call_finish(
            place, n_f, [replicas(own, y) for own, y in zip((sum_0, sum_1, sum_2), got)],
            (wq.shape, wk.shape, wv.shape, wo.shape, wg.shape, wu.shape, wd.shape,
             attn_gain.shape, ffn_gain.shape, rel_bias.shape), done,
        )
        return (layer_out, grad_tokens, grad_attn_gain, gq, gk, gv, go, grad_bias, grad_ffn_gain, gg, gu, gd)

    rows, cols, flat = P(("rep", "fsdp"), None, None), P("fsdp", None), P("fsdp")
    return jax.shard_map(
        body,
        mesh=mesh,
        in_specs=(rows, P("rep", "fsdp"), flat, cols, cols, cols, cols, flat, flat, cols, cols, cols, rows),
        out_specs=(rows, rows, flat, cols, cols, cols, cols, flat, flat, cols, cols, cols),
        check_vma=False,
    )
```
